32 devices in a mesh: seq: 8 (over y, x, core), batch: 4 (over z).
Axes of the slice: x: 2, y: 2, z: 4, core: 2. Of those that a mesh axis runs over, the one named last changes fastest.
Arguments:
- tokens: float32 [4, 1024, 768], P('batch', 'seq'), may hold values from -6 to 6
- cotangent: float32 [4, 1024, 768], P('batch', 'seq'), may hold values from -6 to 6
- group_ids: int32 [4, 1024], P('batch', 'seq'), may hold values from 0 to 7, never falling along the last dimension, each value on 1 to 640 neighbouring positions
- attention_weight: float32 [4, 768, 768], P(None, ('seq', 'batch')), may hold values from -1 to 1, as said below
- ffin_weight: float32 [2, 768, 2048], P(None, ('seq', 'batch')), may hold values from -0.21875 to 0.21875
- ffout_weight: float32 [2048, 768], P(('seq', 'batch')), may hold values from -0.125 to 0.125
- bias_table: float32 [32, 12], replicated, may hold values from -6 to 6
- gains: float32 [2, 768], replicated, may hold values from 0.5 to 1.5
- attention_momentum: float32 [4, 768, 768], P(None, ('seq', 'batch')), may hold values from -2560 to 2560, as said below
- ffin_momentum: float32 [2, 768, 2048], P(None, ('seq', 'batch')), may hold values from -160 to 160
- ffout_momentum: float32 [2048, 768], P(('seq', 'batch')), may hold values from -256 to 256
- bias_momentum: float32 [32, 12], replicated, may hold values from -3072 to 3072
- gain_momentum: float32 [2, 768], replicated, may hold values from -768 to 768
- attention_average: float32 [4, 768, 768], P(None, ('seq', 'batch')), may hold values from -1 to 1, as said below
- ffin_average: float32 [2, 768, 2048], P(None, ('seq', 'batch')), may hold values from -0.21875 to 0.21875
- ffout_average: float32 [2048, 768], P(('seq', 'batch')), may hold values from -0.125 to 0.125
- bias_average: float32 [32, 12], replicated, may hold values from -6 to 6
- gain_average: float32 [2, 768], replicated, may hold values from 0.5 to 1.5
Outputs:
- layer_output: float32 [4, 1024, 768], P('batch', 'seq')
- input_grad: float32 [4, 1024, 768], P('batch', 'seq')
- new_attention_weight: float32 [4, 768, 768], P(None, ('seq', 'batch'))
- new_ffin_weight: float32 [2, 768, 2048], P(None, ('seq', 'batch'))
- new_ffout_weight: float32 [2048, 768], P(('seq', 'batch'))
- new_bias_table: float32 [32, 12], replicated
- new_gains: float32 [2, 768], replicated
- new_attention_momentum: float32 [4, 768, 768], P(None, ('seq', 'batch'))
- new_ffin_momentum: float32 [2, 768, 2048], P(None, ('seq', 'batch'))
- new_ffout_momentum: float32 [2048, 768], P(('seq', 'batch'))
- new_bias_momentum: float32 [32, 12], replicated
- new_gain_momentum: float32 [2, 768], replicated
- new_attention_average: float32 [4, 768, 768], P(None, ('seq', 'batch'))
- new_ffin_average: float32 [2, 768, 2048], P(None, ('seq', 'batch'))
- new_ffout_average: float32 [2048, 768], P(('seq', 'batch'))
- new_bias_average: float32 [32, 12], replicated
- new_gain_average: float32 [2, 768], replicated
- attention_copy: bfloat16 [4, 768, 768], P(None, ('seq', 'batch'))
- ffin_copy: bfloat16 [2, 768, 2048], P(None, ('seq', 'batch'))
- ffout_copy: bfloat16 [2048, 768], P(('seq', 'batch'))
The draws below stay inside these ranges and needn't reach their ends.
Inputs may be any that keep to these rules, and one draw needn't show every extreme that they name: `group_ids`: along each sequence the group ids never fall; every one of the 8 groups holds 1 to 640 positions and one holds exactly 640. `attention_weight`: independent entries. `attention_average`: independent entries. `attention_momentum`: independent entries.
All inputs are finite; a program needn't handle non-finite values.
Results may differ from the reference program's by a relative error of at most 0.017.
Values may be sent and summed in bfloat16 or wider, within the bound.
No kernel may reach another device: no remote copies, remote signals or barrier semaphores. Data moves between devices by JAX's collectives and lax.ppermute only.
A program may use at most 192 MiB of HBM per device.

```python
import math
import jax
import jax.numpy as jnp
import numpy as np
from jax import lax

D = 768
HEADS = 12
HEAD_DIM = 64
FF = 2048
BUCKETS = 32
GROUPS = 8
LENGTH = 1024
SEQUENCES = 4
TOKENS = 4096
GROUP_MOST = 640


def attention_draw(key, salt, scales):
    noise_key = jax.random.fold_in(key, salt)
    noise = jax.random.normal(noise_key, (4, D, D), jnp.float32)
    return noise * jnp.array(scales, jnp.float32)[:, None, None]


def weight_scales():
    return ((4.0 * D) ** (-0.5), (4.0 * D) ** (-0.5), D ** (-0.5), (D / 8.0) ** (-0.5))


def draw_attention_weight(key, part):
    return attention_draw(key, 11, weight_scales())


def draw_attention_average(key, part):
    return attention_draw(key, 23, weight_scales())


def draw_attention_momentum(key, part):
    root = TOKENS ** 0.5
    return attention_draw(key, 37, (6.0 * root, 6.0 * root, 1.5 * root, 0.55 * root))


def block_scale(rng, shape, cuts, least, largest):
    factor_of, own = 1.0, jax.random.fold_in(rng, 6)
    for dim, parts in cuts:
        draws = jnp.exp(jax.random.uniform(jax.random.fold_in(own, dim), (parts,), jnp.float32, least / len(cuts), largest / len(cuts)))
        factor_of = factor_of * jnp.repeat(draws, shape[dim] // parts).reshape([-1 if axis == dim else 1 for axis in range(len(shape))])
    return factor_of


def split_up(amount, total, bound, lean):
    loads = [(1 << 20) // math.isqrt(grade ** lean) + 1 for grade in range(2, amount + 1)]
    rest, given = total - bound - (amount - 1), [1] * (amount - 1)
    while rest > 0:
        candidates = [i for i in range(amount - 1) if given[i] < bound]
        pool, budget = sum([loads[i] for i in candidates]), rest
        for i in candidates:
            more = min(bound - given[i], max(1, budget * loads[i] // pool), rest)
            given[i] = given[i] + more
            rest = rest - more
    return np.array([bound] + given)


def uneven(own_key, amount, total, limit, slope):
    if amount == 2:
        one = jax.random.randint(own_key, (), max(1, total - limit), min(limit, total - 1) + 1)
        return jnp.stack([one, total - one])
    tallies = jnp.asarray(split_up(amount, total, limit, slope), jnp.int32)
    twos = (amount - 1) // 2
    source_of, sink = tallies[1:1 + 2 * twos:2], tallies[2:2 + 2 * twos:2]
    room = jnp.minimum(source_of - 1, limit - sink)
    passed = jax.random.randint(jax.random.fold_in(own_key, 1), (twos,), 0, 1 << 20) % (room + 1)
    tallies = tallies.at[1:1 + 2 * twos:2].set(source_of - passed).at[2:2 + 2 * twos:2].set(sink + passed)
    return tallies[jax.random.permutation(jax.random.fold_in(own_key, 2), amount)]


def scatter_about(stream_key, extent, width, limit, shards=(), kind=jnp.bfloat16):
    entries = width * jax.random.normal(stream_key, extent, jnp.float32)
    if shards:
        entries = entries * block_scale(stream_key, extent, shards, -0.22, 0.18)
    return jnp.clip(entries, -limit, limit).astype(kind)


def setup_inputs(seed: int = 0) -> dict:
    key_list = jax.random.split(jax.random.key(seed), 19)
    tokens = scatter_about(key_list[0], (SEQUENCES, LENGTH, D), 1.0, 6.0, ((0, 4), (1, 8)), jnp.float32)
    cotangent = scatter_about(key_list[1], (SEQUENCES, LENGTH, D), 1.0, 6.0, ((0, 4), (1, 8)), jnp.float32)
    group_ids = jax.vmap(lambda own: jnp.searchsorted(jnp.cumsum(uneven(own, GROUPS, LENGTH, GROUP_MOST, 2)), jnp.arange(LENGTH), side="right"))(jax.random.split(key_list[2], SEQUENCES)).reshape((SEQUENCES, LENGTH)).astype(jnp.int32)
    attention_weight = draw_attention_weight(jax.random.fold_in(key_list[18], 71), 0)
    ffin_weight = scatter_about(key_list[4], (2, D, FF), D ** -0.5, 0.21875, ((1, 32),), jnp.float32)
    ffout_weight = scatter_about(key_list[5], (FF, D), FF ** -0.5, 0.125, ((0, 32),), jnp.float32)
    bias_table = scatter_about(key_list[6], (BUCKETS, HEADS), 1.0, 6.0, (), jnp.float32)
    gains = jnp.clip(1.0 + 0.1 * jax.random.normal(key_list[7], (2, D), jnp.float32), 0.5, 1.5)
    attention_momentum = draw_attention_momentum(jax.random.fold_in(key_list[18], 71), 0)
    ffin_momentum = scatter_about(key_list[9], (2, D, FF), (0.4 * TOKENS ** 0.5), 160.0, ((1, 32),), jnp.float32)
    ffout_momentum = scatter_about(key_list[10], (FF, D), (0.65 * TOKENS ** 0.5), 256.0, ((0, 32),), jnp.float32)
    bias_momentum = scatter_about(key_list[11], (BUCKETS, HEADS), (8.0 * TOKENS ** 0.5), 3072.0, (), jnp.float32)
    gain_momentum = scatter_about(key_list[12], (2, D), (2.0 * TOKENS ** 0.5), 768.0, (), jnp.float32)
    attention_average = draw_attention_average(jax.random.fold_in(key_list[18], 71), 0)
    ffin_average = scatter_about(key_list[14], (2, D, FF), D ** -0.5, 0.21875, ((1, 32),), jnp.float32)
    ffout_average = scatter_about(key_list[15], (FF, D), FF ** -0.5, 0.125, ((0, 32),), jnp.float32)
    bias_average = scatter_about(key_list[16], (BUCKETS, HEADS), 1.0, 6.0, (), jnp.float32)
    gain_average = jnp.clip(1.0 + 0.1 * jax.random.normal(key_list[17], (2, D), jnp.float32), 0.5, 1.5)
    return dict(tokens=tokens, cotangent=cotangent, group_ids=group_ids, attention_weight=attention_weight, ffin_weight=ffin_weight, ffout_weight=ffout_weight, bias_table=bias_table, gains=gains, attention_momentum=attention_momentum, ffin_momentum=ffin_momentum, ffout_momentum=ffout_momentum, bias_momentum=bias_momentum, gain_momentum=gain_momentum, attention_average=attention_average, ffin_average=ffin_average, ffout_average=ffout_average, bias_average=bias_average, gain_average=gain_average)


eps_norm = 1e-06
momentum_coef = 0.5
average_coef = 0.5
attention_rates = (0.0033, 0.0033, 0.025, 0.2)
ffin_rate = 0.063
ffout_rate = 0.023
bias_rate = 0.08
gain_rates = (0.045, 0.22)
thresholds = (12, 16, 23, 32, 46, 64, 91)
masked_score = -1e+30
highest = lax.Precision.HIGHEST

@jax.custom_vjp
def low(v):
    return lax.optimization_barrier(v.astype(jnp.bfloat16)).astype(jnp.float32)

@jax.custom_vjp
def low_back(v):
    return v

def low_keep(v):
    return (low(v), None)

def low_pass(kept, grad):
    return (grad,)

def back_keep(v):
    return (v, None)

def back_low(kept, grad):
    return (low(grad),)
low.defvjp(low_keep, low_pass)
low_back.defvjp(back_keep, back_low)

def rms_norm(values, gain):
    mean_square = lax.optimization_barrier(jnp.mean(values * values, axis=-1, keepdims=True))
    return values * lax.rsqrt(mean_square + eps_norm) * gain

def bucket_of(offset):
    magnitude = jnp.abs(offset)
    beyond = jnp.zeros_like(offset)
    for threshold in thresholds:
        beyond = beyond + (magnitude >= threshold).astype(jnp.int32)
    inside = jnp.where(magnitude < 8, magnitude, 8 + beyond)
    return inside + 16 * (offset > 0).astype(jnp.int32)

def project(left_rows, weight):
    return jnp.dot(left_rows, weight, precision=highest, preferred_element_type=jnp.float32)

def forward_sequence(seq_tokens, groups, attention_weight, ffin_weight, ffout_weight, bias_table, gains):
    attention_low = low(attention_weight)
    ffin_low = low(ffin_weight)
    ffout_low = low(ffout_weight)
    length = seq_tokens.shape[0]
    normed = low(rms_norm(seq_tokens, gains[0]))
    queries = low_back(low(project(normed, attention_low[0]))).reshape(length, HEADS, HEAD_DIM)
    keys_all = low_back(low(project(normed, attention_low[1]))).reshape(length, HEADS, HEAD_DIM)
    values_all = low_back(low(project(normed, attention_low[2]))).reshape(length, HEADS, HEAD_DIM)
    positions = jnp.arange(length, dtype=jnp.int32)
    block = min(512, length)
    starts = jnp.arange(length // block, dtype=jnp.int32) * block

    def attend(block_start):
        query_rows = lax.dynamic_slice_in_dim(queries, block_start, block, 0)
        query_pos = lax.dynamic_slice_in_dim(positions, block_start, block, 0)
        query_groups = lax.dynamic_slice_in_dim(groups, block_start, block, 0)
        raw_scores = jnp.einsum('qhd,khd->hqk', query_rows, keys_all, precision=highest)
        buckets = bucket_of(positions[None, :] - query_pos[:, None])
        offsets = jnp.transpose(bias_table[buckets], (2, 0, 1))
        scores = low_back(raw_scores) + offsets
        allowed = (query_groups[:, None] == groups[None, :])[None]
        scores = jnp.where(allowed, scores, masked_score)
        weights_soft = jax.nn.softmax(scores, axis=-1)
        return jnp.einsum('hqk,khd->qhd', low(weights_soft), values_all, precision=highest)
    attended = lax.map(jax.checkpoint(attend), starts).reshape(length, D)
    attended_low = low_back(low(attended))
    mixed = seq_tokens + low_back(project(attended_low, attention_low[3]))
    ff_input = low(rms_norm(mixed, gains[1]))
    gate_proj = low_back(project(ff_input, ffin_low[0]))
    up_proj = low_back(project(ff_input, ffin_low[1]))
    hidden = low(jax.nn.gelu(gate_proj, approximate=True) * up_proj)
    return mixed + low_back(project(hidden, ffout_low))

def add_trees(first_tree, second_tree):
    return jax.tree.map(jnp.add, first_tree, second_tree)

def update(weight, grad, momentum, average, rate):
    new_momentum = momentum_coef * momentum + grad
    new_weight = weight - rate * (grad + momentum_coef * new_momentum)
    new_average = average_coef * average + (1.0 - average_coef) * new_weight
    return (new_weight, new_momentum, new_average)

def reference(tokens, cotangent, group_ids, attention_weight, ffin_weight, ffout_weight, bias_table, gains, attention_momentum, ffin_momentum, ffout_momentum, bias_momentum, gain_momentum, attention_average, ffin_average, ffout_average, bias_average, gain_average):
    params = (attention_weight, ffin_weight, ffout_weight, bias_table, gains)

    def one_sequence(carry, item):
        seq_tokens, seq_cot, seq_groups = item

        def forward(inputs, weights):
            return forward_sequence(inputs, seq_groups, *weights)
        result, pull = jax.vjp(forward, seq_tokens, params)
        token_grad, param_grads = pull(seq_cot)
        return (add_trees(carry, param_grads), (result, token_grad))
    zero = jax.tree.map(jnp.zeros_like, params)
    grads, stacked = lax.scan(one_sequence, zero, (tokens, cotangent, group_ids))
    layer_output, input_grad = stacked
    inverse_root = 1.0 / math.sqrt(TOKENS)
    attention_rate = jnp.array(attention_rates, dtype=jnp.float32)[:, None, None] * inverse_root
    gain_rate = jnp.array(gain_rates, dtype=jnp.float32)[:, None] * inverse_root
    attn_new = update(attention_weight, grads[0], attention_momentum, attention_average, attention_rate)
    ffin_new = update(ffin_weight, grads[1], ffin_momentum, ffin_average, ffin_rate * inverse_root)
    ffout_new = update(ffout_weight, grads[2], ffout_momentum, ffout_average, ffout_rate * inverse_root)
    bias_new = update(bias_table, grads[3], bias_momentum, bias_average, bias_rate * inverse_root)
    gain_new = update(gains, grads[4], gain_momentum, gain_average, gain_rate)
    return (layer_output, input_grad, attn_new[0], ffin_new[0], ffout_new[0], bias_new[0], gain_new[0], attn_new[1], ffin_new[1], ffout_new[1], bias_new[1], gain_new[1], attn_new[2], ffin_new[2], ffout_new[2], bias_new[2], gain_new[2], attn_new[0].astype(jnp.bfloat16), ffin_new[0].astype(jnp.bfloat16), ffout_new[0].astype(jnp.bfloat16))
```

```python
import functools
import math

import jax
import jax.numpy as jnp
from jax import lax
from jax.experimental import pallas as pl
from jax.experimental.pallas import tpu as pltpu
from jax.sharding import PartitionSpec as P

eps_norm = 1e-06
momentum_coef = 0.5
average_coef = 0.5
attention_rates = (0.0033, 0.0033, 0.025, 0.2)
ffin_rate = 0.063
ffout_rate = 0.023
bias_rate = 0.08
gain_rates = (0.045, 0.22)
thresholds = (12, 16, 23, 32, 46, 64, 91)
masked_score = -1e30
gelu_scale = math.sqrt(2.0 / math.pi)
gelu_cubic = 0.044715
bf16 = jnp.bfloat16
f32 = jnp.float32
vmem_bytes = 60 * 1024 * 1024
lanes = 128


def product(left, right, left_dim, right_dim):
    return lax.dot_general(
        left, right, (((left_dim,), (right_dim,)), ((), ())), preferred_element_type=f32
    )


def mm(left, right):
    return product(left, right, 1, 0)


def mm_nt(left, right):
    return product(left, right, 1, 1)


def mm_tn(left, right):
    return product(left, right, 0, 0)


def bucket_of(offset):
    magnitude = jnp.abs(offset)
    beyond = jnp.zeros_like(offset)
    for threshold in thresholds:
        beyond = beyond + (magnitude >= threshold).astype(jnp.int32)
    inside = jnp.where(magnitude < 8, magnitude, 8 + beyond)
    return inside + 16 * (offset > 0).astype(jnp.int32)


def update(weight, grad, momentum, average, rate):
    new_momentum = momentum_coef * momentum + grad
    new_weight = weight - rate * (grad + momentum_coef * new_momentum)
    new_average = average_coef * average + (1.0 - average_coef) * new_weight
    return (new_weight, new_momentum, new_average)


def rms_scale(values):
    return lax.rsqrt(jnp.mean(values * values, axis=-1, keepdims=True) + eps_norm)


def params():
    return pltpu.CompilerParams(vmem_limit_bytes=vmem_bytes)


def any_spec():
    return pl.BlockSpec(memory_space=pl.ANY)


def cost(flops, nbytes, exps=0):
    return pl.CostEstimate(flops=int(flops), bytes_accessed=int(nbytes), transcendentals=int(exps))


def bias_kernel(table_ref, out_ref):
    head = pl.program_id(0)
    spot = lax.broadcasted_iota(jnp.int32, (8, 2 * lanes), 1)
    for block in range(3):
        buckets = bucket_of(lanes * (block - 1) + lanes - 1 - spot)
        row = jnp.zeros((8, 2 * lanes), f32)
        for bucket in range(table_ref.shape[0]):
            row = jnp.where(buckets == bucket, table_ref[bucket, head], row)
        wide = jnp.broadcast_to(row[:1], (lanes, 2 * lanes))
        rolled = pltpu.roll(wide, lanes + 1, 1, stride=1, stride_axis=0)
        out_ref[0, lanes * (block + 1) : lanes * (block + 2), :] = rolled[:, :lanes]
    out_ref[0, 0:lanes, :] = jnp.full((lanes, lanes), table_ref[15, head], f32)
    out_ref[0, 4 * lanes : 5 * lanes, :] = jnp.full((lanes, lanes), table_ref[31, head], f32)


def bias_rows(table):
    heads = table.shape[1]
    return pl.pallas_call(
        bias_kernel,
        grid=(heads,),
        in_specs=[pl.BlockSpec(memory_space=pltpu.SMEM)],
        out_specs=pl.BlockSpec((1, 5 * lanes, lanes), lambda i: (i, 0, 0)),
        out_shape=jax.ShapeDtypeStruct((heads, 5 * lanes, lanes), f32),
        compiler_params=params(),
        cost_estimate=cost(heads * 3e6, 4e6),
        name="bias_rows",
    )(table)


def bias_sum_kernel(grad_ref, out_ref):
    row_id = lax.broadcasted_iota(jnp.int32, (lanes, 2 * lanes), 0)
    bucket_id = lax.broadcasted_iota(jnp.int32, (2 * lanes, lanes), 1)
    place = lax.broadcasted_iota(jnp.int32, (2 * lanes, lanes), 0)
    total = jnp.zeros((8, lanes), f32)
    for block in range(3):
        part = grad_ref[0, lanes * (block + 1) : lanes * (block + 2), :]
        wide = jnp.concatenate([part, jnp.zeros((lanes, lanes), f32)], axis=1)
        for bit in range(7):
            step = 1 << bit
            moved = pltpu.roll(wide, step, 1)
            wide = jnp.where((row_id & step) == 0, moved, wide)
        sums = jnp.sum(wide.reshape(lanes // 8, 8, 2 * lanes), axis=0)
        onehot = (bucket_of(lanes * (block - 1) + lanes - 1 - place) == bucket_id).astype(f32)
        total = total + lax.dot_general(
            sums,
            onehot,
            (((1,), (0,)), ((), ())),
            precision=lax.Precision.HIGHEST,
            preferred_element_type=f32,
        )
    low = jnp.sum(grad_ref[0, 0:lanes, :])
    high = jnp.sum(grad_ref[0, 4 * lanes : 5 * lanes, :])
    lane = lax.broadcasted_iota(jnp.int32, (1, lanes), 1)
    row = jnp.sum(total, axis=0, keepdims=True)
    row = row + jnp.where(lane == 15, low, 0.0) + jnp.where(lane == 31, high, 0.0)
    out_ref[0] = row


def bias_sums(grad_band):
    heads = grad_band.shape[0]
    summed = pl.pallas_call(
        bias_sum_kernel,
        grid=(heads,),
        in_specs=[pl.BlockSpec((1, 5 * lanes, lanes), lambda i: (i, 0, 0))],
        out_specs=pl.BlockSpec((1, 1, lanes), lambda i: (i, 0, 0)),
        out_shape=jax.ShapeDtypeStruct((heads, 1, lanes), f32),
        compiler_params=params(),
        cost_estimate=cost(heads * 3e6, 4e6),
        name="bias_sums",
    )(grad_band)
    return summed.reshape(heads, lanes)


def row_block(meta_ref, slot, rows):
    start = meta_ref[slot] * rows
    return pl.ds(pl.multiple_of(start, 16) if rows % 16 == 0 else start, rows)


def run_copies(pairs, sem):
    copies = [pltpu.make_async_copy(a, b, sem.at[i]) for i, (a, b) in enumerate(pairs)]
    for copy in copies:
        copy.start()
    return copies


def wait_all(copies):
    for copy in copies:
        copy.wait()


def whole_spec():
    return pl.BlockSpec(memory_space=pltpu.VMEM)


def smem_spec():
    return pl.BlockSpec(memory_space=pltpu.SMEM)


def dma(count):
    return pltpu.SemaphoreType.DMA((count,))


def shaped(kind, *shape):
    return jax.ShapeDtypeStruct(shape, kind)


def rows_kernel(width, count, meta_ref, *refs):
    pieces, (full_ref, turned_ref, mask_ref) = refs[:count], refs[count:]
    chip_ids = pieces[0][:, width : width + lanes].astype(f32).T[:1, :]
    for index, piece in enumerate(pieces):
        rows = piece.shape[0]
        grain = min(rows, lanes)
        for part in range(rows // grain):
            start = meta_ref[index] + part * grain
            place = pl.ds(pl.multiple_of(start, grain), grain)
            local = piece[part * grain : (part + 1) * grain, :]
            full_ref[place, :] = local[:, :width]
            wide = local[:, width : width + lanes].astype(f32)
            same = jnp.concatenate([wide, wide], axis=1) == chip_ids
            mask_ref[place, :] = jnp.where(same, 0.0, masked_score)
    for start in range(0, full_ref.shape[0], lanes):
        turned_ref[:, start : start + lanes] = full_ref[start : start + lanes, :].T


def place_rows(pieces, starts, width):
    length = sum(piece.shape[0] for piece in pieces)
    return pl.pallas_call(
        functools.partial(rows_kernel, width, len(pieces)),
        in_specs=[smem_spec()] + [whole_spec()] * len(pieces),
        out_specs=[whole_spec()] * 3,
        out_shape=[
            shaped(bf16, length, width),
            shaped(bf16, width, length),
            shaped(f32, length, 2 * lanes),
        ],
        compiler_params=params(),
        cost_estimate=cost(3e6, 8e6),
        name="place_rows",
    )(starts, *pieces)


def one_head(matrix, half):
    first = lax.broadcasted_iota(jnp.int32, matrix.shape, 1) < matrix.shape[1] // 2
    return jnp.where(first if half == 0 else jnp.logical_not(first), matrix, jnp.zeros_like(matrix))


def band_place(block, chip, part):
    kind = jnp.clip(block - (2 * chip + part) + 2, 0, 4)
    return pl.ds(pl.multiple_of(kind * lanes, lanes), lanes)


def attend_kernel(plan, meta_ref, rows_ref, mask_ref, bias_ref, *refs):
    count = plan[-1][0] + 1
    pieces = refs[:count]
    q_ref, k_ref, v_ref, p_ref, o_ref = refs[count : count + 5]
    weight, score, soft, sem = refs[count + 5 :]
    pair = pl.program_id(0)
    chip = meta_ref[0]
    length = rows_ref.shape[0]
    blocks = length // lanes
    group = 2 * lanes

    @pl.when(pair == 0)
    def _():
        pairs = []
        for index, lead, target, size, slot in plan:
            size = min(size, 3 - target)
            place = row_block(meta_ref, slot, pieces[index].shape[1])
            pairs.append(
                (pieces[index].at[lead : lead + size], weight.at[target : target + size, place, :])
            )
        wait_all(run_copies(pairs, sem))

    cols = pl.ds(pl.multiple_of(pair * lanes, lanes), lanes)
    own = rows_ref[pl.ds(pl.multiple_of(chip * group, group), group), :]
    query = mm(own, weight[0, :, cols]).astype(bf16)
    both = jnp.concatenate([weight[1, :, cols], weight[2, :, cols]], axis=1)
    key_value = mm(rows_ref[...], both).astype(bf16)
    key, value = key_value[:, :lanes], key_value[:, lanes:]
    q_ref[...] = query
    k_ref[...] = key
    v_ref[...] = value
    turned = []
    for half in range(2):
        score[...] = mm_nt(key, one_head(query, half))
        best = jnp.full((8, group), masked_score, f32)
        for block in range(blocks):
            rows = slice(block * lanes, (block + 1) * lanes)
            bias = [bias_ref[half, band_place(block, chip, part), :] for part in range(2)]
            now = score[rows, :] + jnp.concatenate(bias, axis=1) + mask_ref[rows, :]
            score[rows, :] = now
            best = jnp.maximum(best, jnp.max(now.reshape(lanes // 8, 8, group), axis=0))
        top = jnp.max(best, axis=0, keepdims=True)
        total = jnp.zeros((8, group), f32)
        for block in range(blocks):
            rows = slice(block * lanes, (block + 1) * lanes)
            now = jnp.exp(score[rows, :] - top)
            score[rows, :] = now
            total = total + jnp.sum(now.reshape(lanes // 8, 8, group), axis=0)
        inverse = 1.0 / jnp.sum(total, axis=0, keepdims=True)
        for block in range(blocks):
            rows = slice(block * lanes, (block + 1) * lanes)
            now = score[rows, :] * inverse
            p_ref[half, rows, :] = now
            soft[rows, :] = now.astype(bf16)
        features = lanes // 2
        turned.append(mm_tn(value, soft[...])[half * features : (half + 1) * features])
    o_ref[...] = jnp.concatenate(turned, axis=0).T


def attend(plan, pieces, meta, rows, mask, bias):
    length, width = rows.shape
    half = width // 2
    group = 2 * lanes
    pairs = half // lanes
    col = lambda i, *_: (0, i)
    fixed = lambda i, *_: (0, 0)
    flops = 2 * (group * width * half + 2 * length * width * half + 4 * group * length * half)
    return pl.pallas_call(
        functools.partial(attend_kernel, plan),
        grid_spec=pltpu.PrefetchScalarGridSpec(
            num_scalar_prefetch=1,
            grid=(pairs,),
            in_specs=[
                pl.BlockSpec((length, width), fixed),
                pl.BlockSpec((length, group), fixed),
                pl.BlockSpec((2, 5 * lanes, lanes), lambda i, *_: (i, 0, 0)),
            ]
            + [any_spec()] * len(pieces),
            out_specs=[
                pl.BlockSpec((group, lanes), col),
                pl.BlockSpec((length, lanes), col),
                pl.BlockSpec((length, lanes), col),
                pl.BlockSpec((2, length, group), lambda i, *_: (i, 0, 0)),
                pl.BlockSpec((group, lanes), col),
            ],
            scratch_shapes=[
                pltpu.VMEM((3, width, half), bf16),
                pltpu.VMEM((length, group), f32),
                pltpu.VMEM((length, group), bf16),
                dma(len(plan)),
            ],
        ),
        out_shape=[
            shaped(bf16, group, half),
            shaped(bf16, length, half),
            shaped(bf16, length, half),
            shaped(f32, 2 * pairs, length, group),
            shaped(f32, group, half),
        ],
        compiler_params=params(),
        cost_estimate=cost(flops, 30e6, 2 * group * length * pairs),
        name="attend",
    )(meta, rows, mask, bias, *pieces)


def mix_kernel(meta_ref, attended_ref, near_ref, far_ref, part_ref, weight_ref, sem):
    chips, rows, half = near_ref.shape
    rows = rows // 2
    pairs = []
    for index, source in enumerate((near_ref, far_ref)):
        for step in range(chips):
            place = row_block(meta_ref, 1 + index * chips + step, rows)
            for side in range(2):
                pairs.append(
                    (
                        source.at[step, side * rows : (side + 1) * rows, :],
                        weight_ref.at[place, side * half : (side + 1) * half],
                    )
                )
    wait_all(run_copies(pairs, sem))
    core = meta_ref[0]
    mine = weight_ref[pl.ds(pl.multiple_of(core * half, half), half), :]
    part_ref[...] = mm(attended_ref[...].astype(bf16), mine)


def mix(meta, attended, near, far):
    group, half = attended.shape
    width = 2 * half
    return pl.pallas_call(
        mix_kernel,
        in_specs=[smem_spec(), whole_spec(), any_spec(), any_spec()],
        out_specs=[whole_spec()] * 2,
        out_shape=[shaped(f32, group, width), shaped(bf16, width, width)],
        scratch_shapes=[dma(4 * near.shape[0])],
        compiler_params=params(),
        cost_estimate=cost(2 * group * width * half, 4e6),
        name="mix",
    )(meta, attended, near, far)


def feed_kernel(
    gu_plan,
    down_count,
    meta_ref,
    tokens_ref,
    cot_ref,
    part_ref,
    arrived_ref,
    gain_ref,
    *refs,
):
    refs = list(refs)
    take = lambda n: [refs.pop(0) for _ in range(n)]
    gu_pieces = take(gu_plan[-1][0] + 1)
    down_pieces = take(down_count)
    mixed_ref, out_ref, back_ref, gu_out, down_out = take(5)
    gu, down, grad_gu, grad_down, cot_low, normed_low = take(6)
    gu_sem, down_sem, gu_out_sem, down_out_sem = take(4)
    step = pl.program_id(0)
    steps = pl.num_programs(0)
    block = 256
    chips = gu_out.shape[0]

    @pl.when(step == 0)
    def _():
        pairs = []
        for index, lead, target, size, slot in gu_plan:
            place = row_block(meta_ref, slot, gu_pieces[index].shape[1])
            pairs.append(
                (gu_pieces[index].at[lead : lead + size], gu.at[target : target + size, place, :])
            )
        gu_copies = run_copies(pairs, gu_sem)
        pairs = []
        slot = chips
        for piece in down_pieces:
            for index in range(piece.shape[0]):
                place = row_block(meta_ref, slot, piece.shape[1])
                pairs.append((piece.at[index], down.at[place, :]))
                slot += 1
        down_copies = run_copies(pairs, down_sem)
        mixed = tokens_ref[...] + part_ref[...] + arrived_ref[...]
        mixed_ref[...] = mixed
        normed_low[...] = (mixed * rms_scale(mixed) * gain_ref[...]).astype(bf16)
        cot_low[...] = cot_ref[...].astype(bf16)
        out_ref[...] = jnp.zeros_like(out_ref)
        back_ref[...] = jnp.zeros_like(back_ref)
        wait_all(gu_copies)
        wait_all(down_copies)

    cols = pl.ds(pl.multiple_of(step * block, block), block)
    normed = normed_low[...]
    cot = cot_low[...]
    gate_w, up_w, down_w = gu[0, :, cols], gu[1, :, cols], down[cols, :]
    gate, up = mm(normed, gate_w), mm(normed, up_w)
    square = gate * gate
    curve = jnp.tanh(gelu_scale * gate * (1.0 + gelu_cubic * square))
    half = 0.5 * (1.0 + curve)
    gelu = gate * half
    slope = half + 0.5 * gate * (1.0 - curve * curve) * gelu_scale * (1.0 + 3.0 * gelu_cubic * square)
    hidden = (gelu * up).astype(bf16)
    dh = mm_nt(cot, down_w)
    dgate = (dh * up * slope).astype(bf16)
    dup = (dh * gelu).astype(bf16)
    out_ref[...] += mm(hidden, down_w)
    back_ref[...] += mm_nt(dgate, gate_w) + mm_nt(dup, up_w)
    grad_down[cols, :] = mm_tn(hidden, cot).astype(bf16)
    grad_gu[0, :, cols] = mm_tn(normed, dgate).astype(bf16)
    grad_gu[1, :, cols] = mm_tn(normed, dup).astype(bf16)

    @pl.when(step == steps - 1)
    def _():
        pairs = []
        for index in range(chips):
            place = row_block(meta_ref, index, gu_out.shape[2])
            pairs.append((grad_gu.at[:, place, :], gu_out.at[index]))
        gu_copies = run_copies(pairs, gu_out_sem)
        pairs = []
        for index in range(chips):
            place = row_block(meta_ref, index, down_out.shape[1])
            pairs.append((grad_down.at[place, :], down_out.at[index]))
        down_copies = run_copies(pairs, down_out_sem)
        wait_all(gu_copies)
        wait_all(down_copies)


def feed(gu_plan, gu_pieces, down_pieces, meta, tokens, cot, part, arrived, gain, chips):
    group, width = tokens.shape
    hidden = gu_pieces[0].shape[2]
    block = 256
    fixed = lambda i, *_: (0, 0)
    full = lambda *shape: pl.BlockSpec(shape, fixed)
    flops = 2 * 9 * group * width * hidden
    down_copies = sum(piece.shape[0] for piece in down_pieces)
    return pl.pallas_call(
        functools.partial(feed_kernel, gu_plan, len(down_pieces)),
        grid_spec=pltpu.PrefetchScalarGridSpec(
            num_scalar_prefetch=1,
            grid=(hidden // block,),
            in_specs=[full(group, width)] * 4
            + [full(1, width)]
            + [any_spec()] * (len(gu_pieces) + len(down_pieces)),
            out_specs=[full(group, width)] * 3 + [any_spec()] * 2,
            scratch_shapes=[
                pltpu.VMEM((2, width, hidden), bf16),
                pltpu.VMEM((hidden, width), bf16),
                pltpu.VMEM((2, width, hidden), bf16),
                pltpu.VMEM((hidden, width), bf16),
                pltpu.VMEM((group, width), bf16),
                pltpu.VMEM((group, width), bf16),
                dma(len(gu_plan)),
                dma(down_copies),
                dma(chips),
                dma(chips),
            ],
        ),
        out_shape=[shaped(f32, group, width)] * 3
        + [shaped(bf16, chips, 2, width // chips, hidden), shaped(bf16, chips, hidden // chips, width)],
        compiler_params=params(),
        cost_estimate=cost(flops, 25e6, group * hidden),
        name="feed",
    )(meta, tokens, cot, part, arrived, gain, *gu_pieces, *down_pieces)


def settle_kernel(
    meta_ref,
    mixed_ref,
    cot_ref,
    back_ref,
    arrived_ref,
    attended_ref,
    weight_ref,
    gain_ref,
    dmixed_ref,
    do_ref,
    gain_grad_ref,
    near_ref,
    far_ref,
):
    core = meta_ref[0]
    half = attended_ref.shape[1]
    mixed = mixed_ref[...]
    scale = rms_scale(mixed)
    dn2 = back_ref[...] + arrived_ref[...]
    gained = dn2 * gain_ref[...]
    inner = jnp.mean(gained * mixed, axis=-1, keepdims=True)
    dmixed = cot_ref[...] + scale * gained - mixed * (scale * scale * scale * inner)
    dmixed_ref[...] = dmixed
    gain_grad_ref[...] = 0.5 * jnp.sum(dn2 * mixed * scale, axis=0, keepdims=True)
    branch = dmixed.astype(bf16)
    mine = weight_ref[pl.ds(pl.multiple_of(core * half, half), half), :]
    do_ref[...] = mm_nt(branch, mine).astype(bf16)
    grad = mm_tn(attended_ref[...].astype(bf16), branch).astype(bf16)
    count, rows = near_ref.shape[0], near_ref.shape[1]
    blocks = [grad[i * rows : (i + 1) * rows] for i in range(2 * count)]
    for index in range(count):
        even, odd = blocks[2 * index], blocks[2 * index + 1]
        near_ref[index] = jnp.where(core == 0, even, odd)
        far_ref[index] = jnp.where(core == 0, odd, even)


def settle(meta, mixed, cot, back, arrived, attended, weight, gain, chips):
    group, width = mixed.shape
    half = width // 2
    rows = half // chips
    return pl.pallas_call(
        settle_kernel,
        in_specs=[smem_spec()] + [whole_spec()] * 7,
        out_specs=[whole_spec()] * 5,
        out_shape=[
            shaped(f32, group, width),
            shaped(bf16, group, half),
            shaped(f32, 1, width),
            shaped(bf16, chips // 2, rows, width),
            shaped(bf16, chips // 2, rows, width),
        ],
        compiler_params=params(),
        cost_estimate=cost(4 * group * width * half, 6e6),
        name="settle",
    )(meta, mixed, cot, back, arrived, attended, weight, gain)


def retreat_kernel(meta_ref, do_ref, o_ref, q_ref, k_ref, v_ref, p_ref, dq_ref, dkv_ref, band_ref, low, sums):
    chip = meta_ref[0]
    blocks = k_ref.shape[0] // lanes
    group = 2 * lanes
    features = lanes // 2
    do = do_ref[...]
    spread = (do.astype(f32) * o_ref[...]).T
    band_ref[...] = jnp.zeros_like(band_ref)
    turned = []
    for half in range(2):
        do_half, query_half = one_head(do, half), one_head(q_ref[...], half)
        delta = jnp.sum(spread[half * features : (half + 1) * features], axis=0, keepdims=True)
        for block in range(blocks):
            rows = slice(block * lanes, (block + 1) * lanes)
            soft = p_ref[half, rows, :]
            ds = soft * (mm_nt(v_ref[rows, :], do_half) - delta)
            for part in range(2):
                place = band_place(block, chip, part)
                band_ref[half, place, :] += ds[:, part * lanes : (part + 1) * lanes]
            ds_low = ds.astype(bf16)
            low[rows, :] = ds_low
            dk = mm(ds_low, query_half)
            dv = mm(soft.astype(bf16), do_half)
            if half == 0:
                sums[rows, :lanes] = dk
                sums[rows, lanes:] = dv
            else:
                dkv_ref[rows, :lanes] = (sums[rows, :lanes] + dk).astype(bf16)
                dkv_ref[rows, lanes:] = (sums[rows, lanes:] + dv).astype(bf16)
        turned.append(mm_tn(k_ref[...], low[...])[half * features : (half + 1) * features])
    dq_ref[...] = jnp.concatenate(turned, axis=0).T.astype(bf16)


def retreat(meta, do, o, q, k, v, p):
    length, half = k.shape
    group = do.shape[0]
    pairs = half // lanes
    col = lambda i, *_: (0, i)
    deep = lambda i, *_: (i, 0, 0)
    flops = 2 * 8 * group * length * half
    return pl.pallas_call(
        retreat_kernel,
        grid_spec=pltpu.PrefetchScalarGridSpec(
            num_scalar_prefetch=1,
            grid=(pairs,),
            in_specs=[
                pl.BlockSpec((group, lanes), col),
                pl.BlockSpec((group, lanes), col),
                pl.BlockSpec((group, lanes), col),
                pl.BlockSpec((length, lanes), col),
                pl.BlockSpec((length, lanes), col),
                pl.BlockSpec((2, length, group), deep),
            ],
            out_specs=[
                pl.BlockSpec((group, lanes), col),
                pl.BlockSpec((length, 2 * lanes), col),
                pl.BlockSpec((2, 5 * lanes, lanes), deep),
            ],
            scratch_shapes=[
                pltpu.VMEM((length, group), bf16),
                pltpu.VMEM((length, 2 * lanes), f32),
            ],
        ),
        out_shape=[
            shaped(bf16, group, half),
            shaped(bf16, length, 2 * half),
            shaped(f32, 2 * pairs, 5 * lanes, lanes),
        ],
        compiler_params=params(),
        cost_estimate=cost(flops, 20e6),
        name="retreat",
    )(meta, do, o, q, k, v, p)


def grads_kernel(plan, meta_ref, rows_ref, turned_ref, dq_ref, dkv_ref, gain_ref, near_wo, far_wo, *refs):
    refs = list(refs)
    take = lambda n: [refs.pop(0) for _ in range(n)]
    pieces = take(plan[-1][0] + 1)
    grad_out, near_out, far_out, gain_grad_ref = take(4)
    weight, both, grad, back = take(4)
    sem, grad_sem, wo_sem, row_sem = take(4)
    chip, core = meta_ref[0], meta_ref[1]
    length, width = rows_ref.shape
    half = width // 2
    group = dq_ref.shape[0]
    chips = grad_out.shape[0]
    slots = 2
    pairs = []
    for index, lead, target, size, slot in plan:
        size = min(size, 3 - target)
        place = row_block(meta_ref, slots + slot, pieces[index].shape[1])
        pairs.append((pieces[index].at[lead : lead + size], weight.at[target : target + size, place, :]))
    loads = run_copies(pairs, sem)
    pairs = []
    rows = near_wo.shape[1]
    for source, owner in ((near_wo, core), (far_wo, 1 - core)):
        for index in range(near_wo.shape[0]):
            target = owner * (chips // 2) + index
            for side in range(2):
                pairs.append(
                    (
                        source.at[index, :, side * half : (side + 1) * half],
                        grad_out.at[chip ^ target, 3, side * rows : (side + 1) * rows, :],
                    )
                )
    wo_copies = run_copies(pairs, wo_sem)
    own_rows = pl.ds(pl.multiple_of(chip * group, group), group)
    grad[0] = mm_tn(rows_ref[own_rows, :], dq_ref[...]).astype(bf16)
    for pair in range(half // lanes):
        wide = slice(pair * 2 * lanes, (pair + 1) * 2 * lanes)
        cols = slice(pair * lanes, (pair + 1) * lanes)
        summed = mm(turned_ref[...], dkv_ref[:, wide]).astype(bf16)
        grad[1, :, cols] = summed[:, :lanes]
        grad[2, :, cols] = summed[:, lanes:]
    pairs = []
    for index in range(chips):
        place = row_block(meta_ref, slots + index, grad_out.shape[2])
        pairs.append((grad.at[:, place, :], grad_out.at[index, 0:3]))
    grad_copies = run_copies(pairs, grad_sem)
    wait_all(loads)
    for pair in range(half // lanes):
        wide = pair * 2 * lanes
        cols = slice(pair * lanes, (pair + 1) * lanes)
        both[:, wide : wide + lanes] = weight[1, :, cols]
        both[:, wide + lanes : wide + 2 * lanes] = weight[2, :, cols]
    for start in range(0, length, group):
        back[start : start + group, :] = mm_nt(dkv_ref[start : start + group, :], both[...])
    back[own_rows, :] += mm_nt(dq_ref[...], weight[0])
    gain_sum = jnp.zeros((8, width), f32)
    for start in range(0, length, lanes):
        both_rows = back[start : start + lanes, :] * rows_ref[start : start + lanes, :].astype(f32)
        gain_sum = gain_sum + jnp.sum(both_rows.reshape(lanes // 8, 8, width), axis=0)
    gain_grad_ref[...] = jnp.sum(gain_sum, axis=0, keepdims=True) / gain_ref[...]
    for index in range(chips):
        for side, out in ((core, near_out), (1 - core, far_out)):
            start = meta_ref[slots + index] * group + side * lanes
            out[index] = back[pl.ds(pl.multiple_of(start, lanes), lanes), :].astype(bf16)
    wait_all(grad_copies)
    wait_all(wo_copies)


def weight_grads(plan, pieces, meta, rows, turned, dq, dkv, gain, near_wo, far_wo, chips):
    length, width = rows.shape
    half = width // 2
    group = dq.shape[0]
    flops = 2 * (4 * length * width * half + 2 * group * width * half)
    return pl.pallas_call(
        functools.partial(grads_kernel, plan),
        in_specs=[smem_spec()] + [whole_spec()] * 7 + [any_spec()] * len(pieces),
        out_specs=[any_spec()] + [whole_spec()] * 3,
        out_shape=[
            shaped(bf16, chips, 4, width // chips, half),
            shaped(bf16, chips, lanes, width),
            shaped(bf16, chips, lanes, width),
            shaped(f32, 1, width),
        ],
        scratch_shapes=[
            pltpu.VMEM((3, width, half), bf16),
            pltpu.VMEM((width, width), bf16),
            pltpu.VMEM((3, width, half), bf16),
            pltpu.VMEM((length, width), f32),
            dma(len(plan)),
            dma(chips),
            dma(2 * chips),
            dma(1),
        ],
        compiler_params=params(),
        cost_estimate=cost(flops, 20e6),
        name="weight_grads",
    )(meta, rows, turned, dq, dkv, gain, near_wo, far_wo, *pieces)


def core_swap(value):
    count = lax.axis_size("seq")
    return lax.ppermute(value, "seq", [(i, i ^ 1) for i in range(count)])


def plane_swap(value, step):
    count = lax.axis_size("seq")
    return lax.ppermute(value, "seq", [(i, i ^ (2 * step)) for i in range(count)])


def along(value, step):
    count = lax.axis_size("batch")
    return lax.ppermute(value, "batch", [(i, (i + step) % count) for i in range(count)])


def along_all(value):
    return [value] + [along(value, step) for step in range(1, lax.axis_size("batch"))]


def after(value, *earlier):
    return lax.optimization_barrier((value,) + earlier)[0]


def join_kernel(order_ref, *refs):
    sources, out = refs[:-1], refs[-1]
    for index, source in enumerate(sources):
        out[:, :, order_ref[index]] = source[...]


def join(blocks, order):
    lead, rest = blocks[0].shape[:2], blocks[0].shape[2:]
    return pl.pallas_call(
        join_kernel,
        in_specs=[smem_spec()] + [whole_spec()] * len(blocks),
        out_specs=whole_spec(),
        out_shape=shaped(bf16, *lead, len(blocks), *rest),
        compiler_params=params(),
        cost_estimate=cost(0, 2e6),
        name="join",
    )(order, *blocks)


def gather_plane(value):
    chips = lax.axis_size("seq") // 2
    size = value.shape[0]
    if chips != 4:
        pieces = [value] + [plane_swap(value, step) for step in range(1, chips)]
        return pieces, [(step, 0, 0, size, step) for step in range(chips)]
    first, second = plane_swap(value, 1), plane_swap(value, 2)
    low, high = plane_swap(first[: size // 2], 2), plane_swap(second[size // 2 :], 1)
    plan = [(0, 0, 0, size, 0), (1, 0, 0, size, 1), (2, 0, 0, size, 2)]
    plan += [(3, 0, 0, size // 2, 3), (4, 0, size // 2, size - size // 2, 3)]
    return [value, first, second, low, high], plan


def total(blocks):
    summed = blocks[0].astype(f32)
    for block in blocks[1:]:
        summed = summed + block.astype(f32)
    return summed


def scatter_plane(blocks):
    chips = len(blocks)
    if chips != 4:
        return total(blocks[:1] + [plane_swap(blocks[step], step) for step in range(1, chips)])
    cut = blocks[3].shape[0] // 2
    low, high = plane_swap(blocks[3][:cut], 1), plane_swap(blocks[3][cut:], 2)
    add = lambda a, b: total([a, b]).astype(bf16)
    second = jnp.concatenate([add(blocks[2][:cut], low), blocks[2][cut:]], axis=0)
    first = jnp.concatenate([blocks[1][:cut], add(blocks[1][cut:], high)], axis=0)
    return total([blocks[0], plane_swap(first, 1), plane_swap(second, 2)])


def scatter_direct(blocks):
    chips = len(blocks)
    return total(blocks[:1] + [plane_swap(blocks[step], step) for step in range(1, chips)])


def scatter_along(split, dim, place):
    count = lax.axis_size("batch")
    pick = lambda step: lax.dynamic_index_in_dim(split, (place + step) % count, dim, keepdims=False)
    return total([pick(0)] + [along(pick(step).astype(bf16), step) for step in range(1, count)])


def shards(
    tokens,
    cotangent,
    group_ids,
    attention_weight,
    ffin_weight,
    ffout_weight,
    bias_table,
    gains,
    attention_momentum,
    ffin_momentum,
    ffout_momentum,
    bias_momentum,
    gain_momentum,
    attention_average,
    ffin_average,
    ffout_average,
    bias_average,
    gain_average,
):
    _, tok, width = tokens.shape
    cycle_size, places = lax.axis_size("seq"), lax.axis_size("batch")
    cycle_index = lax.axis_index("seq").astype(jnp.int32)
    place = lax.axis_index("batch").astype(jnp.int32)
    chips = cycle_size // 2
    chip, core = cycle_index // 2, cycle_index % 2
    half = width // 2
    rows = attention_weight.shape[1]
    down_rows = ffout_weight.shape[0]
    hidden = ffin_weight.shape[2]
    grain = hidden // cycle_size
    heads = bias_table.shape[1]
    group = 2 * tok
    first_core = core == 0

    def by_core(mine, theirs):
        return [jnp.where(first_core, mine, theirs), jnp.where(first_core, theirs, mine)]

    steps = [chip ^ step for step in range(chips)]
    order = jnp.stack([(place + places - step) % places for step in range(places)])
    flat_tokens, flat_cot = tokens.reshape(tok, width), cotangent.reshape(tok, width)

    attention_low = attention_weight.astype(bf16)
    sides = [attention_low[..., :half], attention_low[..., half:]]
    own_side = jnp.where(first_core, sides[0][:3], sides[1][:3])
    their_side = core_swap(jnp.where(first_core, sides[1][:3], sides[0][:3]))
    attn_block = jnp.concatenate(
        [jnp.stack(by_core(own_side, their_side), axis=1), jnp.stack([sides[0][3], sides[1][3]])[None]],
        axis=0,
    )
    ffin_cut = ffin_weight.astype(bf16).reshape(2, rows, chips, 2, grain)
    sides = [ffin_cut[:, :, :, side].reshape(2, rows, hidden // 2) for side in range(2)]
    own_side = jnp.where(first_core, sides[0], sides[1])
    their_side = core_swap(jnp.where(first_core, sides[1], sides[0]))
    gu_block = jnp.stack(by_core(own_side, their_side), axis=1)
    down_block = ffout_weight.astype(bf16)

    ids_wide = jnp.broadcast_to(group_ids.reshape(tok, 1), (tok, lanes)).astype(bf16)
    normed = flat_tokens * rms_scale(flat_tokens) * gains[0]
    own_rows = jnp.concatenate([normed.astype(bf16), ids_wide], axis=1)
    chip_rows = jnp.concatenate(by_core(own_rows, core_swap(own_rows)), axis=0)
    chip_tokens = jnp.concatenate(by_core(flat_tokens, core_swap(flat_tokens)), axis=0)
    chip_cot = jnp.concatenate(by_core(flat_cot, core_swap(flat_cot)), axis=0)

    row_pieces, row_plan = gather_plane(own_rows)
    near_rows = jnp.concatenate(row_pieces[1:], axis=0)
    far_rows = core_swap(near_rows)
    starts = [chip * group]
    pieces = [chip_rows]
    for source, side in ((near_rows, core), (far_rows, 1 - core)):
        offset = 0
        for _, _, target, size, step in row_plan[1:]:
            starts.append(steps[step] * group + side * tok + target)
            pieces.append(source[offset : offset + size])
            offset += size
    rows_full, turned, mask = place_rows(pieces, jnp.stack(starts), width)
    own_heads = jnp.where(first_core, bias_table[:, : heads // 2], bias_table[:, heads // 2 :])
    bias = bias_rows(own_heads)

    attn_joined = join(along_all(attn_block), order).reshape(4, 2 * places * rows, half)
    attn_pieces, attn_plan = gather_plane(attn_joined)
    gu_joined = join(along_all(gu_block), order).reshape(2, 2 * places * rows, hidden // 2)
    gu_pieces, gu_plan = gather_plane(gu_joined)
    down_near, down_plan = gather_plane(down_block)
    if chips == 4:
        down_near = down_near[:3] + [jnp.concatenate(down_near[3:], axis=0)]
    down_pieces = along_all(jnp.stack(down_near))

    step_meta = jnp.stack(steps)
    query, key, value, soft, attended = attend(
        attn_plan, attn_pieces, step_meta, rows_full, mask, bias
    )
    wo_near = jnp.stack([attn_pieces[i][lead + 3 - target] for i, lead, target, size, _ in attn_plan if target + size == 4])
    wo_far = core_swap(wo_near)
    wo_meta = jnp.stack([core] + [step * 2 + core for step in steps] + [step * 2 + 1 - core for step in steps])
    part, out_weight = mix(wo_meta, attended, wo_near, wo_far)
    down_meta = [step * places + order[index] for index in range(places) for step in steps]
    mixed, out_part, back_part, gu_grads, down_grads = feed(
        gu_plan,
        gu_pieces,
        down_pieces,
        jnp.stack(steps + down_meta),
        chip_tokens,
        chip_cot,
        part,
        core_swap(part),
        gains[1:2],
        chips,
    )
    dmixed, attended_grad, second_gain, near_wo, far_wo = settle(
        core.reshape(1), mixed, chip_cot, back_part, core_swap(back_part), attended, out_weight, gains[1:2], chips
    )
    mine = lambda value: lax.dynamic_slice_in_dim(value, core * tok, tok, 0)
    theirs = lambda value: lax.dynamic_slice_in_dim(value, (1 - core) * tok, tok, 0)
    layer_output = mine(mixed) + mine(out_part) + core_swap(theirs(out_part))

    dq, dkv, band = retreat(chip.reshape(1), attended_grad, attended, query, key, value, soft)
    attn_grads, near_back, far_back, first_gain = weight_grads(
        attn_plan,
        attn_pieces,
        jnp.stack([chip, core] + steps),
        rows_full,
        turned,
        dq,
        dkv,
        gains[:1],
        near_wo,
        core_swap(far_wo),
        chips,
    )
    bias_part = bias_sums(band)[:, : bias_table.shape[0]].T

    def own_columns(summed, columns):
        keep = jnp.where(first_core, summed[:, 0], summed[:, 1])
        send = jnp.where(first_core, summed[:, 1], summed[:, 0])
        return columns(by_core(keep, core_swap(send)))

    gu_sum = scatter_plane([gu_grads[step] for step in range(chips)]).astype(bf16)
    gu_sum = scatter_along(gu_sum.reshape(2, 2, places, rows, hidden // 2), 2, place)
    weave = lambda parts: jnp.stack(
        [part.reshape(2, rows, chips, grain) for part in parts], axis=3
    ).reshape(2, rows, hidden)
    own_gu = own_columns(gu_sum, weave)
    down_sum = scatter_along(down_grads.reshape(chips, places, down_rows, width), 1, place).astype(bf16)
    own_down = scatter_direct([down_sum[step] for step in range(chips)])
    attn_sum = scatter_direct([attn_grads[step] for step in range(chips)]).astype(bf16)
    attn_sum = scatter_along(attn_sum.reshape(4, 2, places, rows, half), 2, place)
    own_qkv = own_columns(attn_sum[:3], lambda parts: jnp.concatenate(parts, axis=-1))
    own_wo = jnp.concatenate([attn_sum[3, 0], attn_sum[3, 1]], axis=-1)
    own_attention = jnp.concatenate([own_qkv, own_wo[None]], axis=0)

    arrived = core_swap(far_back)
    merged = [total([near_back[step], arrived[step]]).astype(bf16) for step in range(chips)]
    first_grad = scatter_direct(merged)
    scale = rms_scale(flat_tokens)
    gained = first_grad * gains[0]
    inner = jnp.mean(gained * flat_tokens, axis=-1, keepdims=True)
    input_grad = mine(dmixed) + scale * gained - flat_tokens * (scale**3 * inner)

    none = jnp.zeros_like(bias_part)
    bias_wide = jnp.concatenate(by_core(bias_part, none), axis=1)
    small = jnp.concatenate([bias_wide.reshape(-1), first_gain[0], second_gain[0]]).reshape(-1, lanes)
    small = small + core_swap(small)
    small = scatter_direct([small] * chips)
    small = total(along_all(small)).reshape(-1)
    bias_reduced = small[: bias_table.size].reshape(bias_table.shape)
    gains_reduced = small[bias_table.size :].reshape(gains.shape)

    all_tokens = lax.axis_size("batch") * tok * cycle_size
    inverse_root = 1.0 / math.sqrt(all_tokens)
    attention_rate = jnp.array(attention_rates, dtype=f32)[:, None, None] * inverse_root
    gain_rate = jnp.array(gain_rates, dtype=f32)[:, None] * inverse_root
    attn_new = update(
        attention_weight, own_attention, attention_momentum, attention_average, attention_rate
    )
    ffin_new = update(
        ffin_weight, own_gu, ffin_momentum, ffin_average, ffin_rate * inverse_root
    )
    ffout_new = update(
        ffout_weight, own_down, ffout_momentum, ffout_average, ffout_rate * inverse_root
    )
    bias_new = update(bias_table, bias_reduced, bias_momentum, bias_average, bias_rate * inverse_root)
    gain_new = update(gains, gains_reduced, gain_momentum, gain_average, gain_rate)
    return (
        layer_output.reshape(tokens.shape),
        input_grad.reshape(tokens.shape),
        attn_new[0],
        ffin_new[0],
        ffout_new[0],
        bias_new[0],
        gain_new[0],
        attn_new[1],
        ffin_new[1],
        ffout_new[1],
        bias_new[1],
        gain_new[1],
        attn_new[2],
        ffin_new[2],
        ffout_new[2],
        bias_new[2],
        gain_new[2],
        attn_new[0].astype(bf16),
        ffin_new[0].astype(bf16),
        ffout_new[0].astype(bf16),
    )


def solution(mesh):
    rows = P("batch", "seq", None)
    stacked = P(None, ("seq", "batch"), None)
    single = P(("seq", "batch"), None)
    weights = (stacked, stacked, single, P(), P())
    return jax.shard_map(
        shards,
        mesh=mesh,
        in_specs=(rows, rows, P("batch", "seq")) + weights * 3,
        out_specs=(rows, rows) + weights * 3 + (stacked, stacked, single),
        check_vma=False,
    )
```

```python
import functools
import math

import jax
import jax.numpy as jnp
from jax import lax
from jax.experimental import pallas as pl
from jax.experimental.pallas import tpu as pltpu
from jax.sharding import PartitionSpec as P

eps_norm = 1e-06
momentum_coef = 0.5
average_coef = 0.5
attention_rates = (0.0033, 0.0033, 0.025, 0.2)
ffin_rate = 0.063
ffout_rate = 0.023
bias_rate = 0.08
gain_rates = (0.045, 0.22)
thresholds = (12, 16, 23, 32, 46, 64, 91)
masked_score = -1e30
gelu_scale = math.sqrt(2.0 / math.pi)
gelu_cubic = 0.044715
bf16 = jnp.bfloat16
f32 = jnp.float32
vmem_bytes = 60 * 1024 * 1024
lanes = 128


def product(left, right, left_dim, right_dim):
    return lax.dot_general(
        left, right, (((left_dim,), (right_dim,)), ((), ())), preferred_element_type=f32
    )


def mm(left, right):
    return product(left, right, 1, 0)


def mm_nt(left, right):
    return product(left, right, 1, 1)


def mm_tn(left, right):
    return product(left, right, 0, 0)


def bucket_of(offset):
    magnitude = jnp.abs(offset)
    beyond = jnp.zeros_like(offset)
    for threshold in thresholds:
        beyond = beyond + (magnitude >= threshold).astype(jnp.int32)
    inside = jnp.where(magnitude < 8, magnitude, 8 + beyond)
    return inside + 16 * (offset > 0).astype(jnp.int32)


def update(weight, grad, momentum, average, rate):
    new_momentum = momentum_coef * momentum + grad
    new_weight = weight - rate * (grad + momentum_coef * new_momentum)
    new_average = average_coef * average + (1.0 - average_coef) * new_weight
    return (new_weight, new_momentum, new_average)


def rms_scale(values):
    return lax.rsqrt(jnp.mean(values * values, axis=-1, keepdims=True) + eps_norm)


def params():
    return pltpu.CompilerParams(vmem_limit_bytes=vmem_bytes)


def any_spec():
    return pl.BlockSpec(memory_space=pl.ANY)


def cost(flops, nbytes, exps=0):
    return pl.CostEstimate(flops=1, bytes_accessed=1, transcendentals=0)


def bias_kernel(table_ref, out_ref):
    head = pl.program_id(0)
    spot = lax.broadcasted_iota(jnp.int32, (8, 2 * lanes), 1)
    for block in range(3):
        buckets = bucket_of(lanes * (block - 1) + lanes - 1 - spot)
        row = jnp.zeros((8, 2 * lanes), f32)
        for bucket in range(table_ref.shape[0]):
            row = jnp.where(buckets == bucket, table_ref[bucket, head], row)
        wide = jnp.broadcast_to(row[:1], (lanes, 2 * lanes))
        rolled = pltpu.roll(wide, lanes + 1, 1, stride=1, stride_axis=0)
        out_ref[0, lanes * (block + 1) : lanes * (block + 2), :] = rolled[:, :lanes]
    out_ref[0, 0:lanes, :] = jnp.full((lanes, lanes), table_ref[15, head], f32)
    out_ref[0, 4 * lanes : 5 * lanes, :] = jnp.full((lanes, lanes), table_ref[31, head], f32)


def bias_rows(table):
    heads = table.shape[1]
    return pl.pallas_call(
        bias_kernel,
        grid=(heads,),
        in_specs=[pl.BlockSpec(memory_space=pltpu.SMEM)],
        out_specs=pl.BlockSpec((1, 5 * lanes, lanes), lambda i: (i, 0, 0)),
        out_shape=jax.ShapeDtypeStruct((heads, 5 * lanes, lanes), f32),
        compiler_params=params(),
        cost_estimate=cost(heads * 3e6, 4e6),
        name="bias_rows",
    )(table)


def ready_kernel(meta_ref, attn_ref, ffin_ref, ffout_ref, tokens_ref, ids_ref, gain_ref, *outs):
    attn_out, attn_send, gu_out, gu_send, row_out, down_out = outs
    down_out[...] = ffout_ref[...].astype(bf16)
    core = meta_ref[0]
    first = core == 0
    width = tokens_ref.shape[1]
    half = width // 2
    low = attn_ref[...].astype(bf16)
    left, right = low[..., :half], low[..., half:]
    attn_out[0:3, core] = jnp.where(first, left[:3], right[:3])
    attn_send[...] = jnp.where(first, right[:3], left[:3])
    attn_out[3, 0] = left[3]
    attn_out[3, 1] = right[3]
    grain = ffin_ref.shape[2] // (2 * meta_ref.shape[0])
    for index in range(meta_ref.shape[0]):
        start = 2 * index * grain
        even = ffin_ref[:, :, start : start + grain].astype(bf16)
        odd = ffin_ref[:, :, start + grain : start + 2 * grain].astype(bf16)
        cols = slice(index * grain, (index + 1) * grain)
        gu_out[:, core, :, cols] = jnp.where(first, even, odd)
        gu_send[:, :, cols] = jnp.where(first, odd, even)
    tok = tokens_ref.shape[0]
    tokens = tokens_ref[...]
    row_out[:tok, :] = (tokens * rms_scale(tokens) * gain_ref[0:1, :]).astype(bf16)
    ids = jnp.broadcast_to(ids_ref[...].astype(f32), (16, tok))
    ids = jnp.concatenate([ids, jnp.zeros((16, width - tok), f32)], axis=1)
    row_out[tok:, :] = ids.astype(bf16)


def make_ready(core, attention_weight, ffin_weight, ffout_weight, tokens, ids, gain, chips):
    tok, width = tokens.shape
    rows, half, hidden = attention_weight.shape[1], width // 2, ffin_weight.shape[2]
    return pl.pallas_call(
        ready_kernel,
        in_specs=[smem_spec()] + [whole_spec()] * 6,
        out_specs=[whole_spec()] * 6,
        out_shape=[
            shaped(bf16, 4, 2, rows, half),
            shaped(bf16, 3, rows, half),
            shaped(bf16, 2, 2, rows, hidden // 2),
            shaped(bf16, 2, rows, hidden // 2),
            shaped(bf16, tok + 16, width),
            shaped(bf16, *ffout_weight.shape),
        ],
        compiler_params=params(),
        cost_estimate=cost(1e6, 2e6),
        name="make_ready",
    )(jnp.broadcast_to(core, (chips,)), attention_weight, ffin_weight, ffout_weight, tokens, ids, gain)


def fill_kernel(core_ref, kept_ref, arrived_ref, out_ref):
    count = arrived_ref.shape[0]
    out_ref[...] = kept_ref[...]
    out_ref[0:count, 1 - core_ref[0]] = arrived_ref[...]


def fill(core, kept, arrived):
    return pl.pallas_call(
        fill_kernel,
        in_specs=[smem_spec(), whole_spec(), whole_spec()],
        out_specs=whole_spec(),
        out_shape=shaped(bf16, *kept.shape),
        compiler_params=params(),
        cost_estimate=cost(0, 1e6),
        name="fill",
    )(core.reshape(1), kept, arrived)


def row_block(meta_ref, slot, rows):
    start = meta_ref[slot] * rows
    return pl.ds(pl.multiple_of(start, 16) if rows % 16 == 0 else start, rows)


def run_copies(pairs, sem):
    copies = [pltpu.make_async_copy(a, b, sem.at[i]) for i, (a, b) in enumerate(pairs)]
    for copy in copies:
        copy.start()
    return copies


def wait_all(copies):
    for copy in copies:
        copy.wait()


def whole_spec():
    return pl.BlockSpec(memory_space=pltpu.VMEM)


def smem_spec():
    return pl.BlockSpec(memory_space=pltpu.SMEM)


def dma(count):
    return pltpu.SemaphoreType.DMA((count,))


def shaped(kind, *shape):
    return jax.ShapeDtypeStruct(shape, kind)


def rows_kernel(meta_ref, near_ref, far_ref, full_ref, turned_ref, mask_ref):
    chips = near_ref.shape[0]
    core = meta_ref[chips]
    groups = lambda block: block[lanes : lanes + 16, :lanes].astype(f32)[:1, :]
    mine, other = groups(near_ref[0]), groups(far_ref[0])
    chip_ids = jnp.where(
        core == 0,
        jnp.concatenate([mine, other], axis=1),
        jnp.concatenate([other, mine], axis=1),
    )
    for source, side in ((near_ref, core), (far_ref, 1 - core)):
        for step in range(chips):
            block = source[step]
            start = (meta_ref[step] * 2 + side) * lanes
            place = pl.ds(pl.multiple_of(start, lanes), lanes)
            normed = block[:lanes, :]
            full_ref[place, :] = normed
            turned_ref[:, place] = normed.T
            wide = jnp.broadcast_to(groups(block), (lanes, lanes)).T
            same = jnp.concatenate([wide, wide], axis=1) == chip_ids
            mask_ref[place, :] = jnp.where(same, 0.0, masked_score)


def place_rows(meta, near, far):
    chips, _, width = near.shape
    length = 2 * chips * lanes
    return pl.pallas_call(
        rows_kernel,
        in_specs=[smem_spec()] + [whole_spec()] * 2,
        out_specs=[whole_spec()] * 3,
        out_shape=[
            shaped(bf16, length, width),
            shaped(bf16, width, length),
            shaped(f32, length, 2 * lanes),
        ],
        compiler_params=params(),
        cost_estimate=cost(3e6, 8e6),
        name="place_rows",
    )(meta, near, far)


def one_head(matrix, half):
    first = lax.broadcasted_iota(jnp.int32, matrix.shape, 1) < matrix.shape[1] // 2
    return jnp.where(first if half == 0 else jnp.logical_not(first), matrix, jnp.zeros_like(matrix))


def band_place(block, chip, part):
    kind = jnp.clip(block - (2 * chip + part) + 2, 0, 4)
    return pl.ds(pl.multiple_of(kind * lanes, lanes), lanes)


def attend_kernel(plan, meta_ref, rows_ref, mask_ref, bias_ref, *refs):
    count = plan[-1][0] + 1
    pieces = refs[:count]
    q_ref, k_ref, v_ref, p_ref, o_ref = refs[count : count + 5]
    weight, score, soft, sem = refs[count + 5 :]
    pair = pl.program_id(0)
    chip = meta_ref[0]
    length = rows_ref.shape[0]
    blocks = length // lanes
    group = 2 * lanes

    @pl.when(pair == 0)
    def _():
        pairs = []
        for index, lead, target, size, slot in plan:
            size = min(size, 3 - target)
            place = row_block(meta_ref, slot, pieces[index].shape[1])
            pairs.append(
                (pieces[index].at[lead : lead + size], weight.at[target : target + size, place, :])
            )
        wait_all(run_copies(pairs, sem))

    cols = pl.ds(pl.multiple_of(pair * lanes, lanes), lanes)
    own = rows_ref[pl.ds(pl.multiple_of(chip * group, group), group), :]
    query = mm(own, weight[0, :, cols]).astype(bf16)
    both = jnp.concatenate([weight[1, :, cols], weight[2, :, cols]], axis=1)
    key_value = mm(rows_ref[...], both).astype(bf16)
    key, value = key_value[:, :lanes], key_value[:, lanes:]
    q_ref[...] = query
    k_ref[...] = key
    v_ref[...] = value
    turned = []
    for half in range(2):
        score[...] = mm_nt(key, one_head(query, half))
        best = jnp.full((8, group), masked_score, f32)
        for block in range(blocks):
            rows = slice(block * lanes, (block + 1) * lanes)
            bias = [bias_ref[half, band_place(block, chip, part), :] for part in range(2)]
            now = score[rows, :] + jnp.concatenate(bias, axis=1) + mask_ref[rows, :]
            score[rows, :] = now
            best = jnp.maximum(best, jnp.max(now.reshape(lanes // 8, 8, group), axis=0))
        top = jnp.max(best, axis=0, keepdims=True)
        total = jnp.zeros((8, group), f32)
        for block in range(blocks):
            rows = slice(block * lanes, (block + 1) * lanes)
            now = jnp.exp(score[rows, :] - top)
            score[rows, :] = now
            total = total + jnp.sum(now.reshape(lanes // 8, 8, group), axis=0)
        inverse = 1.0 / jnp.sum(total, axis=0, keepdims=True)
        for block in range(blocks):
            rows = slice(block * lanes, (block + 1) * lanes)
            now = score[rows, :] * inverse
            p_ref[half, rows, :] = now
            soft[rows, :] = now.astype(bf16)
        features = lanes // 2
        turned.append(mm_tn(value, soft[...])[half * features : (half + 1) * features])
    o_ref[...] = jnp.concatenate(turned, axis=0).T


def attend(plan, pieces, meta, rows, mask, bias):
    length, width = rows.shape
    half = width // 2
    group = 2 * lanes
    pairs = half // lanes
    col = lambda i, *_: (0, i)
    fixed = lambda i, *_: (0, 0)
    flops = 2 * (group * width * half + 2 * length * width * half + 4 * group * length * half)
    return pl.pallas_call(
        functools.partial(attend_kernel, plan),
        grid_spec=pltpu.PrefetchScalarGridSpec(
            num_scalar_prefetch=1,
            grid=(pairs,),
            in_specs=[
                pl.BlockSpec((length, width), fixed),
                pl.BlockSpec((length, group), fixed),
                pl.BlockSpec((2, 5 * lanes, lanes), lambda i, *_: (i, 0, 0)),
            ]
            + [any_spec()] * len(pieces),
            out_specs=[
                pl.BlockSpec((group, lanes), col),
                pl.BlockSpec((length, lanes), col),
                pl.BlockSpec((length, lanes), col),
                pl.BlockSpec((2, length, group), lambda i, *_: (i, 0, 0)),
                pl.BlockSpec((group, lanes), col),
            ],
            scratch_shapes=[
                pltpu.VMEM((3, width, half), bf16),
                pltpu.VMEM((length, group), f32),
                pltpu.VMEM((length, group), bf16),
                dma(len(plan)),
            ],
        ),
        out_shape=[
            shaped(bf16, group, half),
            shaped(bf16, length, half),
            shaped(bf16, length, half),
            shaped(f32, 2 * pairs, length, group),
            shaped(f32, group, half),
        ],
        compiler_params=params(),
        cost_estimate=cost(flops, 30e6, 2 * group * length * pairs),
        name="attend",
    )(meta, rows, mask, bias, *pieces)


def mix_kernel(meta_ref, attended_ref, near_ref, far_ref, part_ref, weight_ref, sem):
    chips, rows, half = near_ref.shape
    rows = rows // 2
    pairs = []
    for index, source in enumerate((near_ref, far_ref)):
        for step in range(chips):
            place = row_block(meta_ref, 1 + index * chips + step, rows)
            for side in range(2):
                pairs.append(
                    (
                        source.at[step, side * rows : (side + 1) * rows, :],
                        weight_ref.at[place, side * half : (side + 1) * half],
                    )
                )
    wait_all(run_copies(pairs, sem))
    core = meta_ref[0]
    mine = weight_ref[pl.ds(pl.multiple_of(core * half, half), half), :]
    part_ref[...] = mm(attended_ref[...].astype(bf16), mine)


def mix(meta, attended, near, far):
    group, half = attended.shape
    width = 2 * half
    return pl.pallas_call(
        mix_kernel,
        in_specs=[smem_spec(), whole_spec(), any_spec(), any_spec()],
        out_specs=[whole_spec()] * 2,
        out_shape=[shaped(f32, group, width), shaped(bf16, width, width)],
        scratch_shapes=[dma(4 * near.shape[0])],
        compiler_params=params(),
        cost_estimate=cost(2 * group * width * half, 4e6),
        name="mix",
    )(meta, attended, near, far)


def feed_kernel(
    gu_plan,
    chips,
    gu_count,
    places,
    meta_ref,
    tokens_ref,
    cot_ref,
    part_ref,
    arrived_ref,
    gain_ref,
    *refs,
):
    refs = list(refs)
    take = lambda n: [refs.pop(0) for _ in range(n)]
    gu_pieces = take(gu_plan[-1][0] + 1)
    (down_full,) = take(1)
    mixed_ref, out_ref, back_ref = take(3)
    gu_outs, down_outs = take(gu_count), take(places)
    gu, down, grad_gu, grad_down, cot_low, normed_low = take(6)
    gu_sem, down_sem, gu_out_sem, down_out_sem = take(4)
    step = pl.program_id(0)
    steps = pl.num_programs(0)
    block = 256

    @pl.when(step == 0)
    def _():
        pairs = []
        for index, lead, target, size, slot in gu_plan:
            place = row_block(meta_ref, slot, gu_pieces[index].shape[1])
            pairs.append(
                (gu_pieces[index].at[lead : lead + size], gu.at[target : target + size, place, :])
            )
        gu_copies = run_copies(pairs, gu_sem)
        pairs = []
        grain = down.shape[0] // chips
        for index in range(chips):
            source = down_full.at[row_block(meta_ref, chips + index, grain), :]
            pairs.append((source, down.at[index * grain : (index + 1) * grain, :]))
        down_copies = run_copies(pairs, down_sem)
        mixed = tokens_ref[...] + part_ref[...] + arrived_ref[...]
        mixed_ref[...] = mixed
        normed_low[...] = (mixed * rms_scale(mixed) * gain_ref[...]).astype(bf16)
        cot_low[...] = cot_ref[...].astype(bf16)
        out_ref[...] = jnp.zeros_like(out_ref)
        back_ref[...] = jnp.zeros_like(back_ref)
        wait_all(gu_copies)
        wait_all(down_copies)

    cols = pl.ds(pl.multiple_of(step * block, block), block)
    normed = normed_low[...]
    cot = cot_low[...]
    gate_w, up_w, down_w = gu[0, :, cols], gu[1, :, cols], down[cols, :]
    gate, up = mm(normed, gate_w), mm(normed, up_w)
    square = gate * gate
    curve = jnp.tanh(gelu_scale * gate * (1.0 + gelu_cubic * square))
    half = 0.5 * (1.0 + curve)
    gelu = gate * half
    slope = half + 0.5 * gate * (1.0 - curve * curve) * gelu_scale * (1.0 + 3.0 * gelu_cubic * square)
    hidden = (gelu * up).astype(bf16)
    dh = mm_nt(cot, down_w)
    dgate = (dh * up * slope).astype(bf16)
    dup = (dh * gelu).astype(bf16)
    out_ref[...] += mm(hidden, down_w)
    back_ref[...] += mm_nt(dgate, gate_w) + mm_nt(dup, up_w)
    grad_down[cols, :] = mm_tn(hidden, cot).astype(bf16)
    grad_gu[0, :, cols] = mm_tn(normed, dgate).astype(bf16)
    grad_gu[1, :, cols] = mm_tn(normed, dup).astype(bf16)

    @pl.when(step == steps - 1)
    def _():
        pairs = []
        for out, (lead, step) in zip(gu_outs, cut_plan(chips, 2)):
            place = row_block(meta_ref, step, out.shape[1])
            pairs.append((grad_gu.at[lead : lead + out.shape[0], place, :], out))
        gu_copies = run_copies(pairs, gu_out_sem)
        pairs = []
        for turn, out in enumerate(down_outs):
            for spot, step in enumerate(bit_reversed(chips)):
                place = row_block(meta_ref, 2 * chips + turn * chips + step, out.shape[1])
                pairs.append((grad_down.at[place, :], out.at[spot]))
        down_copies = run_copies(pairs, down_out_sem)
        wait_all(gu_copies)
        wait_all(down_copies)


def cut_plan(chips, size):
    if chips != 4:
        return [(0, step) for step in range(chips)]
    return [(0, 0), (0, 1), (0, 2), (0, 3), (size // 2, 3)]


def feed(gu_plan, gu_pieces, down_full, meta, tokens, cot, part, arrived, gain, chips, places):
    group, width = tokens.shape
    hidden = gu_pieces[0].shape[2]
    block = 256
    fixed = lambda i, *_: (0, 0)
    full = lambda *shape: pl.BlockSpec(shape, fixed)
    flops = 2 * 9 * group * width * hidden
    plan = cut_plan(chips, 2)
    size = [1 if chips == 4 and step == 3 else 2 for _, step in plan]
    results = pl.pallas_call(
        functools.partial(feed_kernel, gu_plan, chips, len(plan), places),
        grid_spec=pltpu.PrefetchScalarGridSpec(
            num_scalar_prefetch=1,
            grid=(hidden // block,),
            in_specs=[full(group, width)] * 4
            + [full(1, width)]
            + [any_spec()] * (len(gu_pieces) + 1),
            out_specs=[full(group, width)] * 3 + [any_spec()] * (len(plan) + places),
            scratch_shapes=[
                pltpu.VMEM((2, width, hidden), bf16),
                pltpu.VMEM((hidden, width), bf16),
                pltpu.VMEM((2, width, hidden), bf16),
                pltpu.VMEM((hidden, width), bf16),
                pltpu.VMEM((group, width), bf16),
                pltpu.VMEM((group, width), bf16),
                dma(len(gu_plan)),
                dma(chips),
                dma(len(plan)),
                dma(chips * places),
            ],
        ),
        out_shape=[shaped(f32, group, width)] * 3
        + [shaped(bf16, lead, width // chips, hidden) for lead in size]
        + [shaped(bf16, chips, hidden // (chips * places), width)] * places,
        compiler_params=params(),
        cost_estimate=cost(flops, 25e6, group * hidden),
        name="feed",
    )(meta, tokens, cot, part, arrived, gain, *gu_pieces, down_full)
    return results[:3], results[3 : 3 + len(plan)], results[3 + len(plan) :]


def settle_kernel(
    meta_ref,
    mixed_ref,
    cot_ref,
    back_ref,
    arrived_ref,
    attended_ref,
    weight_ref,
    gain_ref,
    dmixed_ref,
    do_ref,
    gain_grad_ref,
    near_ref,
    far_ref,
):
    core = meta_ref[0]
    half = attended_ref.shape[1]
    mixed = mixed_ref[...]
    scale = rms_scale(mixed)
    dn2 = back_ref[...] + arrived_ref[...]
    gained = dn2 * gain_ref[...]
    inner = jnp.mean(gained * mixed, axis=-1, keepdims=True)
    dmixed = cot_ref[...] + scale * gained - mixed * (scale * scale * scale * inner)
    dmixed_ref[...] = dmixed
    gain_grad_ref[...] = 0.5 * jnp.sum(dn2 * mixed * scale, axis=0, keepdims=True)
    branch = dmixed.astype(bf16)
    mine = weight_ref[pl.ds(pl.multiple_of(core * half, half), half), :]
    do_ref[...] = mm_nt(branch, mine).astype(bf16)
    grad = mm_tn(attended_ref[...].astype(bf16), branch).astype(bf16)
    count, rows = near_ref.shape[0], near_ref.shape[1]
    blocks = [grad[i * rows : (i + 1) * rows] for i in range(2 * count)]
    for index in range(count):
        even, odd = blocks[2 * index], blocks[2 * index + 1]
        near_ref[index] = jnp.where(core == 0, even, odd)
        far_ref[index] = jnp.where(core == 0, odd, even)


def settle(meta, mixed, cot, back, arrived, attended, weight, gain, chips):
    group, width = mixed.shape
    half = width // 2
    rows = half // chips
    return pl.pallas_call(
        settle_kernel,
        in_specs=[smem_spec()] + [whole_spec()] * 7,
        out_specs=[whole_spec()] * 5,
        out_shape=[
            shaped(f32, group, width),
            shaped(bf16, group, half),
            shaped(f32, 1, width),
            shaped(bf16, chips // 2, rows, width),
            shaped(bf16, chips // 2, rows, width),
        ],
        compiler_params=params(),
        cost_estimate=cost(4 * group * width * half, 6e6),
        name="settle",
    )(meta, mixed, cot, back, arrived, attended, weight, gain)


def band_rows(band_ref):
    line = lax.broadcasted_iota(jnp.int32, (8, 2 * lanes), 0)
    none = jnp.zeros((8, lanes), f32)
    found = []
    for block in range(3):
        summed = jnp.zeros((8, 2 * lanes), f32)
        for part in range(lanes // 8):
            start = lanes * (block + 1) + 8 * part
            wide = jnp.concatenate([band_ref[start : start + 8, :], none], axis=1)
            move = lanes - 8 - 8 * part
            summed = summed + (pltpu.roll(wide, move, 1) if move else wide)
        for bit in range(3):
            step = 1 << bit
            summed = jnp.where((line & step) == 0, pltpu.roll(summed, step, 1), summed)
        found.append(jnp.sum(summed, axis=0, keepdims=True))
    return jnp.concatenate(found, axis=1)


def retreat_kernel(meta_ref, do_ref, o_ref, q_ref, k_ref, v_ref, p_ref, dq_ref, dkv_ref, bias_ref, low, sums, band_ref, onehot):
    chip = meta_ref[0]
    blocks = k_ref.shape[0] // lanes
    group = 2 * lanes
    features = lanes // 2
    do = do_ref[...]
    spread = (do.astype(f32) * o_ref[...]).T
    band_ref[...] = jnp.zeros_like(band_ref)
    far = jnp.zeros((8, lanes), f32)
    rows_of = []

    @pl.when(pl.program_id(0) == 0)
    def _():
        bucket = lax.broadcasted_iota(jnp.int32, (6 * lanes, lanes), 1)
        spot = lax.broadcasted_iota(jnp.int32, (6 * lanes, lanes), 0)
        offset = lanes * (spot // (2 * lanes)) - 1 - spot % (2 * lanes)
        onehot[...] = (bucket_of(offset) == bucket).astype(f32)

    turned = []
    for half in range(2):
        do_half, query_half = one_head(do, half), one_head(q_ref[...], half)
        delta = jnp.sum(spread[half * features : (half + 1) * features], axis=0, keepdims=True)
        for block in range(blocks):
            rows = slice(block * lanes, (block + 1) * lanes)
            soft = p_ref[half, rows, :]
            ds = soft * (mm_nt(v_ref[rows, :], do_half) - delta)
            for part in range(2):
                place = band_place(block, chip, part)
                band_ref[place, :] += ds[:, part * lanes : (part + 1) * lanes]
            ds_low = ds.astype(bf16)
            low[rows, :] = ds_low
            dk = mm(ds_low, query_half)
            dv = mm(soft.astype(bf16), do_half)
            if half == 0:
                sums[rows, :lanes] = dk
                sums[rows, lanes:] = dv
            else:
                dkv_ref[rows, :lanes] = (sums[rows, :lanes] + dk).astype(bf16)
                dkv_ref[rows, lanes:] = (sums[rows, lanes:] + dv).astype(bf16)
        turned.append(mm_tn(k_ref[...], low[...])[half * features : (half + 1) * features])
        rows_of.append(band_rows(band_ref))
        low_sum = jnp.sum(band_ref[0:lanes, :])
        high_sum = jnp.sum(band_ref[4 * lanes : 5 * lanes, :])
        lane = lax.broadcasted_iota(jnp.int32, (8, lanes), 1)
        line = lax.broadcasted_iota(jnp.int32, (8, lanes), 0)
        far = far + jnp.where((lane == 15) & (line == half), low_sum, 0.0)
        far = far + jnp.where((lane == 31) & (line == half), high_sum, 0.0)
        if half == 0:
            band_ref[...] = jnp.zeros_like(band_ref)
    dq_ref[...] = jnp.concatenate(turned, axis=0).T.astype(bf16)
    rows_of.append(jnp.zeros((6, rows_of[0].shape[1]), f32))
    near = lax.dot_general(
        jnp.concatenate(rows_of, axis=0),
        onehot[...],
        (((1,), (0,)), ((), ())),
        precision=lax.Precision.HIGHEST,
        preferred_element_type=f32,
    )
    bias_ref[0] = near + far


def retreat(meta, do, o, q, k, v, p):
    length, half = k.shape
    group = do.shape[0]
    pairs = half // lanes
    col = lambda i, *_: (0, i)
    deep = lambda i, *_: (i, 0, 0)
    flops = 2 * 8 * group * length * half
    return pl.pallas_call(
        retreat_kernel,
        grid_spec=pltpu.PrefetchScalarGridSpec(
            num_scalar_prefetch=1,
            grid=(pairs,),
            in_specs=[
                pl.BlockSpec((group, lanes), col),
                pl.BlockSpec((group, lanes), col),
                pl.BlockSpec((group, lanes), col),
                pl.BlockSpec((length, lanes), col),
                pl.BlockSpec((length, lanes), col),
                pl.BlockSpec((2, length, group), deep),
            ],
            out_specs=[
                pl.BlockSpec((group, lanes), col),
                pl.BlockSpec((length, 2 * lanes), col),
                pl.BlockSpec((1, 8, lanes), deep),
            ],
            scratch_shapes=[
                pltpu.VMEM((length, group), bf16),
                pltpu.VMEM((length, 2 * lanes), f32),
                pltpu.VMEM((5 * lanes, lanes), f32),
                pltpu.VMEM((6 * lanes, lanes), f32),
            ],
        ),
        out_shape=[
            shaped(bf16, group, half),
            shaped(bf16, length, 2 * half),
            shaped(f32, pairs, 8, lanes),
        ],
        compiler_params=params(),
        cost_estimate=cost(flops, 20e6),
        name="retreat",
    )(meta, do, o, q, k, v, p)


small_rows = 16


def load_plan(plan, pieces, meta_ref, first, weight):
    pairs = []
    for index, lead, target, size, slot in plan:
        size = min(size, 3 - target)
        place = row_block(meta_ref, first + slot, pieces[index].shape[1])
        pairs.append((pieces[index].at[lead : lead + size], weight.at[target : target + size, place, :]))
    return pairs


def grads_kernel(
    plan, count, meta_ref, rows_ref, turned_ref, dq_ref, dkv_ref, gains_ref, second_ref, bias_ref, near_wo, far_wo, *refs
):
    refs = list(refs)
    take = lambda n: [refs.pop(0) for _ in range(n)]
    pieces = take(plan[-1][0] + 1)
    outs = take(count)
    weight, grad, wo, small, sem, out_sem = take(6)
    chip, core = meta_ref[0], meta_ref[1]
    width = rows_ref.shape[1]
    half = width // 2
    group = dq_ref.shape[0]
    chips = wo.shape[0]
    loads = run_copies(load_plan(plan, pieces, meta_ref, 2, weight), sem)
    for index in range(chips // 2):
        wo[core * (chips // 2) + index] = near_wo[index]
        wo[(1 - core) * (chips // 2) + index] = far_wo[index]
    own_rows = pl.ds(pl.multiple_of(chip * group, group), group)
    query_grad = mm_tn(rows_ref[own_rows, :], dq_ref[...])
    grad[0] = query_grad.astype(bf16)
    wait_all(loads)
    along_row = [query_grad[:, at : at + lanes] * weight[0, :, at : at + lanes].astype(f32) for at in range(0, half, lanes)]
    along_row = sum(along_row[1:], along_row[0])
    for pair in range(half // lanes):
        wide = slice(pair * 2 * lanes, (pair + 1) * 2 * lanes)
        cols = slice(pair * lanes, (pair + 1) * lanes)
        summed = mm(turned_ref[...], dkv_ref[:, wide])
        low = summed.astype(bf16)
        grad[1, :, cols] = low[:, :lanes]
        grad[2, :, cols] = low[:, lanes:]
        along_row = along_row + summed[:, :lanes] * weight[1, :, cols].astype(f32)
        along_row = along_row + summed[:, lanes:] * weight[2, :, cols].astype(f32)
    first_gain = jnp.sum(along_row.T, axis=0, keepdims=True) / gains_ref[...]
    second_gain = second_ref[...]
    lines = [first_gain[:, :half], first_gain[:, half:], second_gain[:, :half], second_gain[:, half:]]
    for pair in range(bias_ref.shape[0]):
        both = [bias_ref[pair, 0:1, :], bias_ref[pair, 1:2, :]]
        both.append(jnp.zeros((1, half - 2 * lanes), f32))
        lines.append(jnp.concatenate(both, axis=1))
    lines.append(jnp.zeros((small_rows - len(lines), half), f32))
    small[...] = jnp.concatenate(lines, axis=0).astype(bf16)
    rows = width // chips
    side_rows = rows // 2
    pairs = []
    for out, (matrix, step) in zip(outs, cut_plan(chips, 4)):
        place = row_block(meta_ref, 2 + step, rows)
        last = 2 if chips == 4 and step == 3 and matrix == 0 else 4
        at = 0
        for index in range(matrix, min(last, 3)):
            pairs.append((grad.at[index, place, :], out.at[at : at + rows, :]))
            at += rows
        if last == 4:
            target = meta_ref[2 + step]
            for side in range(2):
                pairs.append(
                    (wo.at[target, :, side * half : (side + 1) * half], out.at[at : at + side_rows, :])
                )
                at += side_rows
            pairs.append((small, out.at[at : at + small_rows, :]))
    wait_all(run_copies(pairs, out_sem))


def weight_grads(plan, pieces, meta, rows, turned, dq, dkv, gain, second, bias, near_wo, far_wo, chips):
    length, width = rows.shape
    half = width // 2
    group = dq.shape[0]
    flops = 2 * (2 * length * width * half + group * width * half)
    block = width // chips
    cuts = cut_plan(chips, 4)
    sizes = []
    for matrix, step in cuts:
        whole = 4 * block + small_rows
        parted = chips == 4 and step == 3
        sizes.append(whole if not parted else 2 * block if matrix == 0 else whole - 2 * block)
    return pl.pallas_call(
        functools.partial(grads_kernel, plan, len(cuts)),
        in_specs=[smem_spec()] + [whole_spec()] * 9 + [any_spec()] * len(pieces),
        out_specs=[any_spec()] * len(cuts),
        out_shape=[shaped(bf16, size, half) for size in sizes],
        scratch_shapes=[
            pltpu.VMEM((3, width, half), bf16),
            pltpu.VMEM((3, width, half), bf16),
            pltpu.VMEM((chips, block // 2, width), bf16),
            pltpu.VMEM((small_rows, half), bf16),
            dma(len(plan)),
            dma(6 * chips + 1),
        ],
        compiler_params=params(),
        cost_estimate=cost(flops, 12e6),
        name="weight_grads",
    )(meta, rows, turned, dq, dkv, gain, second, bias, near_wo, far_wo, *pieces)


def back_kernel(plan, meta_ref, dq_ref, dkv_ref, *refs):
    refs = list(refs)
    take = lambda n: [refs.pop(0) for _ in range(n)]
    pieces = take(plan[-1][0] + 1)
    near_out, far_out = take(2)
    weight, both, back, sem = take(4)
    chip, core = meta_ref[0], meta_ref[1]
    length = dkv_ref.shape[0]
    half = dq_ref.shape[1]
    group = dq_ref.shape[0]
    chips = near_out.shape[0]
    wait_all(run_copies(load_plan(plan, pieces, meta_ref, 2, weight), sem))
    for pair in range(half // lanes):
        wide = pair * 2 * lanes
        cols = slice(pair * lanes, (pair + 1) * lanes)
        both[:, wide : wide + lanes] = weight[1, :, cols]
        both[:, wide + lanes : wide + 2 * lanes] = weight[2, :, cols]
    for start in range(0, length, group):
        back[start : start + group, :] = mm_nt(dkv_ref[start : start + group, :], both[...])
    own_rows = pl.ds(pl.multiple_of(chip * group, group), group)
    back[own_rows, :] += mm_nt(dq_ref[...], weight[0])
    for index, step in enumerate(bit_reversed(chips)):
        for side, out in ((core, near_out), (1 - core, far_out)):
            start = meta_ref[2 + step] * group + side * lanes
            out[index] = back[pl.ds(pl.multiple_of(start, lanes), lanes), :].astype(bf16)


def row_grads(plan, pieces, meta, dq, dkv, chips):
    length, width = dkv.shape
    half = width // 2
    return pl.pallas_call(
        functools.partial(back_kernel, plan),
        in_specs=[smem_spec()] + [whole_spec()] * 2 + [any_spec()] * len(pieces),
        out_specs=[whole_spec()] * 2,
        out_shape=[shaped(bf16, chips, lanes, width)] * 2,
        scratch_shapes=[
            pltpu.VMEM((3, width, half), bf16),
            pltpu.VMEM((width, width), bf16),
            pltpu.VMEM((length, width), f32),
            dma(len(plan)),
        ],
        compiler_params=params(),
        cost_estimate=cost(4 * length * width * half, 8e6),
        name="row_grads",
    )(meta, dq, dkv, *pieces)


def sum_kernel(order_ref, *refs):
    places = order_ref.shape[0]
    sources, outs, total_ref = refs[: -1 - places], refs[-1 - places : -1], refs[-1]
    total_ref[...] = total([source[...] for source in sources])
    height = total_ref.shape[0] - small_rows
    rows = height // (8 * places)
    last = total_ref[height:, :]
    for turn, out in enumerate(outs):
        parts = []
        for block in range(8):
            start = block * places * rows + order_ref[turn] * rows
            parts.append(total_ref[pl.ds(pl.multiple_of(start, 8), rows), :])
        out[...] = jnp.concatenate(parts + [last], axis=0).astype(bf16)


def sum_plane(blocks, order):
    height, half = blocks[0].shape
    places = order.shape[0]
    rows = (height - small_rows) // (8 * places)
    if rows % 8:
        summed = total(blocks).astype(bf16)
        split, last = summed[:-small_rows].reshape(8, places, rows, half), summed[-small_rows:]
        pick = lambda turn: lax.dynamic_index_in_dim(split, order[turn], 1, keepdims=False)
        return [jnp.concatenate([pick(turn).reshape(-1, half), last], axis=0) for turn in range(places)]
    return pl.pallas_call(
        sum_kernel,
        in_specs=[smem_spec()] + [whole_spec()] * len(blocks),
        out_specs=[whole_spec()] * places,
        out_shape=[shaped(bf16, (height - small_rows) // places + small_rows, half)] * places,
        scratch_shapes=[pltpu.VMEM((height, half), f32)],
        compiler_params=params(),
        cost_estimate=cost(1e6, 4e6),
        name="sum_plane",
    )(order, *blocks)


def core_swap(value):
    count = lax.axis_size("seq")
    return lax.ppermute(value, "seq", [(i, i ^ 1) for i in range(count)])


def plane_swap(value, step):
    count = lax.axis_size("seq")
    return lax.ppermute(value, "seq", [(i, i ^ (2 * step)) for i in range(count)])


def along(value, step):
    count = lax.axis_size("batch")
    return lax.ppermute(value, "batch", [(i, (i + step) % count) for i in range(count)])


def along_all(value):
    return [value] + [along(value, step) for step in range(1, lax.axis_size("batch"))]


def after(value, *earlier):
    return lax.optimization_barrier((value,) + earlier)[0]


def join_kernel(order_ref, *refs):
    sources, out = refs[:-1], refs[-1]
    for index, source in enumerate(sources):
        out[:, :, order_ref[index]] = source[...]


def join(blocks, order):
    lead, rest = blocks[0].shape[:2], blocks[0].shape[2:]
    return pl.pallas_call(
        join_kernel,
        in_specs=[smem_spec()] + [whole_spec()] * len(blocks),
        out_specs=whole_spec(),
        out_shape=shaped(bf16, *lead, len(blocks), *rest),
        compiler_params=params(),
        cost_estimate=cost(0, 2e6),
        name="join",
    )(order, *blocks)


def gather_plane(value, later=None):
    chips = lax.axis_size("seq") // 2
    size = value.shape[0]
    if chips != 4:
        pieces = [value] + [plane_swap(value, step) for step in range(1, chips)]
        if later is not None:
            later(pieces)
        return pieces, [(step, 0, 0, size, step) for step in range(chips)], pieces[-1]
    first, second = plane_swap(value, 1), plane_swap(value, 2)
    if later is not None:
        first, second = lax.optimization_barrier((first, second, later((first, second))))[:2]
    passed = first[: size // 2], second[size // 2 :]
    low, high = plane_swap(passed[0], 2), plane_swap(passed[1], 1)
    plan = [(0, 0, 0, size, 0), (1, 0, 0, size, 1), (2, 0, 0, size, 2)]
    plan += [(3, 0, 0, size // 2, 3), (4, 0, size // 2, size - size // 2, 3)]
    return [value, first, second, low, high], plan, passed


def total(blocks):
    summed = blocks[0].astype(f32)
    for block in blocks[1:]:
        summed = summed + block.astype(f32)
    return summed


def scatter_first(blocks):
    if lax.axis_size("seq") != 8:
        return None
    return plane_swap(blocks[3], 1), plane_swap(blocks[4], 2)


def passing_kernel(first_ref, second_ref, low_ref, high_ref, first_out, second_out, held, sem):
    at, low_rows = low_ref.shape[0], pl.ds(0, low_ref.shape[0])
    high_rows = pl.ds(at, high_ref.shape[0])
    spots = [(second_out.at[low_rows], low_ref, held.at[0, low_rows])]
    spots.append((first_out.at[high_rows], high_ref, held.at[1, pl.ds(0, high_ref.shape[0])]))
    loads = run_copies([(place, room) for place, _, room in spots], sem)
    stores = []
    for index, (place, moved, room) in enumerate(spots):
        loads[index].wait()
        room[...] = (room[...].astype(f32) + moved[...].astype(f32)).astype(bf16)
        store = pltpu.make_async_copy(room, place, sem.at[index])
        store.start()
        stores.append(store)
    wait_all(stores)


def scatter_second(blocks, passing):
    if passing is None:
        return blocks[1:]
    low, high = passing
    most = max(low.shape[0], high.shape[0])
    return pl.pallas_call(
        passing_kernel,
        in_specs=[any_spec()] * 2 + [whole_spec()] * 2,
        out_specs=[any_spec()] * 2,
        out_shape=[shaped(bf16, *blocks[1].shape)] * 2,
        scratch_shapes=[pltpu.VMEM((2, most) + low.shape[1:], bf16), dma(2)],
        input_output_aliases={0: 0, 1: 1},
        compiler_params=params(),
        cost_estimate=cost(0, 2e6),
        name="passing",
    )(blocks[1], blocks[2], low, high)


def scatter_sent(parts):
    return [plane_swap(part, step + 1) for step, part in enumerate(parts)]


def bit_reversed(chips):
    order = [0]
    while len(order) < chips:
        order = [2 * step for step in order] + [2 * step + 1 for step in order]
    return order


def halved(blocks, step):
    count = blocks.shape[0] // 2
    return blocks[:count], plane_swap(blocks[count:], step)


def summed_half(halves):
    return total(halves).astype(bf16)


def finished(halves, step):
    while halves[0].shape[0] > 1:
        step *= 2
        halves = halved(summed_half(halves), step)
    return total(halves)[0]


def spread(values):
    return [values[0]] + [along(value, step) for step, value in enumerate(values) if step]


def spread_along(split, dim, place):
    count = lax.axis_size("batch")
    pick = lambda step: lax.dynamic_index_in_dim(split, (place + step) % count, dim, keepdims=False)
    return [pick(0)] + [along(pick(step), step) for step in range(1, count)]


def shards(
    tokens,
    cotangent,
    group_ids,
    attention_weight,
    ffin_weight,
    ffout_weight,
    bias_table,
    gains,
    attention_momentum,
    ffin_momentum,
    ffout_momentum,
    bias_momentum,
    gain_momentum,
    attention_average,
    ffin_average,
    ffout_average,
    bias_average,
    gain_average,
):
    _, tok, width = tokens.shape
    cycle_size, places = lax.axis_size("seq"), lax.axis_size("batch")
    cycle_index = lax.axis_index("seq").astype(jnp.int32)
    place = lax.axis_index("batch").astype(jnp.int32)
    chips = cycle_size // 2
    chip, core = cycle_index // 2, cycle_index % 2
    half = width // 2
    rows = attention_weight.shape[1]
    down_rows = ffout_weight.shape[0]
    hidden = ffin_weight.shape[2]
    grain = hidden // cycle_size
    heads = bias_table.shape[1]
    group = 2 * tok
    first_core = core == 0

    def by_core(mine, theirs):
        return [jnp.where(first_core, mine, theirs), jnp.where(first_core, theirs, mine)]

    steps = [chip ^ step for step in range(chips)]
    order = jnp.stack([(place + places - step) % places for step in range(places)])
    onward = jnp.stack([(place + step) % places for step in range(places)])
    flat_tokens, flat_cot = tokens.reshape(tok, width), cotangent.reshape(tok, width)

    attn_kept, attn_sent, gu_kept, gu_sent, row_block_own, down_own = make_ready(
        core,
        attention_weight,
        ffin_weight,
        ffout_weight,
        flat_tokens,
        group_ids,
        gains,
        chips,
    )
    their_tokens, their_cot = core_swap(flat_tokens), core_swap(flat_cot)
    attn_from, gu_from = core_swap(attn_sent), core_swap(gu_sent)
    row_block_own, attn_kept = lax.optimization_barrier((row_block_own, attn_kept, their_tokens, their_cot))[:2]
    attn_block = fill(core, after(attn_kept, gu_from), attn_from)
    gu_block = fill(core, gu_kept, gu_from)

    attn_blocks = along_all(attn_block)
    near_rows, step = row_block_own[None], 1
    while step < chips:
        arrived = plane_swap(near_rows, step)
        arrived = after(arrived, attn_block if step * 2 < chips else attn_blocks)
        near_rows = jnp.concatenate([near_rows, arrived], axis=0)
        step *= 2
    own_heads = jnp.where(first_core, bias_table[:, : heads // 2], bias_table[:, heads // 2 :])
    bias = bias_rows(after(own_heads, attn_block))
    down_full = lax.all_gather(down_own, ("seq", "batch"), axis=0, tiled=True)

    attn_joined = join(after(attn_blocks, near_rows, bias, gu_block), order).reshape(4, 2 * places * rows, half)
    gu_joined = join(along_all(after(gu_block, attn_joined)), order)
    attn_pieces, attn_plan, attn_first = gather_plane(attn_joined, lambda _: gu_joined)
    near_rows = after(near_rows, attn_first)
    far_rows = core_swap(near_rows)
    gu_joined = after(gu_joined, attn_first).reshape(2, 2 * places * rows, hidden // 2)
    rows_full, turned, mask = place_rows(jnp.stack(steps + [core]), near_rows, far_rows)
    attn_pieces, rows_full = lax.optimization_barrier((attn_pieces, rows_full))
    wo_near = jnp.stack([attn_pieces[i][lead + 3 - target] for i, lead, target, size, _ in attn_plan if target + size == 4])
    wo_far = core_swap(wo_near)
    chip_tokens = jnp.concatenate(by_core(flat_tokens, their_tokens), axis=0)
    chip_cot = jnp.concatenate(by_core(flat_cot, their_cot), axis=0)

    step_meta = jnp.stack(steps)
    query, key, value, soft, attended = attend(
        attn_plan, attn_pieces, step_meta, rows_full, mask, bias
    )
    wo_meta = jnp.stack([core] + [step * 2 + core for step in steps] + [step * 2 + 1 - core for step in steps])
    part, out_weight = mix(wo_meta, attended, wo_near, wo_far)
    their_part = core_swap(part)
    gu_pieces, gu_plan, _ = gather_plane(gu_joined, lambda _: attended)
    down_meta = [2 * step + core for step in range(chips)]
    down_meta += [step * places + onward[index] for index in range(places) for step in steps]
    (mixed, out_part, back_part), gu_grads, down_grads = feed(
        gu_plan,
        gu_pieces,
        down_full,
        jnp.stack(steps + down_meta),
        chip_tokens,
        chip_cot,
        part,
        their_part,
        gains[1:2],
        chips,
        places,
    )
    gu_passing = scatter_first(gu_grads)
    their_back = core_swap(back_part)
    add = lambda a, b: total([a, b]).astype(bf16)
    down_moving = along(down_grads[-1], 1)
    dmixed, attended_grad, second_gain, near_wo, far_wo = settle(
        core.reshape(1), mixed, chip_cot, back_part, their_back, attended, out_weight, gains[1:2], chips
    )
    gu_passing, far_wo, attended_grad, down_moving = lax.optimization_barrier(
        (gu_passing, far_wo, attended_grad, down_moving)
    )
    gu_parts = scatter_second(gu_grads, gu_passing)
    far_wo = core_swap(after(far_wo, gu_passing))
    gu_parts, attended_grad, _ = lax.optimization_barrier((gu_parts, attended_grad, far_wo))
    gu_arrived = scatter_sent(gu_parts)
    down_moving = add(down_moving, down_grads[-2])
    attended_grad, down_moving = lax.optimization_barrier((attended_grad, down_moving))
    down_moving = along(down_moving, 1)
    dq, dkv, bias_part = retreat(chip.reshape(1), attended_grad, attended, query, key, value, soft)
    pair_meta = jnp.stack([chip, core] + steps)
    down_moving = after(down_moving, dq)
    for step in range(places - 3, 0, -1):
        down_moving = add(down_moving, down_grads[step])
        if step == places - 3:
            dq, down_moving = lax.optimization_barrier((dq, down_moving))
        down_moving = along(down_moving, 1)
    attn_grads = weight_grads(
        attn_plan,
        attn_pieces,
        pair_meta,
        rows_full,
        turned,
        dq,
        dkv,
        gains[:1],
        second_gain,
        bias_part,
        near_wo,
        far_wo,
        chips,
    )

    attn_grads, gu_arrived = lax.optimization_barrier((attn_grads, gu_arrived))
    attn_passing = scatter_first(attn_grads)
    gu_sum = total([gu_grads[0]] + list(gu_arrived)).astype(bf16)
    gu_split = gu_sum.reshape(2, 2, places, rows, hidden // 2)
    gu_cut = lambda step: lax.dynamic_index_in_dim(gu_split, (place + step) % places, 2, keepdims=False)
    gu_moving = along(gu_cut(places - 1), 1)
    down_sum = add(after(down_moving, attn_grads), down_grads[0])
    down_halves = halved(down_sum, 1)
    near_back, far_back = row_grads(attn_plan, attn_pieces, pair_meta, after(dq, attn_grads), dkv, chips)
    if attn_passing is not None:
        attn_passing = after(attn_passing, near_back, down_halves)
    attn_parts = scatter_second(attn_grads, attn_passing)
    attn_arrived = scatter_sent(attn_parts)
    back_arrived = core_swap(far_back)
    gu_moving = after(gu_moving, attn_parts)
    for step in range(places - 2, 0, -1):
        gu_moving = along(add(gu_moving, gu_cut(step)), 1)
    gu_sum = total([gu_moving, gu_cut(0)])
    pick = lambda value, first, dim: jnp.where(
        first, lax.index_in_dim(value, 0, dim, False), lax.index_in_dim(value, 1, dim, False)
    )
    gu_own = pick(gu_sum, first_core, 1)
    gu_their = core_swap(pick(gu_sum, core == 1, 1))
    down_sum = summed_half(down_halves)
    down_halves = halved(after(down_sum, attn_parts), 2)
    mine = lambda value: lax.dynamic_slice_in_dim(value, core * tok, tok, 0)
    theirs = lambda value: lax.dynamic_slice_in_dim(value, (1 - core) * tok, tok, 0)
    their_out = core_swap(after(theirs(out_part), near_back))
    attn_cuts = sum_plane([attn_grads[0]] + list(attn_arrived), onward)
    attn_sum = spread(attn_cuts)
    merged = total([near_back, back_arrived]).astype(bf16)
    back_halves = halved(after(merged, attn_cuts), 1)
    own_down = finished(after(down_halves, attn_cuts), 2)
    back_sum = summed_half(back_halves)
    back_halves = halved(back_sum, 2)

    weave = lambda parts: jnp.stack(
        [part.reshape(2, rows, chips, grain) for part in parts], axis=3
    ).reshape(2, rows, hidden)
    own_gu = weave(by_core(gu_own, gu_their))
    all_tokens = places * tok * cycle_size
    inverse_root = 1.0 / math.sqrt(all_tokens)
    ffin_new = update(ffin_weight, own_gu, ffin_momentum, ffin_average, ffin_rate * inverse_root)
    ffout_new = update(
        ffout_weight, own_down, ffout_momentum, ffout_average, ffout_rate * inverse_root
    )
    layer_output = mine(mixed) + mine(out_part) + their_out
    attn_sum, ffin_new, ffout_new, layer_output, _ = lax.optimization_barrier(
        (attn_sum, ffin_new, ffout_new, layer_output, back_sum)
    )
    attn_sum = total(attn_sum)
    first_grad = finished(back_halves, 2)
    blocks = attn_sum[:-small_rows].reshape(4, 2, rows, half)
    small_own = attn_sum[-small_rows:]
    sent = pick(blocks[:3], core == 1, 1).reshape(3 * rows, half)
    arrived = core_swap(jnp.concatenate([sent, small_own], axis=0))
    own_qkv = jnp.concatenate(
        by_core(pick(blocks[:3], first_core, 1), arrived[: 3 * rows].reshape(3, rows, half)), axis=-1
    )
    own_wo = jnp.concatenate([blocks[3, 0], blocks[3, 1]], axis=-1)
    own_attention = jnp.concatenate([own_qkv, own_wo[None]], axis=0)

    scale = rms_scale(flat_tokens)
    gained = first_grad * gains[0]
    inner = jnp.mean(gained * flat_tokens, axis=-1, keepdims=True)
    input_grad = mine(dmixed) + scale * gained - flat_tokens * (scale**3 * inner)

    small_their = arrived[3 * rows :]
    gains_reduced = (small_own[:4] + small_their[:4]).reshape(gains.shape)
    pairs = heads // 4
    heads_of = lambda value: value[4 : 4 + pairs, : 2 * lanes].reshape(heads // 2, lanes)[:, : bias_table.shape[0]]
    bias_reduced = jnp.concatenate(by_core(heads_of(small_own), heads_of(small_their)), axis=0).T

    attention_rate = jnp.array(attention_rates, dtype=f32)[:, None, None] * inverse_root
    gain_rate = jnp.array(gain_rates, dtype=f32)[:, None] * inverse_root
    attn_new = update(
        attention_weight, own_attention, attention_momentum, attention_average, attention_rate
    )
    bias_new = update(bias_table, bias_reduced, bias_momentum, bias_average, bias_rate * inverse_root)
    gain_new = update(gains, gains_reduced, gain_momentum, gain_average, gain_rate)
    return (
        layer_output.reshape(tokens.shape),
        input_grad.reshape(tokens.shape),
        attn_new[0],
        ffin_new[0],
        ffout_new[0],
        bias_new[0],
        gain_new[0],
        attn_new[1],
        ffin_new[1],
        ffout_new[1],
        bias_new[1],
        gain_new[1],
        attn_new[2],
        ffin_new[2],
        ffout_new[2],
        bias_new[2],
        gain_new[2],
        attn_new[0].astype(bf16),
        ffin_new[0].astype(bf16),
        ffout_new[0].astype(bf16),
    )


def solution(mesh):
    rows = P("batch", "seq", None)
    stacked = P(None, ("seq", "batch"), None)
    single = P(("seq", "batch"), None)
    weights = (stacked, stacked, single, P(), P())
    return jax.shard_map(
        shards,
        mesh=mesh,
        in_specs=(rows, rows, P("batch", "seq")) + weights * 3,
        out_specs=(rows, rows) + weights * 3 + (stacked, stacked, single),
        check_vma=False,
    )
```

```python
import functools
import math

import jax
import jax.numpy as jnp
from jax import lax
from jax.experimental import pallas as pl
from jax.experimental.pallas import tpu as pltpu
from jax.sharding import PartitionSpec as P

eps_norm = 1e-06
momentum_coef = 0.5
average_coef = 0.5
attention_rates = (0.0033, 0.0033, 0.025, 0.2)
ffin_rate = 0.063
ffout_rate = 0.023
bias_rate = 0.08
gain_rates = (0.045, 0.22)
thresholds = (12, 16, 23, 32, 46, 64, 91)
masked_score = -1e30
gelu_scale = math.sqrt(2.0 / math.pi)
gelu_cubic = 0.044715
bf16 = jnp.bfloat16
f32 = jnp.float32
vmem_bytes = 60 * 1024 * 1024
lanes = 128


def product(left, right, left_dim, right_dim):
    return lax.dot_general(
        left, right, (((left_dim,), (right_dim,)), ((), ())), preferred_element_type=f32
    )


def mm(left, right):
    return product(left, right, 1, 0)


def mm_nt(left, right):
    return product(left, right, 1, 1)


def mm_tn(left, right):
    return product(left, right, 0, 0)


def bucket_of(offset):
    magnitude = jnp.abs(offset)
    beyond = jnp.zeros_like(offset)
    for threshold in thresholds:
        beyond = beyond + (magnitude >= threshold).astype(jnp.int32)
    inside = jnp.where(magnitude < 8, magnitude, 8 + beyond)
    return inside + 16 * (offset > 0).astype(jnp.int32)


def update(weight, grad, momentum, average, rate):
    new_momentum = momentum_coef * momentum + grad
    new_weight = weight - rate * (grad + momentum_coef * new_momentum)
    new_average = average_coef * average + (1.0 - average_coef) * new_weight
    return (new_weight, new_momentum, new_average)


def rms_scale(values):
    return lax.rsqrt(jnp.mean(values * values, axis=-1, keepdims=True) + eps_norm)


def params():
    return pltpu.CompilerParams(vmem_limit_bytes=vmem_bytes)


def any_spec():
    return pl.BlockSpec(memory_space=pl.ANY)


def cost(flops, nbytes, exps=0):
    return pl.CostEstimate(flops=1, bytes_accessed=1, transcendentals=0)


def bias_kernel(table_ref, out_ref):
    head = pl.program_id(0)
    spot = lax.broadcasted_iota(jnp.int32, (8, 2 * lanes), 1)
    for block in range(3):
        buckets = bucket_of(lanes * (block - 1) + lanes - 1 - spot)
        row = jnp.zeros((8, 2 * lanes), f32)
        for bucket in range(table_ref.shape[0]):
            row = jnp.where(buckets == bucket, table_ref[bucket, head], row)
        wide = jnp.broadcast_to(row[:1], (lanes, 2 * lanes))
        rolled = pltpu.roll(wide, lanes + 1, 1, stride=1, stride_axis=0)
        out_ref[0, lanes * (block + 1) : lanes * (block + 2), :] = rolled[:, :lanes]
    out_ref[0, 0:lanes, :] = jnp.full((lanes, lanes), table_ref[15, head], f32)
    out_ref[0, 4 * lanes : 5 * lanes, :] = jnp.full((lanes, lanes), table_ref[31, head], f32)


def bias_rows(table):
    heads = table.shape[1]
    return pl.pallas_call(
        bias_kernel,
        grid=(heads,),
        in_specs=[pl.BlockSpec(memory_space=pltpu.SMEM)],
        out_specs=pl.BlockSpec((1, 5 * lanes, lanes), lambda i: (i, 0, 0)),
        out_shape=jax.ShapeDtypeStruct((heads, 5 * lanes, lanes), f32),
        compiler_params=params(),
        cost_estimate=cost(heads * 3e6, 4e6),
        name="bias_rows",
    )(table)


def ready_kernel(meta_ref, attn_ref, ffin_ref, ffout_ref, tokens_ref, ids_ref, gain_ref, *outs):
    attn_out, attn_send, gu_out, gu_send, row_out = outs
    core = meta_ref[0]
    first = core == 0
    width = tokens_ref.shape[1]
    half = width // 2
    low = attn_ref[...].astype(bf16)
    left, right = low[..., :half], low[..., half:]
    attn_out[0:3, core] = jnp.where(first, left[:3], right[:3])
    attn_send[...] = jnp.where(first, right[:3], left[:3])
    attn_out[3, 0] = left[3]
    attn_out[3, 1] = right[3]
    grain = ffin_ref.shape[2] // (2 * meta_ref.shape[0])
    for index in range(meta_ref.shape[0]):
        start = 2 * index * grain
        even = ffin_ref[:, :, start : start + grain].astype(bf16)
        odd = ffin_ref[:, :, start + grain : start + 2 * grain].astype(bf16)
        cols = slice(index * grain, (index + 1) * grain)
        gu_out[:, core, :, cols] = jnp.where(first, even, odd)
        gu_send[:, :, cols] = jnp.where(first, odd, even)
    tok = tokens_ref.shape[0]
    tokens = tokens_ref[...]
    row_out[:tok, :] = (tokens * rms_scale(tokens) * gain_ref[0:1, :]).astype(bf16)
    ids = jnp.broadcast_to(ids_ref[...].astype(f32), (16, tok))
    ids = jnp.concatenate([ids, jnp.zeros((16, width - tok), f32)], axis=1)
    row_out[tok : tok + 16, :] = ids.astype(bf16)
    row_out[tok + 16 :, :] = ffout_ref[...].astype(bf16)


def make_ready(core, attention_weight, ffin_weight, ffout_weight, tokens, ids, gain, chips):
    tok, width = tokens.shape
    rows, half, hidden = attention_weight.shape[1], width // 2, ffin_weight.shape[2]
    return pl.pallas_call(
        ready_kernel,
        in_specs=[smem_spec()] + [whole_spec()] * 6,
        out_specs=[whole_spec()] * 5,
        out_shape=[
            shaped(bf16, 4, 2, rows, half),
            shaped(bf16, 3, rows, half),
            shaped(bf16, 2, 2, rows, hidden // 2),
            shaped(bf16, 2, rows, hidden // 2),
            shaped(bf16, tok + 16 + ffout_weight.shape[0], width),
        ],
        compiler_params=params(),
        cost_estimate=cost(1e6, 2e6),
        name="make_ready",
    )(jnp.broadcast_to(core, (chips,)), attention_weight, ffin_weight, ffout_weight, tokens, ids, gain)


def fill_kernel(core_ref, kept_ref, arrived_ref, out_ref):
    count = arrived_ref.shape[0]
    out_ref[...] = kept_ref[...]
    out_ref[0:count, 1 - core_ref[0]] = arrived_ref[...]


def fill(core, kept, arrived):
    return pl.pallas_call(
        fill_kernel,
        in_specs=[smem_spec(), whole_spec(), whole_spec()],
        out_specs=whole_spec(),
        out_shape=shaped(bf16, *kept.shape),
        compiler_params=params(),
        cost_estimate=cost(0, 1e6),
        name="fill",
    )(core.reshape(1), kept, arrived)


def row_block(meta_ref, slot, rows):
    start = meta_ref[slot] * rows
    return pl.ds(pl.multiple_of(start, 16) if rows % 16 == 0 else start, rows)


def run_copies(pairs, sem):
    copies = [pltpu.make_async_copy(a, b, sem.at[i]) for i, (a, b) in enumerate(pairs)]
    for copy in copies:
        copy.start()
    return copies


def wait_all(copies):
    for copy in copies:
        copy.wait()


def whole_spec():
    return pl.BlockSpec(memory_space=pltpu.VMEM)


def smem_spec():
    return pl.BlockSpec(memory_space=pltpu.SMEM)


def dma(count):
    return pltpu.SemaphoreType.DMA((count,))


def shaped(kind, *shape):
    return jax.ShapeDtypeStruct(shape, kind)


def rows_kernel(meta_ref, near_ref, far_ref, full_ref, turned_ref, mask_ref):
    chips = near_ref.shape[0]
    core = meta_ref[chips]
    groups = lambda block: block[lanes : lanes + 16, :lanes].astype(f32)[:1, :]
    mine, other = groups(near_ref[0]), groups(far_ref[0])
    chip_ids = jnp.where(
        core == 0,
        jnp.concatenate([mine, other], axis=1),
        jnp.concatenate([other, mine], axis=1),
    )
    for source, side in ((near_ref, core), (far_ref, 1 - core)):
        for step in range(chips):
            block = source[step]
            start = (meta_ref[step] * 2 + side) * lanes
            place = pl.ds(pl.multiple_of(start, lanes), lanes)
            normed = block[:lanes, :]
            full_ref[place, :] = normed
            turned_ref[:, place] = normed.T
            wide = jnp.broadcast_to(groups(block), (lanes, lanes)).T
            same = jnp.concatenate([wide, wide], axis=1) == chip_ids
            mask_ref[place, :] = jnp.where(same, 0.0, masked_score)


def place_rows(meta, near, far):
    chips, _, width = near.shape
    length = 2 * chips * lanes
    return pl.pallas_call(
        rows_kernel,
        in_specs=[smem_spec()] + [whole_spec()] * 2,
        out_specs=[whole_spec()] * 3,
        out_shape=[
            shaped(bf16, length, width),
            shaped(bf16, width, length),
            shaped(f32, length, 2 * lanes),
        ],
        compiler_params=params(),
        cost_estimate=cost(3e6, 8e6),
        name="place_rows",
    )(meta, near, far)


def one_head(matrix, half):
    first = lax.broadcasted_iota(jnp.int32, matrix.shape, 1) < matrix.shape[1] // 2
    return jnp.where(first if half == 0 else jnp.logical_not(first), matrix, jnp.zeros_like(matrix))


def band_place(block, chip, part):
    kind = jnp.clip(block - (2 * chip + part) + 2, 0, 4)
    return pl.ds(pl.multiple_of(kind * lanes, lanes), lanes)


def attend_kernel(count, meta_ref, rows_ref, mask_ref, bias_ref, *refs):
    pieces = refs[:count]
    q_ref, k_ref, v_ref, p_ref, o_ref, low_ref = refs[count : count + 6]
    weight, score, soft, sem = refs[count + 6 :]
    pair = pl.program_id(0)
    chip = meta_ref[0]
    length = rows_ref.shape[0]
    blocks = length // lanes
    group = 2 * lanes

    @pl.when(pair == 0)
    def _():
        wait_all(run_copies(load_pairs(pieces, meta_ref, 0, weight), sem))

    cols = pl.ds(pl.multiple_of(pair * lanes, lanes), lanes)
    own = rows_ref[pl.ds(pl.multiple_of(chip * group, group), group), :]
    query = mm(own, weight[0, :, cols]).astype(bf16)
    both = jnp.concatenate([weight[1, :, cols], weight[2, :, cols]], axis=1)
    key_value = mm(rows_ref[...], both).astype(bf16)
    key, value = key_value[:, :lanes], key_value[:, lanes:]
    q_ref[...] = query
    k_ref[...] = key
    v_ref[...] = value
    turned = []
    for half in range(2):
        score[...] = mm_nt(key, one_head(query, half))
        best = jnp.full((8, group), masked_score, f32)
        for block in range(blocks):
            rows = slice(block * lanes, (block + 1) * lanes)
            bias = [bias_ref[half, band_place(block, chip, part), :] for part in range(2)]
            now = score[rows, :] + jnp.concatenate(bias, axis=1) + mask_ref[rows, :]
            score[rows, :] = now
            best = jnp.maximum(best, jnp.max(now.reshape(lanes // 8, 8, group), axis=0))
        top = jnp.max(best, axis=0, keepdims=True)
        total = jnp.zeros((8, group), f32)
        for block in range(blocks):
            rows = slice(block * lanes, (block + 1) * lanes)
            now = jnp.exp(score[rows, :] - top)
            score[rows, :] = now
            total = total + jnp.sum(now.reshape(lanes // 8, 8, group), axis=0)
        inverse = 1.0 / jnp.sum(total, axis=0, keepdims=True)
        for block in range(blocks):
            rows = slice(block * lanes, (block + 1) * lanes)
            now = score[rows, :] * inverse
            p_ref[half, rows, :] = now
            soft[rows, :] = now.astype(bf16)
        features = lanes // 2
        turned.append(mm_tn(value, soft[...])[half * features : (half + 1) * features])
    attended = jnp.concatenate(turned, axis=0).T
    o_ref[...] = attended
    low_ref[...] = attended.astype(bf16)


def attend(pieces, meta, rows, mask, bias):
    length, width = rows.shape
    half = width // 2
    group = 2 * lanes
    pairs = half // lanes
    col = lambda i, *_: (0, i)
    fixed = lambda i, *_: (0, 0)
    flops = 2 * (group * width * half + 2 * length * width * half + 4 * group * length * half)
    return pl.pallas_call(
        functools.partial(attend_kernel, len(pieces)),
        grid_spec=pltpu.PrefetchScalarGridSpec(
            num_scalar_prefetch=1,
            grid=(pairs,),
            in_specs=[
                pl.BlockSpec((length, width), fixed),
                pl.BlockSpec((length, group), fixed),
                pl.BlockSpec((2, 5 * lanes, lanes), lambda i, *_: (i, 0, 0)),
            ]
            + [any_spec()] * len(pieces),
            out_specs=[
                pl.BlockSpec((group, lanes), col),
                pl.BlockSpec((length, lanes), col),
                pl.BlockSpec((length, lanes), col),
                pl.BlockSpec((2, length, group), lambda i, *_: (i, 0, 0)),
                pl.BlockSpec((group, lanes), col),
                pl.BlockSpec((group, lanes), col),
            ],
            scratch_shapes=[
                pltpu.VMEM((3, width, half), bf16),
                pltpu.VMEM((length, group), f32),
                pltpu.VMEM((length, group), bf16),
                dma(len(pieces)),
            ],
        ),
        out_shape=[
            shaped(bf16, group, half),
            shaped(bf16, length, half),
            shaped(bf16, length, half),
            shaped(f32, 2 * pairs, length, group),
            shaped(f32, group, half),
            shaped(bf16, group, half),
        ],
        compiler_params=params(),
        cost_estimate=cost(flops, 30e6, 2 * group * length * pairs),
        name="attend",
    )(meta, rows, mask, bias, *pieces)


def mix_kernel(
    meta_ref, tokens_ref, own_ref, their_ref, gain_ref, near_ref, far_ref, mixed_ref, normed_ref, joined_ref, weight_ref, sem
):
    chips, rows, half = near_ref.shape
    rows = rows // 2
    pairs = []
    for index, source in enumerate((near_ref, far_ref)):
        for step in range(chips):
            place = row_block(meta_ref, 1 + index * chips + step, rows)
            for side in range(2):
                pairs.append(
                    (
                        source.at[step, side * rows : (side + 1) * rows, :],
                        weight_ref.at[place, side * half : (side + 1) * half],
                    )
                )
    copies = run_copies(pairs, sem)
    first = meta_ref[0] == 0
    joined_ref[:, :half] = jnp.where(first, own_ref[...], their_ref[...])
    joined_ref[:, half:] = jnp.where(first, their_ref[...], own_ref[...])
    wait_all(copies)
    mixed = tokens_ref[...] + mm(joined_ref[...], weight_ref[...])
    mixed_ref[...] = mixed
    normed_ref[...] = (mixed * rms_scale(mixed) * gain_ref[...]).astype(bf16)


def mix(meta, tokens, own, their, gain, near, far):
    group, half = own.shape
    width = 2 * half
    return pl.pallas_call(
        mix_kernel,
        in_specs=[smem_spec()] + [whole_spec()] * 4 + [any_spec()] * 2,
        out_specs=[whole_spec()] * 4,
        out_shape=[
            shaped(f32, group, width),
            shaped(bf16, group, width),
            shaped(bf16, group, width),
            shaped(bf16, width, width),
        ],
        scratch_shapes=[dma(4 * near.shape[0])],
        compiler_params=params(),
        cost_estimate=cost(4 * group * width * half, 4e6),
        name="mix",
    )(meta, tokens, own, their, gain, near, far)


def feed_kernel(
    chips,
    places,
    gu_count,
    meta_ref,
    normed_low,
    cot_ref,
    *refs,
):
    refs = list(refs)
    take = lambda n: [refs.pop(0) for _ in range(n)]
    gu_pieces = take(gu_count)
    down_pieces = take(places)
    out_ref, back_ref = take(2)
    gu_outs, down_outs = take(chips), take(2)
    gu, down, grad_gu, grad_down, cot_low = take(5)
    gu_sem, down_sem, gu_out_sem, down_out_sem = take(4)
    step = pl.program_id(0)
    steps = pl.num_programs(0)
    block = 256

    count = gu.shape[2] // block

    def gu_loads(turn):
        columns = pl.ds(pl.multiple_of(turn * block, block), block)
        pairs = []
        for index, piece in enumerate(gu_pieces):
            place = row_block(meta_ref, min(index, chips - 1), piece.shape[1])
            lead = slice(0, 2) if piece.shape[0] == 2 else slice(index - 3, index - 2)
            pairs.append((piece.at[:, :, columns], gu.at[lead, place, columns]))
        return [
            pltpu.make_async_copy(a, b, gu_sem.at[turn, index]) for index, (a, b) in enumerate(pairs)
        ]

    def gu_stores(turn):
        columns = pl.ds(pl.multiple_of(turn * block, block), block)
        copies = []
        for chip, out in enumerate(gu_outs):
            source = grad_gu.at[:, row_block(meta_ref, chip, out.shape[1]), columns]
            copies.append(pltpu.make_async_copy(source, out.at[:, :, columns], gu_out_sem.at[turn, chip]))
        return copies

    @pl.when(step == 0)
    def _():
        for copy in gu_loads(0):
            copy.start()
        pairs = []
        slot = chips
        for piece in down_pieces:
            for chip in range(chips):
                pairs.append((piece.at[chip], down.at[row_block(meta_ref, slot, piece.shape[1]), :]))
                slot += 1
        down_copies = run_copies(pairs, down_sem)
        for turn in range(1, count):
            for copy in gu_loads(turn):
                copy.start()
        cot_low[...] = cot_ref[...].astype(bf16)
        out_ref[...] = jnp.zeros_like(out_ref)
        back_ref[...] = jnp.zeros_like(back_ref)
        wait_all(down_copies)

    for copy in gu_loads(step):
        copy.wait()
    cols = pl.ds(pl.multiple_of(step * block, block), block)
    normed = normed_low[...]
    cot = cot_low[...]
    gate_w, up_w, down_w = gu[0, :, cols], gu[1, :, cols], down[cols, :]
    gate, up = mm(normed, gate_w), mm(normed, up_w)
    square = gate * gate
    curve = jnp.tanh(gelu_scale * gate * (1.0 + gelu_cubic * square))
    half = 0.5 * (1.0 + curve)
    gelu = gate * half
    slope = half + 0.5 * gate * (1.0 - curve * curve) * gelu_scale * (1.0 + 3.0 * gelu_cubic * square)
    hidden = (gelu * up).astype(bf16)
    dh = mm_nt(cot, down_w)
    dgate = (dh * up * slope).astype(bf16)
    dup = (dh * gelu).astype(bf16)
    out_ref[...] += mm(hidden, down_w)
    back_ref[...] += mm_nt(dgate, gate_w) + mm_nt(dup, up_w)
    grad_down[cols, :] = mm_tn(hidden, cot).astype(bf16)
    grad_gu[0, :, cols] = mm_tn(normed, dgate).astype(bf16)
    grad_gu[1, :, cols] = mm_tn(normed, dup).astype(bf16)

    for copy in gu_stores(step):
        copy.start()

    @pl.when(step == steps - 1)
    def _():
        pairs = []
        for turn, out in enumerate(down_outs):
            for spot in range(places // 2):
                for chip in range(chips):
                    slot = chips * (1 + places + turn * (places // 2) + spot) + chip
                    place = row_block(meta_ref, slot, out.shape[2])
                    pairs.append((grad_down.at[place, :], out.at[spot, chip]))
        down_copies = run_copies(pairs, down_out_sem)
        for turn in range(count):
            wait_all(gu_stores(turn))
        wait_all(down_copies)


def feed(gu_pieces, down_pieces, meta, normed, cot, chips, places):
    group, width = normed.shape
    hidden = gu_pieces[0].shape[2]
    block = 256
    fixed = lambda i, *_: (0, 0)
    full = lambda *shape: pl.BlockSpec(shape, fixed)
    flops = 2 * 9 * group * width * hidden
    results = pl.pallas_call(
        functools.partial(feed_kernel, chips, places, len(gu_pieces)),
        grid_spec=pltpu.PrefetchScalarGridSpec(
            num_scalar_prefetch=1,
            grid=(hidden // block,),
            in_specs=[full(group, width)] * 2
            + [any_spec()] * (len(gu_pieces) + places),
            out_specs=[full(group, width)] * 2 + [any_spec()] * (chips + 2),
            scratch_shapes=[
                pltpu.VMEM((2, width, hidden), bf16),
                pltpu.VMEM((hidden, width), bf16),
                pltpu.VMEM((2, width, hidden), bf16),
                pltpu.VMEM((hidden, width), bf16),
                pltpu.VMEM((group, width), bf16),
                pltpu.SemaphoreType.DMA((hidden // block, len(gu_pieces))),
                dma(chips * places),
                pltpu.SemaphoreType.DMA((hidden // block, chips)),
                dma(chips * places),
            ],
        ),
        out_shape=[shaped(f32, group, width)] * 2
        + [shaped(bf16, 2, width // chips, hidden)] * chips
        + [shaped(bf16, places // 2, chips, hidden // (chips * places), width)] * 2,
        compiler_params=params(),
        cost_estimate=cost(flops, 25e6, group * hidden),
        name="feed",
    )(meta, normed, cot, *gu_pieces, *down_pieces)
    return results[:2], results[2 : 2 + chips], results[2 + chips :]


def settle_kernel(
    meta_ref,
    mixed_ref,
    cot_ref,
    back_ref,
    arrived_ref,
    weight_ref,
    gain_ref,
    dmixed_ref,
    do_ref,
    gain_grad_ref,
    branch_ref,
):
    core = meta_ref[0]
    half = do_ref.shape[1]
    mixed = mixed_ref[...]
    scale = rms_scale(mixed)
    dn2 = back_ref[...] + arrived_ref[...]
    gained = dn2 * gain_ref[...]
    inner = jnp.mean(gained * mixed, axis=-1, keepdims=True)
    dmixed = cot_ref[...] + scale * gained - mixed * (scale * scale * scale * inner)
    dmixed_ref[...] = dmixed
    gain_grad_ref[...] = 0.5 * jnp.sum(dn2 * mixed * scale, axis=0, keepdims=True)
    branch = dmixed.astype(bf16)
    branch_ref[...] = branch
    mine = weight_ref[pl.ds(pl.multiple_of(core * half, half), half), :]
    do_ref[...] = mm_nt(branch, mine).astype(bf16)


def settle(meta, mixed, cot, back, arrived, weight, gain):
    group, width = mixed.shape
    half = width // 2
    return pl.pallas_call(
        settle_kernel,
        in_specs=[smem_spec()] + [whole_spec()] * 6,
        out_specs=[whole_spec()] * 4,
        out_shape=[
            shaped(f32, group, width),
            shaped(bf16, group, half),
            shaped(f32, 1, width),
            shaped(bf16, group, width),
        ],
        compiler_params=params(),
        cost_estimate=cost(2 * group * width * half, 6e6),
        name="settle",
    )(meta, mixed, cot, back, arrived, weight, gain)


def band_rows(band_ref):
    line = lax.broadcasted_iota(jnp.int32, (8, 2 * lanes), 0)
    none = jnp.zeros((8, lanes), f32)
    found = []
    for block in range(3):
        summed = jnp.zeros((8, 2 * lanes), f32)
        for part in range(lanes // 8):
            start = lanes * (block + 1) + 8 * part
            wide = jnp.concatenate([band_ref[start : start + 8, :], none], axis=1)
            move = lanes - 8 - 8 * part
            summed = summed + (pltpu.roll(wide, move, 1) if move else wide)
        for bit in range(3):
            step = 1 << bit
            summed = jnp.where((line & step) == 0, pltpu.roll(summed, step, 1), summed)
        found.append(jnp.sum(summed, axis=0, keepdims=True))
    return jnp.concatenate(found, axis=1)


def retreat_kernel(meta_ref, do_ref, o_ref, q_ref, k_ref, v_ref, p_ref, dq_ref, dkv_ref, bias_ref, low, sums, band_ref, onehot):
    chip = meta_ref[0]
    blocks = k_ref.shape[0] // lanes
    group = 2 * lanes
    features = lanes // 2
    do = do_ref[...]
    spread = (do.astype(f32) * o_ref[...]).T
    band_ref[...] = jnp.zeros_like(band_ref)
    far = jnp.zeros((8, lanes), f32)
    rows_of = []

    @pl.when(pl.program_id(0) == 0)
    def _():
        bucket = lax.broadcasted_iota(jnp.int32, (6 * lanes, lanes), 1)
        spot = lax.broadcasted_iota(jnp.int32, (6 * lanes, lanes), 0)
        offset = lanes * (spot // (2 * lanes)) - 1 - spot % (2 * lanes)
        onehot[...] = (bucket_of(offset) == bucket).astype(f32)

    turned = []
    for half in range(2):
        do_half, query_half = one_head(do, half), one_head(q_ref[...], half)
        delta = jnp.sum(spread[half * features : (half + 1) * features], axis=0, keepdims=True)
        for block in range(blocks):
            rows = slice(block * lanes, (block + 1) * lanes)
            soft = p_ref[half, rows, :]
            ds = soft * (mm_nt(v_ref[rows, :], do_half) - delta)
            for part in range(2):
                place = band_place(block, chip, part)
                band_ref[place, :] += ds[:, part * lanes : (part + 1) * lanes]
            ds_low = ds.astype(bf16)
            low[rows, :] = ds_low
            dk = mm(ds_low, query_half)
            dv = mm(soft.astype(bf16), do_half)
            if half == 0:
                sums[rows, :lanes] = dk
                sums[rows, lanes:] = dv
            else:
                dkv_ref[rows, :lanes] = (sums[rows, :lanes] + dk).astype(bf16)
                dkv_ref[rows, lanes:] = (sums[rows, lanes:] + dv).astype(bf16)
        turned.append(mm_tn(k_ref[...], low[...])[half * features : (half + 1) * features])
        rows_of.append(band_rows(band_ref))
        low_sum = jnp.sum(band_ref[0:lanes, :])
        high_sum = jnp.sum(band_ref[4 * lanes : 5 * lanes, :])
        lane = lax.broadcasted_iota(jnp.int32, (8, lanes), 1)
        line = lax.broadcasted_iota(jnp.int32, (8, lanes), 0)
        far = far + jnp.where((lane == 15) & (line == half), low_sum, 0.0)
        far = far + jnp.where((lane == 31) & (line == half), high_sum, 0.0)
        if half == 0:
            band_ref[...] = jnp.zeros_like(band_ref)
    dq_ref[...] = jnp.concatenate(turned, axis=0).T.astype(bf16)
    rows_of.append(jnp.zeros((6, rows_of[0].shape[1]), f32))
    near = lax.dot_general(
        jnp.concatenate(rows_of, axis=0),
        onehot[...],
        (((1,), (0,)), ((), ())),
        precision=lax.Precision.HIGHEST,
        preferred_element_type=f32,
    )
    bias_ref[0] = near + far


def retreat(meta, do, o, q, k, v, p):
    length, half = k.shape
    group = do.shape[0]
    pairs = half // lanes
    col = lambda i, *_: (0, i)
    deep = lambda i, *_: (i, 0, 0)
    flops = 2 * 8 * group * length * half
    return pl.pallas_call(
        retreat_kernel,
        grid_spec=pltpu.PrefetchScalarGridSpec(
            num_scalar_prefetch=1,
            grid=(pairs,),
            in_specs=[
                pl.BlockSpec((group, lanes), col),
                pl.BlockSpec((group, lanes), col),
                pl.BlockSpec((group, lanes), col),
                pl.BlockSpec((length, lanes), col),
                pl.BlockSpec((length, lanes), col),
                pl.BlockSpec((2, length, group), deep),
            ],
            out_specs=[
                pl.BlockSpec((group, lanes), col),
                pl.BlockSpec((length, 2 * lanes), col),
                pl.BlockSpec((1, 8, lanes), deep),
            ],
            scratch_shapes=[
                pltpu.VMEM((length, group), bf16),
                pltpu.VMEM((length, 2 * lanes), f32),
                pltpu.VMEM((5 * lanes, lanes), f32),
                pltpu.VMEM((6 * lanes, lanes), f32),
            ],
        ),
        out_shape=[
            shaped(bf16, group, half),
            shaped(bf16, length, 2 * half),
            shaped(f32, pairs, 8, lanes),
        ],
        compiler_params=params(),
        cost_estimate=cost(flops, 20e6),
        name="retreat",
    )(meta, do, o, q, k, v, p)


small_rows = 16


def load_pairs(pieces, meta_ref, first, weight):
    pairs = []
    for step, piece in enumerate(pieces):
        place = row_block(meta_ref, first + step, piece.shape[1])
        pairs.append((piece.at[0:3], weight.at[:, place, :]))
    return pairs


def grads_kernel(
    chips, meta_ref, rows_ref, turned_ref, dq_ref, dkv_ref, gains_ref, second_ref, bias_ref, joined_ref, branch_ref, *refs
):
    refs = list(refs)
    take = lambda n: [refs.pop(0) for _ in range(n)]
    pieces, outs = take(chips), take(chips)
    weight, grad, wo, small, sem, out_sem = take(6)
    chip, core = meta_ref[0], meta_ref[1]
    width = rows_ref.shape[1]
    half = width // 2
    group = dq_ref.shape[0]
    loads = run_copies(load_pairs(pieces, meta_ref, 2, weight), sem)
    out_grad = mm_tn(joined_ref[...], branch_ref[...]).astype(bf16)
    wo_rows = wo.shape[1]
    for index in range(chips):
        even = out_grad[2 * index * wo_rows : (2 * index + 1) * wo_rows]
        odd = out_grad[(2 * index + 1) * wo_rows : (2 * index + 2) * wo_rows]
        wo[index] = jnp.where(core == 0, even, odd)
    own_rows = pl.ds(pl.multiple_of(chip * group, group), group)
    query_grad = mm_tn(rows_ref[own_rows, :], dq_ref[...])
    grad[0] = query_grad.astype(bf16)
    wait_all(loads)
    along_row = [query_grad[:, at : at + lanes] * weight[0, :, at : at + lanes].astype(f32) for at in range(0, half, lanes)]
    along_row = sum(along_row[1:], along_row[0])
    for pair in range(half // lanes):
        wide = slice(pair * 2 * lanes, (pair + 1) * 2 * lanes)
        cols = slice(pair * lanes, (pair + 1) * lanes)
        summed = mm(turned_ref[...], dkv_ref[:, wide])
        low = summed.astype(bf16)
        grad[1, :, cols] = low[:, :lanes]
        grad[2, :, cols] = low[:, lanes:]
        along_row = along_row + summed[:, :lanes] * weight[1, :, cols].astype(f32)
        along_row = along_row + summed[:, lanes:] * weight[2, :, cols].astype(f32)
    first_gain = jnp.sum(along_row.T, axis=0, keepdims=True) / gains_ref[...]
    second_gain = second_ref[...]
    lines = [first_gain[:, :half], first_gain[:, half:], second_gain[:, :half], second_gain[:, half:]]
    for pair in range(bias_ref.shape[0]):
        both = [bias_ref[pair, 0:1, :], bias_ref[pair, 1:2, :]]
        both.append(jnp.zeros((1, half - 2 * lanes), f32))
        lines.append(jnp.concatenate(both, axis=1))
    lines.append(jnp.zeros((small_rows - len(lines), half), f32))
    small[...] = jnp.concatenate(lines, axis=0).astype(bf16)
    rows = width // chips
    side_rows = rows // 2
    pairs = []
    for step, out in enumerate(outs):
        place = row_block(meta_ref, 2 + step, rows)
        at = 0
        for matrix in range(3):
            pairs.append((grad.at[matrix, place, :], out.at[at : at + rows, :]))
            at += rows
        for side in range(2):
            source = wo.at[meta_ref[2 + step], :, side * half : (side + 1) * half]
            pairs.append((source, out.at[at : at + side_rows, :]))
            at += side_rows
        pairs.append((small, out.at[at : at + small_rows, :]))
    wait_all(run_copies(pairs, out_sem))


def weight_grads(pieces, meta, rows, turned, dq, dkv, gain, second, bias, joined, branch, chips):
    length, width = rows.shape
    half = width // 2
    group = dq.shape[0]
    flops = 2 * (2 * length * width * half + group * width * half)
    block = width // chips
    return pl.pallas_call(
        functools.partial(grads_kernel, chips),
        in_specs=[smem_spec()] + [whole_spec()] * 9 + [any_spec()] * len(pieces),
        out_specs=[any_spec()] * chips,
        out_shape=[shaped(bf16, 4 * block + small_rows, half)] * chips,
        scratch_shapes=[
            pltpu.VMEM((3, width, half), bf16),
            pltpu.VMEM((3, width, half), bf16),
            pltpu.VMEM((chips, block // 2, width), bf16),
            pltpu.VMEM((small_rows, half), bf16),
            dma(chips),
            dma(6 * chips),
        ],
        compiler_params=params(),
        cost_estimate=cost(flops, 12e6),
        name="weight_grads",
    )(meta, rows, turned, dq, dkv, gain, second, bias, joined, branch, *pieces)


def back_kernel(chips, meta_ref, dq_ref, dkv_ref, *refs):
    refs = list(refs)
    take = lambda n: [refs.pop(0) for _ in range(n)]
    pieces = take(chips)
    near_out, far_out = take(2)
    weight, both, back, sem = take(4)
    chip, core = meta_ref[0], meta_ref[1]
    length = dkv_ref.shape[0]
    half = dq_ref.shape[1]
    group = dq_ref.shape[0]
    wait_all(run_copies(load_pairs(pieces, meta_ref, 2, weight), sem))
    for pair in range(half // lanes):
        wide = pair * 2 * lanes
        cols = slice(pair * lanes, (pair + 1) * lanes)
        both[:, wide : wide + lanes] = weight[1, :, cols]
        both[:, wide + lanes : wide + 2 * lanes] = weight[2, :, cols]
    for start in range(0, length, group):
        back[start : start + group, :] = mm_nt(dkv_ref[start : start + group, :], both[...])
    own_rows = pl.ds(pl.multiple_of(chip * group, group), group)
    back[own_rows, :] += mm_nt(dq_ref[...], weight[0])
    for index, step in enumerate(bit_reversed(chips)):
        for side, out in ((core, near_out), (1 - core, far_out)):
            start = meta_ref[2 + step] * group + side * lanes
            out[index] = back[pl.ds(pl.multiple_of(start, lanes), lanes), :].astype(bf16)


def row_grads(pieces, meta, dq, dkv, chips):
    length, width = dkv.shape
    half = width // 2
    return pl.pallas_call(
        functools.partial(back_kernel, chips),
        in_specs=[smem_spec()] + [whole_spec()] * 2 + [any_spec()] * len(pieces),
        out_specs=[whole_spec()] * 2,
        out_shape=[shaped(bf16, chips, lanes, width)] * 2,
        scratch_shapes=[
            pltpu.VMEM((3, width, half), bf16),
            pltpu.VMEM((width, width), bf16),
            pltpu.VMEM((length, width), f32),
            dma(chips),
        ],
        compiler_params=params(),
        cost_estimate=cost(4 * length * width * half, 8e6),
        name="row_grads",
    )(meta, dq, dkv, *pieces)


def sum_kernel(order_ref, *refs):
    places = order_ref.shape[0]
    sources, outs, total_ref = refs[: -1 - places], refs[-1 - places : -1], refs[-1]
    total_ref[...] = total([source[...] for source in sources])
    height = total_ref.shape[0] - small_rows
    rows = height // (8 * places)
    last = total_ref[height:, :]
    for turn, out in enumerate(outs):
        parts = []
        for block in range(8):
            start = block * places * rows + order_ref[turn] * rows
            parts.append(total_ref[pl.ds(pl.multiple_of(start, 8), rows), :])
        out[...] = jnp.concatenate(parts + [last], axis=0).astype(bf16)


def sum_plane(blocks, order):
    height, half = blocks[0].shape
    places = order.shape[0]
    rows = (height - small_rows) // (8 * places)
    if rows % 8:
        summed = total(blocks).astype(bf16)
        split, last = summed[:-small_rows].reshape(8, places, rows, half), summed[-small_rows:]
        pick = lambda turn: lax.dynamic_index_in_dim(split, order[turn], 1, keepdims=False)
        return [jnp.concatenate([pick(turn).reshape(-1, half), last], axis=0) for turn in range(places)]
    return pl.pallas_call(
        sum_kernel,
        in_specs=[smem_spec()] + [whole_spec()] * len(blocks),
        out_specs=[whole_spec()] * places,
        out_shape=[shaped(bf16, (height - small_rows) // places + small_rows, half)] * places,
        scratch_shapes=[pltpu.VMEM((height, half), f32)],
        compiler_params=params(),
        cost_estimate=cost(1e6, 4e6),
        name="sum_plane",
    )(order, *blocks)


def last_kernel(core_ref, *refs):
    sources, (sum_ref, sent_ref) = refs[:-2], refs[-2:]
    summed = total([source[...] for source in sources])
    sum_ref[...] = summed
    rows = (summed.shape[0] - small_rows) // 8
    first = core_ref[0] == 0
    block = lambda index: summed[index * rows : (index + 1) * rows]
    parts = [jnp.where(first, block(2 * matrix + 1), block(2 * matrix)) for matrix in range(3)]
    sent_ref[...] = jnp.concatenate(parts + [summed[8 * rows :]], axis=0)


def last_sum(core, arrived):
    height, half = arrived[0].shape
    rows = (height - small_rows) // 8
    return pl.pallas_call(
        last_kernel,
        in_specs=[smem_spec()] + [whole_spec()] * len(arrived),
        out_specs=[whole_spec()] * 2,
        out_shape=[shaped(f32, height, half), shaped(f32, 3 * rows + small_rows, half)],
        compiler_params=params(),
        cost_estimate=cost(1e6, 1e6),
        name="last_sum",
    )(core.reshape(1), *arrived)


def attention_kernel(
    rates, core_ref, sum_ref, arrived_ref, weight_ref, momentum_ref, average_ref, *outs
):
    new_weight, new_momentum, new_average, copy = outs
    rows, width = weight_ref.shape[1:]
    half = width // 2
    first = core_ref[0] == 0
    block = lambda index: sum_ref[index * rows : (index + 1) * rows, :]
    for matrix in range(4):
        left, right = block(2 * matrix), block(2 * matrix + 1)
        if matrix < 3:
            mine = jnp.where(first, left, right)
            theirs = arrived_ref[matrix * rows : (matrix + 1) * rows, :]
            left, right = jnp.where(first, mine, theirs), jnp.where(first, theirs, mine)
        for side, grad in enumerate((left, right)):
            at = (matrix, slice(None), slice(side * half, (side + 1) * half))
            values = update(
                weight_ref[at], grad, momentum_ref[at], average_ref[at], rates[matrix]
            )
            new_weight[at], new_momentum[at], new_average[at] = values
            copy[at] = values[0].astype(bf16)


def attention_update(core, summed, arrived, weight, momentum, average, rates):
    return pl.pallas_call(
        functools.partial(attention_kernel, rates),
        in_specs=[smem_spec()] + [whole_spec()] * 5,
        out_specs=[whole_spec()] * 4,
        out_shape=[shaped(f32, *weight.shape)] * 3 + [shaped(bf16, *weight.shape)],
        compiler_params=params(),
        cost_estimate=cost(1e6, 2e6),
        name="attention_update",
    )(core.reshape(1), summed, arrived, weight, momentum, average)


def core_swap(value):
    count = lax.axis_size("seq")
    return lax.ppermute(value, "seq", [(i, i ^ 1) for i in range(count)])


def plane_swap(value, step):
    count = lax.axis_size("seq")
    return lax.ppermute(value, "seq", [(i, i ^ (2 * step)) for i in range(count)])


def along(value, step):
    count = lax.axis_size("batch")
    return lax.ppermute(value, "batch", [(i, (i + step) % count) for i in range(count)])


def along_all(value):
    return [value] + [along(value, step) for step in range(1, lax.axis_size("batch"))]


def after(value, *earlier):
    return lax.optimization_barrier((value,) + earlier)[0]


def join_kernel(order_ref, *refs):
    sources, out = refs[:-1], refs[-1]
    for index, source in enumerate(sources):
        out[:, :, order_ref[index]] = source[...]


def join(blocks, order):
    lead, rest = blocks[0].shape[:2], blocks[0].shape[2:]
    return pl.pallas_call(
        join_kernel,
        in_specs=[smem_spec()] + [whole_spec()] * len(blocks),
        out_specs=whole_spec(),
        out_shape=shaped(bf16, *lead, len(blocks), *rest),
        compiler_params=params(),
        cost_estimate=cost(0, 2e6),
        name="join",
    )(order, *blocks)


def gather_plane(value):
    return [value] + [plane_swap(value, step) for step in range(1, lax.axis_size("seq") // 2)]


def total(blocks):
    summed = blocks[0].astype(f32)
    for block in blocks[1:]:
        summed = summed + block.astype(f32)
    return summed


def scatter_plane(blocks):
    return [blocks[0]] + [plane_swap(part, step) for step, part in enumerate(blocks) if step]


def bit_reversed(chips):
    order = [0]
    while len(order) < chips:
        order = [2 * step for step in order] + [2 * step + 1 for step in order]
    return order


def halves_along(value, dim, place):
    count = value.shape[dim] // 2
    split = value.reshape(value.shape[:dim] + (2, count) + value.shape[dim + 1 :])
    side = (place // count) % 2
    pick = lambda index: lax.dynamic_index_in_dim(split, index, dim, keepdims=False)
    return pick(side), pick(1 - side)


def across(value, step):
    count = lax.axis_size("batch")
    return lax.ppermute(value, "batch", [(i, i ^ step) for i in range(count)])


def halved(blocks, step):
    count = blocks.shape[0] // 2
    return blocks[:count], plane_swap(blocks[count:], step)


def summed_half(halves):
    return total(halves).astype(bf16)


def finished(halves, steps):
    for step in steps:
        halves = halved(summed_half(halves), step)
    return total(halves)[0]


def spread(values):
    return [values[0]] + [along(value, step) for step, value in enumerate(values) if step]


def spread_along(split, dim, place):
    count = lax.axis_size("batch")
    pick = lambda step: lax.dynamic_index_in_dim(split, (place + step) % count, dim, keepdims=False)
    return [pick(0)] + [along(pick(step), step) for step in range(1, count)]


def shards(
    tokens,
    cotangent,
    group_ids,
    attention_weight,
    ffin_weight,
    ffout_weight,
    bias_table,
    gains,
    attention_momentum,
    ffin_momentum,
    ffout_momentum,
    bias_momentum,
    gain_momentum,
    attention_average,
    ffin_average,
    ffout_average,
    bias_average,
    gain_average,
):
    _, tok, width = tokens.shape
    cycle_size, places = lax.axis_size("seq"), lax.axis_size("batch")
    cycle_index = lax.axis_index("seq").astype(jnp.int32)
    place = lax.axis_index("batch").astype(jnp.int32)
    chips = cycle_size // 2
    chip, core = cycle_index // 2, cycle_index % 2
    half = width // 2
    rows = attention_weight.shape[1]
    down_rows = ffout_weight.shape[0]
    hidden = ffin_weight.shape[2]
    grain = hidden // cycle_size
    heads = bias_table.shape[1]
    group = 2 * tok
    first_core = core == 0

    def by_core(mine, theirs):
        return [jnp.where(first_core, mine, theirs), jnp.where(first_core, theirs, mine)]

    steps = [chip ^ step for step in range(chips)]
    order = jnp.stack([(place + places - step) % places for step in range(places)])
    onward = jnp.stack([(place + step) % places for step in range(places)])
    flat_tokens, flat_cot = tokens.reshape(tok, width), cotangent.reshape(tok, width)

    attn_kept, attn_sent, gu_kept, gu_sent, row_block_own = make_ready(
        core,
        attention_weight,
        ffin_weight,
        ffout_weight,
        flat_tokens,
        group_ids,
        gains,
        chips,
    )
    their_tokens, their_cot = core_swap(flat_tokens), core_swap(flat_cot)
    attn_from, gu_from = core_swap(attn_sent), core_swap(gu_sent)
    row_block_own, attn_kept = lax.optimization_barrier((row_block_own, attn_kept, their_tokens, their_cot))[:2]
    attn_block = fill(core, after(attn_kept, gu_from), attn_from)
    gu_block = fill(core, gu_kept, gu_from)

    attn_blocks = along_all(attn_block)
    row_blocks, step = row_block_own[None], 1
    while step < chips:
        arrived = plane_swap(row_blocks, step)
        arrived = after(arrived, attn_block if step * 2 < chips else attn_blocks)
        row_blocks = jnp.concatenate([row_blocks, arrived], axis=0)
        step *= 2
    near_rows, down_block = row_blocks[:, : tok + 16], row_blocks[:, tok + 16 :]
    own_heads = jnp.where(first_core, bias_table[:, : heads // 2], bias_table[:, heads // 2 :])
    bias = bias_rows(after(own_heads, attn_block))

    attn_joined = join(after(attn_blocks, near_rows, bias, gu_block), order).reshape(4, 2 * places * rows, half)
    far_rows = core_swap(after(near_rows, attn_joined))
    rows_full, turned, mask = place_rows(jnp.stack(steps + [core]), near_rows, far_rows)
    attn_pieces = gather_plane(attn_joined)
    gu_blocks = [after(gu_block, attn_joined)]
    for step in range(1, places):
        if step == 2:
            gu_blocks[-1], down_block = lax.optimization_barrier((gu_blocks[-1], down_block, rows_full))[:2]
        gu_blocks.append(along(gu_blocks[-1], 1))
    down_pieces = [down_block, along(down_block, 1)]
    gu_joined = join(gu_blocks, order)
    attn_pieces, rows_full, gu_joined, down_pieces = lax.optimization_barrier(
        (attn_pieces, rows_full, gu_joined, down_pieces)
    )
    wo_near = jnp.stack([piece[3] for piece in attn_pieces])
    wo_far = core_swap(wo_near)
    gu_joined, down_pieces, mask = lax.optimization_barrier((gu_joined, down_pieces, mask, wo_far))[:3]
    down_pieces.append(along(down_pieces[-1], 1))
    gu_own = gu_joined.reshape(2, 2 * places * rows, hidden // 2)
    gu_pieces = [gu_own] + [plane_swap(gu_own, step) for step in range(1, 3 if chips == 4 else chips)]
    chip_tokens = jnp.concatenate(by_core(flat_tokens, their_tokens), axis=0)
    chip_cot = jnp.concatenate(by_core(flat_cot, their_cot), axis=0)

    step_meta = jnp.stack(steps)
    query, key, value, soft, attended, attended_low = attend(
        attn_pieces, step_meta, rows_full, mask, bias
    )
    wo_meta = jnp.stack([core] + [step * 2 + core for step in steps] + [step * 2 + 1 - core for step in steps])
    their_attended = core_swap(attended_low)
    their_attended, gu_pieces, down_pieces = lax.optimization_barrier((their_attended, gu_pieces, down_pieces))
    if chips == 4:
        passed = [gu_pieces[1][:1], gu_pieces[2][1:]]
        their_attended, passed = lax.optimization_barrier((their_attended, passed))
        gu_pieces += [plane_swap(passed[0], 2), plane_swap(passed[1], 1)]
    for _ in range(3, places):
        down_pieces.append(along(down_pieces[-1], 1))
    mixed, second_low, joined, out_weight = mix(
        wo_meta, chip_tokens, attended_low, their_attended, gains[1:2], wo_near, wo_far
    )
    down_meta = [step * places + order[index] for index in range(places) for step in steps]
    high = place // (places // 2)
    for side in (high, 1 - high):
        for spot in range(places // 2):
            down_meta += [step * places + side * (places // 2) + spot for step in steps]
    (out_part, back_part), gu_grads, down_grads = feed(
        gu_pieces, down_pieces, jnp.stack(steps + down_meta), second_low, chip_cot, chips, places
    )
    add = lambda a, b: total([a, b]).astype(bf16)
    gu_arrived = scatter_plane(gu_grads)
    down_moving = across(down_grads[1], places // 2)
    their_back = core_swap(back_part)
    dmixed, attended_grad, second_gain, branch = settle(
        core.reshape(1), mixed, chip_cot, back_part, their_back, out_weight, gains[1:2]
    )
    dq, dkv, bias_part = retreat(chip.reshape(1), attended_grad, attended, query, key, value, soft)
    pair_meta = jnp.stack([chip, core] + steps)
    attn_grads = weight_grads(
        attn_pieces,
        pair_meta,
        rows_full,
        turned,
        dq,
        dkv,
        gains[:1],
        second_gain,
        bias_part,
        joined,
        branch,
        chips,
    )

    near_back, far_back = row_grads(attn_pieces, pair_meta, after(dq, attn_grads), dkv, chips)
    mine = lambda value: lax.dynamic_slice_in_dim(value, core * tok, tok, 0)
    theirs = lambda value: lax.dynamic_slice_in_dim(value, (1 - core) * tok, tok, 0)
    back_arrived = core_swap(far_back)
    attn_grads, gu_arrived, down_moving = lax.optimization_barrier(
        (attn_grads, gu_arrived, down_moving, back_arrived)
    )[:3]
    attn_arrived = [attn_grads[0]] + [plane_swap(attn_grads[step], step) for step in range(1, min(chips, 3))]
    gu_sum = total(gu_arrived).astype(bf16).reshape(2, 2, places, rows, hidden // 2)
    down_sum = add(down_moving, down_grads[0])
    reach = places // 2
    gu_kept, gu_sent = halves_along(gu_sum, 2, place)
    gu_moving = across(gu_sent, reach)
    down_kept, down_sent = halves_along(down_sum, 0, place)
    down_moving = across(down_sent, reach // 2)
    attn_arrived, gu_moving, down_moving, out_part = lax.optimization_barrier(
        (attn_arrived, gu_moving, down_moving, out_part)
    )
    their_out = core_swap(theirs(out_part))
    last_attn = [plane_swap(attn_grads[step], step) for step in range(3, chips)]
    while reach > 1:
        gu_kept, gu_sent = halves_along(add(gu_kept, gu_moving), 2, place)
        reach //= 2
        gu_moving = across(gu_sent, reach)
        if reach > 1:
            down_kept, down_sent = halves_along(add(down_kept, down_moving), 0, place)
            down_moving = across(down_sent, reach // 2)
    gu_sum = total([gu_kept, gu_moving])[:, :, 0]
    down_halves = halved(add(down_kept, down_moving)[0], chips // 2)
    layer_output = mine(mixed) + mine(out_part) + their_out
    attn_arrived, gu_sum, down_halves, layer_output = lax.optimization_barrier(
        (attn_arrived + last_attn, gu_sum, down_halves, layer_output)
    )
    pick = lambda value, first, dim: jnp.where(
        first, lax.index_in_dim(value, 0, dim, False), lax.index_in_dim(value, 1, dim, False)
    )
    gu_own = pick(gu_sum, first_core, 1)
    gu_their = core_swap(pick(gu_sum, core == 1, 1))
    attn_cuts = sum_plane(attn_arrived, onward)
    attn_sum = spread(attn_cuts)
    merged = total([near_back, back_arrived]).astype(bf16)
    later_steps = [chips // 2 >> turn for turn in range(1, chips.bit_length() - 1)]
    down_sum = after(summed_half(down_halves), attn_cuts)
    own_down = finished(halved(down_sum, later_steps[0]), later_steps[1:])
    back_sum = summed_half(halved(after(merged, attn_cuts), 1))
    back_halves = halved(back_sum, 2)

    weave = lambda parts: jnp.stack(
        [part.reshape(2, rows, chips, grain) for part in parts], axis=3
    ).reshape(2, rows, hidden)
    own_gu = weave(by_core(gu_own, gu_their))
    all_tokens = places * tok * cycle_size
    inverse_root = 1.0 / math.sqrt(all_tokens)
    ffin_new = update(ffin_weight, own_gu, ffin_momentum, ffin_average, ffin_rate * inverse_root)
    ffout_new = update(
        ffout_weight, own_down, ffout_momentum, ffout_average, ffout_rate * inverse_root
    )
    attn_sum, ffin_new, ffout_new, _ = lax.optimization_barrier((attn_sum, ffin_new, ffout_new, back_sum))
    first_grad = finished(back_halves, [2 << turn for turn in range(1, chips.bit_length() - 2)])
    summed, sent = last_sum(core, attn_sum)
    arrived = core_swap(sent)
    scale = rms_scale(flat_tokens)
    gained = first_grad * gains[0]
    inner = jnp.mean(gained * flat_tokens, axis=-1, keepdims=True)
    input_grad = mine(dmixed) + scale * gained - flat_tokens * (scale**3 * inner)

    attn_new = attention_update(
        core,
        summed,
        arrived,
        attention_weight,
        attention_momentum,
        attention_average,
        [rate * inverse_root for rate in attention_rates],
    )
    small_own, small_their = summed[-small_rows:], arrived[-small_rows:]
    gains_reduced = (small_own[:4] + small_their[:4]).reshape(gains.shape)
    pairs = heads // 4
    heads_of = lambda value: value[4 : 4 + pairs, : 2 * lanes].reshape(heads // 2, lanes)[:, : bias_table.shape[0]]
    bias_reduced = jnp.concatenate(by_core(heads_of(small_own), heads_of(small_their)), axis=0).T

    gain_rate = jnp.array(gain_rates, dtype=f32)[:, None] * inverse_root
    bias_new = update(bias_table, bias_reduced, bias_momentum, bias_average, bias_rate * inverse_root)
    gain_new = update(gains, gains_reduced, gain_momentum, gain_average, gain_rate)
    return (
        layer_output.reshape(tokens.shape),
        input_grad.reshape(tokens.shape),
        attn_new[0],
        ffin_new[0],
        ffout_new[0],
        bias_new[0],
        gain_new[0],
        attn_new[1],
        ffin_new[1],
        ffout_new[1],
        bias_new[1],
        gain_new[1],
        attn_new[2],
        ffin_new[2],
        ffout_new[2],
        bias_new[2],
        gain_new[2],
        attn_new[3],
        ffin_new[0].astype(bf16),
        ffout_new[0].astype(bf16),
    )


def solution(mesh):
    rows = P("batch", "seq", None)
    stacked = P(None, ("seq", "batch"), None)
    single = P(("seq", "batch"), None)
    weights = (stacked, stacked, single, P(), P())
    return jax.shard_map(
        shards,
        mesh=mesh,
        in_specs=(rows, rows, P("batch", "seq")) + weights * 3,
        out_specs=(rows, rows) + weights * 3 + (stacked, stacked, single),
        check_vma=False,
    )
```

```python
import functools
import math

import jax
import jax.numpy as jnp
from jax import lax
from jax.experimental import pallas as pl
from jax.experimental.pallas import tpu as pltpu
from jax.sharding import PartitionSpec as P

eps_norm = 1e-06
momentum_coef = 0.5
average_coef = 0.5
attention_rates = (0.0033, 0.0033, 0.025, 0.2)
ffin_rate = 0.063
ffout_rate = 0.023
bias_rate = 0.08
gain_rates = (0.045, 0.22)
thresholds = (12, 16, 23, 32, 46, 64, 91)
masked_score = -1e30
gelu_scale = math.sqrt(2.0 / math.pi)
gelu_cubic = 0.044715
bf16 = jnp.bfloat16
f32 = jnp.float32
vmem_bytes = 60 * 1024 * 1024
lanes = 128


def product(left, right, left_dim, right_dim):
    return lax.dot_general(
        left, right, (((left_dim,), (right_dim,)), ((), ())), preferred_element_type=f32
    )


def mm(left, right):
    return product(left, right, 1, 0)


def mm_nt(left, right):
    return product(left, right, 1, 1)


def mm_tn(left, right):
    return product(left, right, 0, 0)


def bucket_of(offset):
    magnitude = jnp.abs(offset)
    beyond = jnp.zeros_like(offset)
    for threshold in thresholds:
        beyond = beyond + (magnitude >= threshold).astype(jnp.int32)
    inside = jnp.where(magnitude < 8, magnitude, 8 + beyond)
    return inside + 16 * (offset > 0).astype(jnp.int32)


def update(weight, grad, momentum, average, rate):
    new_momentum = momentum_coef * momentum + grad
    new_weight = weight - rate * (grad + momentum_coef * new_momentum)
    new_average = average_coef * average + (1.0 - average_coef) * new_weight
    return (new_weight, new_momentum, new_average)


def rms_scale(values):
    return lax.rsqrt(jnp.mean(values * values, axis=-1, keepdims=True) + eps_norm)


def params():
    return pltpu.CompilerParams(vmem_limit_bytes=vmem_bytes)


def any_spec():
    return pl.BlockSpec(memory_space=pl.ANY)


def cost(flops, nbytes, exps=0):
    return pl.CostEstimate(flops=1, bytes_accessed=1, transcendentals=0)


def bias_kernel(table_ref, out_ref):
    head = pl.program_id(0)
    spot = lax.broadcasted_iota(jnp.int32, (8, 2 * lanes), 1)
    for block in range(3):
        buckets = bucket_of(lanes * (block - 1) + lanes - 1 - spot)
        row = jnp.zeros((8, 2 * lanes), f32)
        for bucket in range(table_ref.shape[0]):
            row = jnp.where(buckets == bucket, table_ref[bucket, head], row)
        wide = jnp.broadcast_to(row[:1], (lanes, 2 * lanes))
        rolled = pltpu.roll(wide, lanes + 1, 1, stride=1, stride_axis=0)
        out_ref[0, lanes * (block + 1) : lanes * (block + 2), :] = rolled[:, :lanes]
    out_ref[0, 0:lanes, :] = jnp.full((lanes, lanes), table_ref[15, head], f32)
    out_ref[0, 4 * lanes : 5 * lanes, :] = jnp.full((lanes, lanes), table_ref[31, head], f32)


def bias_rows(table):
    heads = table.shape[1]
    return pl.pallas_call(
        bias_kernel,
        grid=(heads,),
        in_specs=[pl.BlockSpec(memory_space=pltpu.SMEM)],
        out_specs=pl.BlockSpec((1, 5 * lanes, lanes), lambda i: (i, 0, 0)),
        out_shape=jax.ShapeDtypeStruct((heads, 5 * lanes, lanes), f32),
        compiler_params=params(),
        cost_estimate=cost(heads * 3e6, 4e6),
        name="bias_rows",
    )(table)


def ready_kernel(meta_ref, attn_ref, ffin_ref, ffout_ref, tokens_ref, ids_ref, gain_ref, *outs):
    attn_out, attn_send, gu_out, gu_send, row_out = outs
    core = meta_ref[0]
    first = core == 0
    width = tokens_ref.shape[1]
    half = width // 2
    low = attn_ref[...].astype(bf16)
    left, right = low[..., :half], low[..., half:]
    attn_out[0:3, core] = jnp.where(first, left[:3], right[:3])
    attn_send[...] = jnp.where(first, right[:3], left[:3])
    attn_out[3, 0] = left[3]
    attn_out[3, 1] = right[3]
    grain = ffin_ref.shape[2] // (2 * meta_ref.shape[0])
    for index in range(meta_ref.shape[0]):
        start = 2 * index * grain
        even = ffin_ref[:, :, start : start + grain].astype(bf16)
        odd = ffin_ref[:, :, start + grain : start + 2 * grain].astype(bf16)
        cols = slice(index * grain, (index + 1) * grain)
        gu_out[:, core, :, cols] = jnp.where(first, even, odd)
        gu_send[:, :, cols] = jnp.where(first, odd, even)
    tok = tokens_ref.shape[0]
    tokens = tokens_ref[...]
    row_out[:tok, :] = (tokens * rms_scale(tokens) * gain_ref[0:1, :]).astype(bf16)
    ids = jnp.broadcast_to(ids_ref[...].astype(f32), (16, tok))
    ids = jnp.concatenate([ids, jnp.zeros((16, width - tok), f32)], axis=1)
    row_out[tok : tok + 16, :] = ids.astype(bf16)
    row_out[tok + 16 :, :] = ffout_ref[...].astype(bf16)


def make_ready(core, attention_weight, ffin_weight, ffout_weight, tokens, ids, gain, chips):
    tok, width = tokens.shape
    rows, half, hidden = attention_weight.shape[1], width // 2, ffin_weight.shape[2]
    return pl.pallas_call(
        ready_kernel,
        in_specs=[smem_spec()] + [whole_spec()] * 6,
        out_specs=[whole_spec()] * 5,
        out_shape=[
            shaped(bf16, 4, 2, rows, half),
            shaped(bf16, 3, rows, half),
            shaped(bf16, 2, 2, rows, hidden // 2),
            shaped(bf16, 2, rows, hidden // 2),
            shaped(bf16, tok + 16 + ffout_weight.shape[0], width),
        ],
        compiler_params=params(),
        cost_estimate=cost(1e6, 2e6),
        name="make_ready",
    )(jnp.broadcast_to(core, (chips,)), attention_weight, ffin_weight, ffout_weight, tokens, ids, gain)


def fill_kernel(core_ref, kept_ref, arrived_ref, out_ref):
    count = arrived_ref.shape[0]
    out_ref[...] = kept_ref[...]
    out_ref[0:count, 1 - core_ref[0]] = arrived_ref[...]


def fill(core, kept, arrived):
    return pl.pallas_call(
        fill_kernel,
        in_specs=[smem_spec(), whole_spec(), whole_spec()],
        out_specs=whole_spec(),
        out_shape=shaped(bf16, *kept.shape),
        compiler_params=params(),
        cost_estimate=cost(0, 1e6),
        name="fill",
    )(core.reshape(1), kept, arrived)


def row_block(meta_ref, slot, rows):
    start = meta_ref[slot] * rows
    return pl.ds(pl.multiple_of(start, 16) if rows % 16 == 0 else start, rows)


def run_copies(pairs, sem):
    copies = [pltpu.make_async_copy(a, b, sem.at[i]) for i, (a, b) in enumerate(pairs)]
    for copy in copies:
        copy.start()
    return copies


def wait_all(copies):
    for copy in copies:
        copy.wait()


def whole_spec():
    return pl.BlockSpec(memory_space=pltpu.VMEM)


def smem_spec():
    return pl.BlockSpec(memory_space=pltpu.SMEM)


def dma(count):
    return pltpu.SemaphoreType.DMA((count,))


def shaped(kind, *shape):
    return jax.ShapeDtypeStruct(shape, kind)


def rows_kernel(meta_ref, near_ref, far_ref, full_ref, turned_ref, mask_ref):
    chips = near_ref.shape[0]
    core = meta_ref[chips]
    groups = lambda block: block[lanes : lanes + 16, :lanes].astype(f32)[:1, :]
    mine, other = groups(near_ref[0]), groups(far_ref[0])
    chip_ids = jnp.where(
        core == 0,
        jnp.concatenate([mine, other], axis=1),
        jnp.concatenate([other, mine], axis=1),
    )
    for source, side in ((near_ref, core), (far_ref, 1 - core)):
        for step in range(chips):
            block = source[step]
            start = (meta_ref[step] * 2 + side) * lanes
            place = pl.ds(pl.multiple_of(start, lanes), lanes)
            normed = block[:lanes, :]
            full_ref[place, :] = normed
            turned_ref[:, place] = normed.T
            wide = jnp.broadcast_to(groups(block), (lanes, lanes)).T
            same = jnp.concatenate([wide, wide], axis=1) == chip_ids
            mask_ref[place, :] = jnp.where(same, 0.0, masked_score)


def place_rows(meta, near, far):
    chips, _, width = near.shape
    length = 2 * chips * lanes
    return pl.pallas_call(
        rows_kernel,
        in_specs=[smem_spec()] + [whole_spec()] * 2,
        out_specs=[whole_spec()] * 3,
        out_shape=[
            shaped(bf16, length, width),
            shaped(bf16, width, length),
            shaped(f32, length, 2 * lanes),
        ],
        compiler_params=params(),
        cost_estimate=cost(3e6, 8e6),
        name="place_rows",
    )(meta, near, far)


def one_head(matrix, half):
    first = lax.broadcasted_iota(jnp.int32, matrix.shape, 1) < matrix.shape[1] // 2
    return jnp.where(first if half == 0 else jnp.logical_not(first), matrix, jnp.zeros_like(matrix))


def band_place(block, chip, part):
    kind = jnp.clip(block - (2 * chip + part) + 2, 0, 4)
    return pl.ds(pl.multiple_of(kind * lanes, lanes), lanes)


def attend_kernel(count, meta_ref, rows_ref, mask_ref, bias_ref, *refs):
    pieces = refs[:count]
    q_ref, k_ref, v_ref, p_ref, o_ref, low_ref, out_rows = refs[count : count + 7]
    weight, score, soft, sem, out_sem = refs[count + 7 :]
    pair = pl.program_id(0)
    chip = meta_ref[0]
    length = rows_ref.shape[0]
    blocks = length // lanes
    group = 2 * lanes
    stacked = [(piece.at[3], out_rows.at[step]) for step, piece in enumerate(pieces)]

    @pl.when(pair == 0)
    def _():
        loads = run_copies(load_pairs(pieces, meta_ref, 0, weight), sem)
        run_copies(stacked, out_sem)
        wait_all(loads)

    cols = pl.ds(pl.multiple_of(pair * lanes, lanes), lanes)
    own = rows_ref[pl.ds(pl.multiple_of(chip * group, group), group), :]
    query = mm(own, weight[0, :, cols]).astype(bf16)
    both = jnp.concatenate([weight[1, :, cols], weight[2, :, cols]], axis=1)
    key_value = mm(rows_ref[...], both).astype(bf16)
    key, value = key_value[:, :lanes], key_value[:, lanes:]
    q_ref[...] = query
    k_ref[...] = key
    v_ref[...] = value
    score[...] = mm_nt(key, jnp.concatenate([one_head(query, half) for half in range(2)], axis=0))
    for half in range(2):
        lane = slice(half * group, (half + 1) * group)
        best = jnp.full((8, group), masked_score, f32)
        for block in range(blocks):
            rows = slice(block * lanes, (block + 1) * lanes)
            bias = [bias_ref[half, band_place(block, chip, part), :] for part in range(2)]
            now = score[rows, lane] + jnp.concatenate(bias, axis=1) + mask_ref[rows, :]
            score[rows, lane] = now
            best = jnp.maximum(best, jnp.max(now.reshape(lanes // 8, 8, group), axis=0))
        top = jnp.max(best, axis=0, keepdims=True)
        total = jnp.zeros((8, group), f32)
        for block in range(blocks):
            rows = slice(block * lanes, (block + 1) * lanes)
            now = jnp.exp(score[rows, lane] - top)
            score[rows, lane] = now
            total = total + jnp.sum(now.reshape(lanes // 8, 8, group), axis=0)
        inverse = 1.0 / jnp.sum(total, axis=0, keepdims=True)
        for block in range(blocks):
            rows = slice(block * lanes, (block + 1) * lanes)
            now = score[rows, lane] * inverse
            p_ref[half, rows, :] = now
            soft[rows, lane] = now.astype(bf16)
    features = lanes // 2
    both_turned = mm_tn(value, soft[...])
    turned = [both_turned[:features, :group], both_turned[features:, group:]]
    attended = jnp.concatenate(turned, axis=0).T
    o_ref[...] = attended
    low_ref[...] = attended.astype(bf16)

    @pl.when(pair == pl.num_programs(0) - 1)
    def _():
        wait_all([pltpu.make_async_copy(a, b, out_sem.at[i]) for i, (a, b) in enumerate(stacked)])


def attend(pieces, meta, rows, mask, bias):
    length, width = rows.shape
    half = width // 2
    group = 2 * lanes
    pairs = half // lanes
    col = lambda i, *_: (0, i)
    fixed = lambda i, *_: (0, 0)
    flops = 2 * (group * width * half + 2 * length * width * half + 4 * group * length * half)
    return pl.pallas_call(
        functools.partial(attend_kernel, len(pieces)),
        grid_spec=pltpu.PrefetchScalarGridSpec(
            num_scalar_prefetch=1,
            grid=(pairs,),
            in_specs=[
                pl.BlockSpec((length, width), fixed),
                pl.BlockSpec((length, group), fixed),
                pl.BlockSpec((2, 5 * lanes, lanes), lambda i, *_: (i, 0, 0)),
            ]
            + [any_spec()] * len(pieces),
            out_specs=[
                pl.BlockSpec((group, lanes), col),
                pl.BlockSpec((length, lanes), col),
                pl.BlockSpec((length, lanes), col),
                pl.BlockSpec((2, length, group), lambda i, *_: (i, 0, 0)),
                pl.BlockSpec((group, lanes), col),
                pl.BlockSpec((group, lanes), col),
                pl.BlockSpec((len(pieces),) + pieces[0].shape[1:], lambda i, *_: (0, 0, 0)),
            ],
            scratch_shapes=[
                pltpu.VMEM((3, width, half), bf16),
                pltpu.VMEM((length, 2 * group), f32),
                pltpu.VMEM((length, 2 * group), bf16),
                dma(len(pieces)),
                dma(len(pieces)),
            ],
        ),
        out_shape=[
            shaped(bf16, group, half),
            shaped(bf16, length, half),
            shaped(bf16, length, half),
            shaped(f32, 2 * pairs, length, group),
            shaped(f32, group, half),
            shaped(bf16, group, half),
            shaped(bf16, len(pieces), *pieces[0].shape[1:]),
        ],
        compiler_params=params(),
        cost_estimate=cost(flops, 30e6, 2 * group * length * pairs),
        name="attend",
    )(meta, rows, mask, bias, *pieces)


def mix_kernel(
    meta_ref, tokens_ref, own_ref, their_ref, gain_ref, near_ref, far_ref, mixed_ref, normed_ref, turned_ref, joined_ref, weight_ref, held, sem
):
    chips, rows, half = near_ref.shape
    rows = rows // 2
    pairs = []
    for index, source in enumerate((near_ref, far_ref)):
        for step in range(chips):
            place = row_block(meta_ref, 1 + index * chips + step, rows)
            for side in range(2):
                pairs.append(
                    (
                        source.at[step, side * rows : (side + 1) * rows, :],
                        weight_ref.at[place, side * half : (side + 1) * half],
                    )
                )
    copies = run_copies(pairs, sem)
    first = meta_ref[0] == 0
    held[:, :half] = jnp.where(first, own_ref[...], their_ref[...])
    held[:, half:] = jnp.where(first, their_ref[...], own_ref[...])
    joined_ref[...] = held[...].T
    wait_all(copies)
    mixed = tokens_ref[...] + mm(held[...], weight_ref[...])
    mixed_ref[...] = mixed
    normed = (mixed * rms_scale(mixed) * gain_ref[...]).astype(bf16)
    normed_ref[...] = normed
    turned_ref[...] = normed.T


def mix(meta, tokens, own, their, gain, near, far):
    group, half = own.shape
    width = 2 * half
    return pl.pallas_call(
        mix_kernel,
        in_specs=[smem_spec()] + [whole_spec()] * 4 + [any_spec()] * 2,
        out_specs=[whole_spec()] * 5,
        out_shape=[
            shaped(f32, group, width),
            shaped(bf16, group, width),
            shaped(bf16, width, group),
            shaped(bf16, width, group),
            shaped(bf16, width, width),
        ],
        scratch_shapes=[pltpu.VMEM((group, width), bf16), dma(4 * near.shape[0])],
        compiler_params=params(),
        cost_estimate=cost(4 * group * width * half, 4e6),
        name="mix",
    )(meta, tokens, own, their, gain, near, far)


def feed_kernel(
    chips,
    places,
    gu_count,
    meta_ref,
    normed_low,
    turned_low,
    cot_ref,
    *refs,
):
    refs = list(refs)
    take = lambda n: [refs.pop(0) for _ in range(n)]
    gu_pieces = take(gu_count)
    down_pieces = take(places)
    out_ref, back_ref = take(2)
    gu_outs, down_outs = take(chips), take(2)
    gu, down, grad_gu, grad_down, cot_low = take(5)
    gu_sem, down_sem, gu_out_sem, down_out_sem = take(4)
    step = pl.program_id(0)
    steps = pl.num_programs(0)
    block = 512

    count = gu.shape[2] // block

    def gu_loads(turn):
        columns = pl.ds(pl.multiple_of(turn * block, block), block)
        pairs = []
        for index, piece in enumerate(gu_pieces):
            place = row_block(meta_ref, min(index, chips - 1), piece.shape[1])
            lead = slice(0, 2) if piece.shape[0] == 2 else slice(index - 3, index - 2)
            pairs.append((piece.at[:, :, columns], gu.at[lead, place, columns]))
        return [
            pltpu.make_async_copy(a, b, gu_sem.at[turn, index]) for index, (a, b) in enumerate(pairs)
        ]

    def gu_stores(turn):
        columns = pl.ds(pl.multiple_of(turn * block, block), block)
        copies = []
        for chip, out in enumerate(gu_outs):
            source = grad_gu.at[:, row_block(meta_ref, chip, out.shape[1]), columns]
            copies.append(pltpu.make_async_copy(source, out.at[:, :, columns], gu_out_sem.at[turn, chip]))
        return copies

    @pl.when(step == 0)
    def _():
        for copy in gu_loads(0):
            copy.start()
        pairs = []
        slot = chips
        for piece in down_pieces:
            for chip in range(chips):
                pairs.append((piece.at[chip], down.at[row_block(meta_ref, slot, piece.shape[1]), :]))
                slot += 1
        down_copies = run_copies(pairs, down_sem)
        for turn in range(1, count):
            for copy in gu_loads(turn):
                copy.start()
        cot_low[...] = cot_ref[...].astype(bf16)
        out_ref[...] = jnp.zeros_like(out_ref)
        back_ref[...] = jnp.zeros_like(back_ref)
        wait_all(down_copies)

    for copy in gu_loads(step):
        copy.wait()
    cols = pl.ds(pl.multiple_of(step * block, block), block)
    normed = normed_low[...]
    cot = cot_low[...]
    gate_w, up_w, down_w = gu[0, :, cols], gu[1, :, cols], down[cols, :]
    gate, up = mm(normed, gate_w), mm(normed, up_w)
    square = gate * gate
    curve = jnp.tanh(gelu_scale * gate * (1.0 + gelu_cubic * square))
    half = 0.5 * (1.0 + curve)
    gelu = gate * half
    slope = half + 0.5 * gate * (1.0 - curve * curve) * gelu_scale * (1.0 + 3.0 * gelu_cubic * square)
    hidden = (gelu * up).astype(bf16)
    dh = mm_nt(cot, down_w)
    dgate = (dh * up * slope).astype(bf16)
    dup = (dh * gelu).astype(bf16)
    out_ref[...] += mm(hidden, down_w)
    back_ref[...] += mm_nt(dgate, gate_w) + mm_nt(dup, up_w)
    grad_down[cols, :] = mm_tn(hidden, cot).astype(bf16)
    both = mm(turned_low[...], jnp.concatenate([dgate, dup], axis=1)).astype(bf16)
    grad_gu[0, :, cols] = both[:, :block]
    grad_gu[1, :, cols] = both[:, block:]

    for copy in gu_stores(step):
        copy.start()

    @pl.when(step == steps - 1)
    def _():
        pairs = []
        for turn, out in enumerate(down_outs):
            for spot in range(places // 2):
                for chip in range(chips):
                    slot = chips * (1 + places + turn * (places // 2) + spot) + chip
                    place = row_block(meta_ref, slot, out.shape[2])
                    pairs.append((grad_down.at[place, :], out.at[spot, chip]))
        down_copies = run_copies(pairs, down_out_sem)
        for turn in range(count):
            wait_all(gu_stores(turn))
        wait_all(down_copies)


def feed(gu_pieces, down_pieces, meta, normed, turned, cot, chips, places):
    group, width = normed.shape
    hidden = gu_pieces[0].shape[2]
    block = 512
    fixed = lambda i, *_: (0, 0)
    full = lambda *shape: pl.BlockSpec(shape, fixed)
    flops = 2 * 9 * group * width * hidden
    results = pl.pallas_call(
        functools.partial(feed_kernel, chips, places, len(gu_pieces)),
        grid_spec=pltpu.PrefetchScalarGridSpec(
            num_scalar_prefetch=1,
            grid=(hidden // block,),
            in_specs=[full(group, width), full(width, group), full(group, width)]
            + [any_spec()] * (len(gu_pieces) + places),
            out_specs=[full(group, width)] * 2 + [any_spec()] * (chips + 2),
            scratch_shapes=[
                pltpu.VMEM((2, width, hidden), bf16),
                pltpu.VMEM((hidden, width), bf16),
                pltpu.VMEM((2, width, hidden), bf16),
                pltpu.VMEM((hidden, width), bf16),
                pltpu.VMEM((group, width), bf16),
                pltpu.SemaphoreType.DMA((hidden // block, len(gu_pieces))),
                dma(chips * places),
                pltpu.SemaphoreType.DMA((hidden // block, chips)),
                dma(chips * places),
            ],
        ),
        out_shape=[shaped(f32, group, width)] * 2
        + [shaped(bf16, 2, width // chips, hidden)] * chips
        + [shaped(bf16, places // 2, chips, hidden // (chips * places), width)] * 2,
        compiler_params=params(),
        cost_estimate=cost(flops, 25e6, group * hidden),
        name="feed",
    )(meta, normed, turned, cot, *gu_pieces, *down_pieces)
    return results[:2], results[2 : 2 + chips], results[2 + chips :]


def settle_kernel(
    meta_ref,
    mixed_ref,
    cot_ref,
    back_ref,
    arrived_ref,
    weight_ref,
    gain_ref,
    dmixed_ref,
    do_ref,
    gain_grad_ref,
    branch_ref,
):
    core = meta_ref[0]
    half = do_ref.shape[1]
    mixed = mixed_ref[...]
    scale = rms_scale(mixed)
    dn2 = back_ref[...] + arrived_ref[...]
    gained = dn2 * gain_ref[...]
    inner = jnp.mean(gained * mixed, axis=-1, keepdims=True)
    dmixed = cot_ref[...] + scale * gained - mixed * (scale * scale * scale * inner)
    dmixed_ref[...] = dmixed
    gain_grad_ref[...] = 0.5 * jnp.sum(dn2 * mixed * scale, axis=0, keepdims=True)
    branch = dmixed.astype(bf16)
    branch_ref[...] = branch
    mine = weight_ref[pl.ds(pl.multiple_of(core * half, half), half), :]
    do_ref[...] = mm_nt(branch, mine).astype(bf16)


def settle(meta, mixed, cot, back, arrived, weight, gain):
    group, width = mixed.shape
    half = width // 2
    return pl.pallas_call(
        settle_kernel,
        in_specs=[smem_spec()] + [whole_spec()] * 6,
        out_specs=[whole_spec()] * 4,
        out_shape=[
            shaped(f32, group, width),
            shaped(bf16, group, half),
            shaped(f32, 1, width),
            shaped(bf16, group, width),
        ],
        compiler_params=params(),
        cost_estimate=cost(2 * group * width * half, 6e6),
        name="settle",
    )(meta, mixed, cot, back, arrived, weight, gain)


def band_rows(band_ref):
    line = lax.broadcasted_iota(jnp.int32, (8, 2 * lanes), 0)
    none = jnp.zeros((8, lanes), f32)
    found = []
    for block in range(3):
        summed = jnp.zeros((8, 2 * lanes), f32)
        for part in range(lanes // 8):
            start = lanes * (block + 1) + 8 * part
            wide = jnp.concatenate([band_ref[start : start + 8, :], none], axis=1)
            move = lanes - 8 - 8 * part
            summed = summed + (pltpu.roll(wide, move, 1) if move else wide)
        for bit in range(3):
            step = 1 << bit
            summed = jnp.where((line & step) == 0, pltpu.roll(summed, step, 1), summed)
        found.append(jnp.sum(summed, axis=0, keepdims=True))
    return jnp.concatenate(found, axis=1)


def retreat_kernel(meta_ref, do_ref, o_ref, q_ref, k_ref, v_ref, p_ref, dq_ref, dkv_ref, bias_ref, low, soft_low, spread_of, band_ref, onehot):
    chip = meta_ref[0]
    blocks = k_ref.shape[0] // lanes
    group = 2 * lanes
    features = lanes // 2
    do = do_ref[...]
    spread = (do.astype(f32) * o_ref[...]).T
    band_ref[...] = jnp.zeros_like(band_ref)
    far = jnp.zeros((8, lanes), f32)
    rows_of = []

    @pl.when(pl.program_id(0) == 0)
    def _():
        bucket = lax.broadcasted_iota(jnp.int32, (6 * lanes, lanes), 1)
        spot = lax.broadcasted_iota(jnp.int32, (6 * lanes, lanes), 0)
        offset = lanes * (spot // (2 * lanes)) - 1 - spot % (2 * lanes)
        onehot[...] = (bucket_of(offset) == bucket).astype(f32)

    do_two = jnp.concatenate([one_head(do, half) for half in range(2)], axis=0)
    query_two = jnp.concatenate([one_head(q_ref[...], half) for half in range(2)], axis=0)
    spread_of[...] = mm_nt(v_ref[...], do_two)
    for half in range(2):
        lane = slice(half * group, (half + 1) * group)
        delta = jnp.sum(spread[half * features : (half + 1) * features], axis=0, keepdims=True)
        for block in range(blocks):
            rows = slice(block * lanes, (block + 1) * lanes)
            soft = p_ref[half, rows, :]
            ds = soft * (spread_of[rows, lane] - delta)
            for part in range(2):
                place = band_place(block, chip, part)
                band_ref[place, :] += ds[:, part * lanes : (part + 1) * lanes]
            low[rows, lane] = ds.astype(bf16)
            soft_low[rows, lane] = soft.astype(bf16)
        rows_of.append(band_rows(band_ref))
        low_sum = jnp.sum(band_ref[0:lanes, :])
        high_sum = jnp.sum(band_ref[4 * lanes : 5 * lanes, :])
        lane_id = lax.broadcasted_iota(jnp.int32, (8, lanes), 1)
        line = lax.broadcasted_iota(jnp.int32, (8, lanes), 0)
        far = far + jnp.where((lane_id == 15) & (line == half), low_sum, 0.0)
        far = far + jnp.where((lane_id == 31) & (line == half), high_sum, 0.0)
        if half == 0:
            band_ref[...] = jnp.zeros_like(band_ref)
    dkv_ref[:, :lanes] = mm(low[...], query_two).astype(bf16)
    dkv_ref[:, lanes:] = mm(soft_low[...], do_two).astype(bf16)
    both_turned = mm_tn(k_ref[...], low[...])
    turned = [both_turned[:features, :group], both_turned[features:, group:]]
    dq_ref[...] = jnp.concatenate(turned, axis=0).T.astype(bf16)
    rows_of.append(jnp.zeros((6, rows_of[0].shape[1]), f32))
    near = lax.dot_general(
        jnp.concatenate(rows_of, axis=0),
        onehot[...],
        (((1,), (0,)), ((), ())),
        precision=lax.Precision.HIGHEST,
        preferred_element_type=f32,
    )
    bias_ref[0] = near + far


def retreat(meta, do, o, q, k, v, p):
    length, half = k.shape
    group = do.shape[0]
    pairs = half // lanes
    col = lambda i, *_: (0, i)
    deep = lambda i, *_: (i, 0, 0)
    flops = 2 * 8 * group * length * half
    return pl.pallas_call(
        retreat_kernel,
        grid_spec=pltpu.PrefetchScalarGridSpec(
            num_scalar_prefetch=1,
            grid=(pairs,),
            in_specs=[
                pl.BlockSpec((group, lanes), col),
                pl.BlockSpec((group, lanes), col),
                pl.BlockSpec((group, lanes), col),
                pl.BlockSpec((length, lanes), col),
                pl.BlockSpec((length, lanes), col),
                pl.BlockSpec((2, length, group), deep),
            ],
            out_specs=[
                pl.BlockSpec((group, lanes), col),
                pl.BlockSpec((length, 2 * lanes), col),
                pl.BlockSpec((1, 8, lanes), deep),
            ],
            scratch_shapes=[
                pltpu.VMEM((length, 2 * group), bf16),
                pltpu.VMEM((length, 2 * group), bf16),
                pltpu.VMEM((length, 2 * group), f32),
                pltpu.VMEM((5 * lanes, lanes), f32),
                pltpu.VMEM((6 * lanes, lanes), f32),
            ],
        ),
        out_shape=[
            shaped(bf16, group, half),
            shaped(bf16, length, 2 * half),
            shaped(f32, pairs, 8, lanes),
        ],
        compiler_params=params(),
        cost_estimate=cost(flops, 20e6),
        name="retreat",
    )(meta, do, o, q, k, v, p)


small_rows = 16


def load_pairs(pieces, meta_ref, first, weight):
    pairs = []
    for step, piece in enumerate(pieces):
        place = row_block(meta_ref, first + step, piece.shape[1])
        pairs.append((piece.at[0:3], weight.at[:, place, :]))
    return pairs


def grads_kernel(
    chips, meta_ref, turned_ref, dq_ref, dkv_ref, gains_ref, second_ref, bias_ref, joined_ref, branch_ref, *refs
):
    refs = list(refs)
    take = lambda n: [refs.pop(0) for _ in range(n)]
    pieces, outs = take(chips), take(chips)
    weight, grad, wo, small, sem, out_sem = take(6)
    chip, core = meta_ref[0], meta_ref[1]
    width = turned_ref.shape[0]
    half = width // 2
    group = dq_ref.shape[0]
    loads = run_copies(load_pairs(pieces, meta_ref, 2, weight), sem)
    wo_rows = wo.shape[1]
    mine = []
    for index in range(chips):
        even = joined_ref[2 * index * wo_rows : (2 * index + 1) * wo_rows, :]
        odd = joined_ref[(2 * index + 1) * wo_rows : (2 * index + 2) * wo_rows, :]
        mine.append(jnp.where(core == 0, even, odd))
    out_grad = mm(jnp.concatenate(mine, axis=0), branch_ref[...]).astype(bf16)
    for index in range(chips):
        wo[index] = out_grad[index * wo_rows : (index + 1) * wo_rows]
    own_rows = pl.ds(pl.multiple_of(chip * group, group), group)
    query_grad = mm(turned_ref[:, own_rows], dq_ref[...])
    grad[0] = query_grad.astype(bf16)
    wait_all(loads)
    along_row = [query_grad[:, at : at + lanes] * weight[0, :, at : at + lanes].astype(f32) for at in range(0, half, lanes)]
    along_row = sum(along_row[1:], along_row[0])
    for pair in range(half // lanes):
        wide = slice(pair * 2 * lanes, (pair + 1) * 2 * lanes)
        cols = slice(pair * lanes, (pair + 1) * lanes)
        summed = mm(turned_ref[...], dkv_ref[:, wide])
        low = summed.astype(bf16)
        grad[1, :, cols] = low[:, :lanes]
        grad[2, :, cols] = low[:, lanes:]
        along_row = along_row + summed[:, :lanes] * weight[1, :, cols].astype(f32)
        along_row = along_row + summed[:, lanes:] * weight[2, :, cols].astype(f32)
    first_gain = jnp.sum(along_row.T, axis=0, keepdims=True) / gains_ref[...]
    second_gain = second_ref[...]
    lines = [first_gain[:, :half], first_gain[:, half:], second_gain[:, :half], second_gain[:, half:]]
    for pair in range(bias_ref.shape[0]):
        both = [bias_ref[pair, 0:1, :], bias_ref[pair, 1:2, :]]
        both.append(jnp.zeros((1, half - 2 * lanes), f32))
        lines.append(jnp.concatenate(both, axis=1))
    lines.append(jnp.zeros((small_rows - len(lines), half), f32))
    small[...] = jnp.concatenate(lines, axis=0).astype(bf16)
    rows = width // chips
    side_rows = rows // 2
    pairs = []
    for step, out in enumerate(outs):
        place = row_block(meta_ref, 2 + step, rows)
        at = 0
        for matrix in range(3):
            pairs.append((grad.at[matrix, place, :], out.at[at : at + rows, :]))
            at += rows
        for side in range(2):
            source = wo.at[meta_ref[2 + step], :, side * half : (side + 1) * half]
            pairs.append((source, out.at[at : at + side_rows, :]))
            at += side_rows
        pairs.append((small, out.at[at : at + small_rows, :]))
    wait_all(run_copies(pairs, out_sem))


def weight_grads(pieces, meta, turned, dq, dkv, gain, second, bias, joined, branch, chips):
    width, length = turned.shape
    half = width // 2
    group = dq.shape[0]
    flops = 2 * (2 * length * width * half + group * width * half)
    block = width // chips
    return pl.pallas_call(
        functools.partial(grads_kernel, chips),
        in_specs=[smem_spec()] + [whole_spec()] * 8 + [any_spec()] * len(pieces),
        out_specs=[any_spec()] * chips,
        out_shape=[shaped(bf16, 4 * block + small_rows, half)] * chips,
        scratch_shapes=[
            pltpu.VMEM((3, width, half), bf16),
            pltpu.VMEM((3, width, half), bf16),
            pltpu.VMEM((chips, block // 2, width), bf16),
            pltpu.VMEM((small_rows, half), bf16),
            dma(chips),
            dma(6 * chips),
        ],
        compiler_params=params(),
        cost_estimate=cost(flops, 12e6),
        name="weight_grads",
    )(meta, turned, dq, dkv, gain, second, bias, joined, branch, *pieces)


def back_kernel(chips, meta_ref, dq_ref, dkv_ref, *refs):
    refs = list(refs)
    take = lambda n: [refs.pop(0) for _ in range(n)]
    pieces = take(chips)
    near_out, far_out = take(2)
    weight, both, back, sem = take(4)
    chip, core = meta_ref[0], meta_ref[1]
    length = dkv_ref.shape[0]
    half = dq_ref.shape[1]
    group = dq_ref.shape[0]
    wait_all(run_copies(load_pairs(pieces, meta_ref, 2, weight), sem))
    for pair in range(half // lanes):
        wide = pair * 2 * lanes
        cols = slice(pair * lanes, (pair + 1) * lanes)
        both[:, wide : wide + lanes] = weight[1, :, cols]
        both[:, wide + lanes : wide + 2 * lanes] = weight[2, :, cols]
    for start in range(0, length, group):
        back[start : start + group, :] = mm_nt(dkv_ref[start : start + group, :], both[...])
    own_rows = pl.ds(pl.multiple_of(chip * group, group), group)
    back[own_rows, :] += mm_nt(dq_ref[...], weight[0])
    for index, step in enumerate(bit_reversed(chips)):
        for side, out in ((core, near_out), (1 - core, far_out)):
            start = meta_ref[2 + step] * group + side * lanes
            out[index] = back[pl.ds(pl.multiple_of(start, lanes), lanes), :].astype(bf16)


def row_grads(pieces, meta, dq, dkv, chips):
    length, width = dkv.shape
    half = width // 2
    return pl.pallas_call(
        functools.partial(back_kernel, chips),
        in_specs=[smem_spec()] + [whole_spec()] * 2 + [any_spec()] * len(pieces),
        out_specs=[whole_spec()] * 2,
        out_shape=[shaped(bf16, chips, lanes, width)] * 2,
        scratch_shapes=[
            pltpu.VMEM((3, width, half), bf16),
            pltpu.VMEM((width, width), bf16),
            pltpu.VMEM((length, width), f32),
            dma(chips),
        ],
        compiler_params=params(),
        cost_estimate=cost(4 * length * width * half, 8e6),
        name="row_grads",
    )(meta, dq, dkv, *pieces)


def cut_kernel(side_ref, *refs):
    sources, (kept_ref, sent_ref) = refs[:-2], refs[-2:]
    count = kept_ref.shape[2]
    for index, out in ((side_ref[0], kept_ref), (1 - side_ref[0], sent_ref)):
        for part in range(2):
            start = pl.multiple_of((2 * part + index) * count, count)
            out[0, part] = total([source[0, pl.ds(start, count), :] for source in sources]).astype(bf16)


def cut_plane(blocks, side):
    lead, height, width = blocks[0].shape
    shape = (lead, 2, height // 4, width)
    row = lambda *shape: pl.BlockSpec((1,) + shape, lambda i: (i,) + (0,) * len(shape))
    return pl.pallas_call(
        cut_kernel,
        grid=(lead,),
        in_specs=[smem_spec()] + [row(height, width)] * len(blocks),
        out_specs=[row(*shape[1:])] * 2,
        out_shape=[shaped(bf16, *shape)] * 2,
        compiler_params=params(),
        cost_estimate=cost(1e6, 6e6),
        name="cut_plane",
    )(side.reshape(1), *blocks)


def sum_kernel(order_ref, *refs):
    places = order_ref.shape[0]
    sources, outs, total_ref = refs[: -1 - places], refs[-1 - places : -1], refs[-1]
    total_ref[...] = total([source[...] for source in sources])
    height = total_ref.shape[0] - small_rows
    rows = height // (8 * places)
    last = total_ref[height:, :]
    for turn, out in enumerate(outs):
        parts = []
        for block in range(8):
            start = block * places * rows + order_ref[turn] * rows
            parts.append(total_ref[pl.ds(pl.multiple_of(start, 8), rows), :])
        out[...] = jnp.concatenate(parts + [last], axis=0).astype(bf16)


def sum_plane(blocks, order):
    height, half = blocks[0].shape
    places = order.shape[0]
    rows = (height - small_rows) // (8 * places)
    if rows % 8:
        summed = total(blocks).astype(bf16)
        split, last = summed[:-small_rows].reshape(8, places, rows, half), summed[-small_rows:]
        pick = lambda turn: lax.dynamic_index_in_dim(split, order[turn], 1, keepdims=False)
        return [jnp.concatenate([pick(turn).reshape(-1, half), last], axis=0) for turn in range(places)]
    return pl.pallas_call(
        sum_kernel,
        in_specs=[smem_spec()] + [whole_spec()] * len(blocks),
        out_specs=[whole_spec()] * places,
        out_shape=[shaped(bf16, (height - small_rows) // places + small_rows, half)] * places,
        scratch_shapes=[pltpu.VMEM((height, half), f32)],
        compiler_params=params(),
        cost_estimate=cost(1e6, 4e6),
        name="sum_plane",
    )(order, *blocks)


def last_kernel(core_ref, *refs):
    sources, (sum_ref, sent_ref) = refs[:-2], refs[-2:]
    summed = total([source[...] for source in sources])
    sum_ref[...] = summed
    rows = (summed.shape[0] - small_rows) // 8
    first = core_ref[0] == 0
    block = lambda index: summed[index * rows : (index + 1) * rows]
    parts = [jnp.where(first, block(2 * matrix + 1), block(2 * matrix)) for matrix in range(3)]
    sent_ref[...] = jnp.concatenate(parts + [summed[8 * rows :]], axis=0)


def last_sum(core, arrived):
    height, half = arrived[0].shape
    rows = (height - small_rows) // 8
    return pl.pallas_call(
        last_kernel,
        in_specs=[smem_spec()] + [whole_spec()] * len(arrived),
        out_specs=[whole_spec()] * 2,
        out_shape=[shaped(f32, height, half), shaped(f32, 3 * rows + small_rows, half)],
        compiler_params=params(),
        cost_estimate=cost(1e6, 1e6),
        name="last_sum",
    )(core.reshape(1), *arrived)


def attention_kernel(
    rates, core_ref, sum_ref, arrived_ref, weight_ref, momentum_ref, average_ref, *outs
):
    new_weight, new_momentum, new_average, copy = outs
    rows, width = weight_ref.shape[1:]
    half = width // 2
    first = core_ref[0] == 0
    block = lambda index: sum_ref[index * rows : (index + 1) * rows, :]
    for matrix in range(4):
        left, right = block(2 * matrix), block(2 * matrix + 1)
        if matrix < 3:
            mine = jnp.where(first, left, right)
            theirs = arrived_ref[matrix * rows : (matrix + 1) * rows, :]
            left, right = jnp.where(first, mine, theirs), jnp.where(first, theirs, mine)
        for side, grad in enumerate((left, right)):
            at = (matrix, slice(None), slice(side * half, (side + 1) * half))
            values = update(
                weight_ref[at], grad, momentum_ref[at], average_ref[at], rates[matrix]
            )
            new_weight[at], new_momentum[at], new_average[at] = values
            copy[at] = values[0].astype(bf16)


def attention_update(core, summed, arrived, weight, momentum, average, rates):
    return pl.pallas_call(
        functools.partial(attention_kernel, rates),
        in_specs=[smem_spec()] + [whole_spec()] * 5,
        out_specs=[whole_spec()] * 4,
        out_shape=[shaped(f32, *weight.shape)] * 3 + [shaped(bf16, *weight.shape)],
        compiler_params=params(),
        cost_estimate=cost(1e6, 2e6),
        name="attention_update",
    )(core.reshape(1), summed, arrived, weight, momentum, average)


def core_swap(value):
    count = lax.axis_size("seq")
    return lax.ppermute(value, "seq", [(i, i ^ 1) for i in range(count)])


def plane_swap(value, step):
    count = lax.axis_size("seq")
    return lax.ppermute(value, "seq", [(i, i ^ (2 * step)) for i in range(count)])


def along(value, step):
    count = lax.axis_size("batch")
    return lax.ppermute(value, "batch", [(i, (i + step) % count) for i in range(count)])


def along_all(value):
    return [value] + [along(value, step) for step in range(1, lax.axis_size("batch"))]


def after(value, *earlier):
    return lax.optimization_barrier((value,) + earlier)[0]


def join_kernel(order_ref, *refs):
    sources, out = refs[:-1], refs[-1]
    for index, source in enumerate(sources):
        out[:, :, order_ref[index]] = source[...]


def join(blocks, order):
    lead, rest = blocks[0].shape[:2], blocks[0].shape[2:]
    return pl.pallas_call(
        join_kernel,
        in_specs=[smem_spec()] + [whole_spec()] * len(blocks),
        out_specs=whole_spec(),
        out_shape=shaped(bf16, *lead, len(blocks), *rest),
        compiler_params=params(),
        cost_estimate=cost(0, 2e6),
        name="join",
    )(order, *blocks)


def gather_plane(value):
    return [value] + [plane_swap(value, step) for step in range(1, lax.axis_size("seq") // 2)]


def total(blocks):
    summed = blocks[0].astype(f32)
    for block in blocks[1:]:
        summed = summed + block.astype(f32)
    return summed


def scatter_plane(blocks):
    return [blocks[0]] + [plane_swap(part, step) for step, part in enumerate(blocks) if step]


def bit_reversed(chips):
    order = [0]
    while len(order) < chips:
        order = [2 * step for step in order] + [2 * step + 1 for step in order]
    return order


def halves_along(value, dim, place):
    count = value.shape[dim] // 2
    split = value.reshape(value.shape[:dim] + (2, count) + value.shape[dim + 1 :])
    side = (place // count) % 2
    pick = lambda index: lax.dynamic_index_in_dim(split, index, dim, keepdims=False)
    return pick(side), pick(1 - side)


def across(value, step):
    count = lax.axis_size("batch")
    return lax.ppermute(value, "batch", [(i, i ^ step) for i in range(count)])


def halved(blocks, step):
    count = blocks.shape[0] // 2
    return blocks[:count], plane_swap(blocks[count:], step)


def summed_half(halves):
    return total(halves).astype(bf16)


def finished(halves, steps):
    for step in steps:
        halves = halved(summed_half(halves), step)
    return total(halves)[0]


def spread(values):
    return [values[0]] + [along(value, step) for step, value in enumerate(values) if step]


def spread_along(split, dim, place):
    count = lax.axis_size("batch")
    pick = lambda step: lax.dynamic_index_in_dim(split, (place + step) % count, dim, keepdims=False)
    return [pick(0)] + [along(pick(step), step) for step in range(1, count)]


def shards(
    tokens,
    cotangent,
    group_ids,
    attention_weight,
    ffin_weight,
    ffout_weight,
    bias_table,
    gains,
    attention_momentum,
    ffin_momentum,
    ffout_momentum,
    bias_momentum,
    gain_momentum,
    attention_average,
    ffin_average,
    ffout_average,
    bias_average,
    gain_average,
):
    _, tok, width = tokens.shape
    cycle_size, places = lax.axis_size("seq"), lax.axis_size("batch")
    cycle_index = lax.axis_index("seq").astype(jnp.int32)
    place = lax.axis_index("batch").astype(jnp.int32)
    chips = cycle_size // 2
    chip, core = cycle_index // 2, cycle_index % 2
    half = width // 2
    rows = attention_weight.shape[1]
    down_rows = ffout_weight.shape[0]
    hidden = ffin_weight.shape[2]
    grain = hidden // cycle_size
    heads = bias_table.shape[1]
    group = 2 * tok
    first_core = core == 0

    def by_core(mine, theirs):
        return [jnp.where(first_core, mine, theirs), jnp.where(first_core, theirs, mine)]

    steps = [chip ^ step for step in range(chips)]
    order = jnp.stack([(place + places - step) % places for step in range(places)])
    onward = jnp.stack([(place + step) % places for step in range(places)])
    flat_tokens, flat_cot = tokens.reshape(tok, width), cotangent.reshape(tok, width)

    attn_kept, attn_sent, gu_kept, gu_sent, row_block_own = make_ready(
        core,
        attention_weight,
        ffin_weight,
        ffout_weight,
        flat_tokens,
        group_ids,
        gains,
        chips,
    )
    their_tokens, their_cot = core_swap(flat_tokens), core_swap(flat_cot)
    attn_from, gu_from = core_swap(attn_sent), core_swap(gu_sent)
    row_block_own, attn_kept = lax.optimization_barrier((row_block_own, attn_kept, their_tokens, their_cot))[:2]
    attn_block = fill(core, after(attn_kept, gu_from), attn_from)
    gu_block = fill(core, gu_kept, gu_from)

    attn_blocks = along_all(attn_block)
    row_blocks, step = row_block_own[None], 1
    while step < chips:
        arrived = plane_swap(row_blocks, step)
        arrived = after(arrived, attn_block if step * 2 < chips else attn_blocks)
        row_blocks = jnp.concatenate([row_blocks, arrived], axis=0)
        step *= 2
    near_rows, down_block = row_blocks[:, : tok + 16], row_blocks[:, tok + 16 :]
    own_heads = jnp.where(first_core, bias_table[:, : heads // 2], bias_table[:, heads // 2 :])
    bias = bias_rows(after(own_heads, attn_block))

    attn_joined = join(after(attn_blocks, near_rows, bias, gu_block), order).reshape(4, 2 * places * rows, half)
    chip_tokens = jnp.concatenate(by_core(flat_tokens, their_tokens), axis=0)
    chip_cot = jnp.concatenate(by_core(flat_cot, their_cot), axis=0)
    far_rows = core_swap(after(near_rows, attn_joined))
    rows_full, turned, mask = place_rows(jnp.stack(steps + [core]), near_rows, far_rows)
    attn_pieces = gather_plane(attn_joined)
    gu_blocks = [after(gu_block, attn_joined)]
    for step in range(1, places):
        if step == 2:
            gu_blocks[-1], down_block = lax.optimization_barrier((gu_blocks[-1], down_block, rows_full))[:2]
        gu_blocks.append(along(gu_blocks[-1], 1))
    down_pieces = [down_block, along(down_block, 1)]
    gu_joined = join(gu_blocks, order)
    attn_pieces, rows_full, gu_joined, down_pieces = lax.optimization_barrier(
        (attn_pieces, rows_full, gu_joined, down_pieces)
    )
    chip_tokens, chip_cot, mask = lax.optimization_barrier((chip_tokens, chip_cot, mask))
    gu_joined, down_pieces, mask = lax.optimization_barrier((gu_joined, down_pieces, mask))
    down_pieces.append(along(down_pieces[-1], 1))
    gu_own = gu_joined.reshape(2, 2 * places * rows, hidden // 2)
    gu_pieces = [gu_own] + [plane_swap(gu_own, step) for step in range(1, 3 if chips == 4 else chips)]
    step_meta = jnp.stack(steps)
    query, key, value, soft, attended, attended_low, wo_near = attend(
        attn_pieces, step_meta, rows_full, mask, bias
    )
    wo_meta = jnp.stack([core] + [step * 2 + core for step in steps] + [step * 2 + 1 - core for step in steps])
    their_attended = core_swap(attended_low)
    their_attended, gu_pieces, down_pieces, wo_near = lax.optimization_barrier(
        (their_attended, gu_pieces, down_pieces, wo_near)
    )
    if chips == 4:
        passed = [gu_pieces[1][:1], gu_pieces[2][1:]]
        their_attended, passed, wo_near = lax.optimization_barrier((their_attended, passed, wo_near))
        gu_pieces += [plane_swap(passed[0], 2), plane_swap(passed[1], 1)]
    for _ in range(3, places):
        down_pieces.append(along(down_pieces[-1], 1))
    wo_far = core_swap(wo_near)
    mixed, second_low, second_turned, joined, out_weight = mix(
        wo_meta, chip_tokens, attended_low, their_attended, gains[1:2], wo_near, wo_far
    )
    down_meta = [step * places + order[index] for index in range(places) for step in steps]
    high = place // (places // 2)
    for side in (high, 1 - high):
        for spot in range(places // 2):
            down_meta += [step * places + side * (places // 2) + spot for step in steps]
    (out_part, back_part), gu_grads, down_grads = feed(
        gu_pieces, down_pieces, jnp.stack(steps + down_meta), second_low, second_turned, chip_cot, chips, places
    )
    add = lambda a, b: total([a, b]).astype(bf16)
    gu_arrived = scatter_plane(gu_grads)
    down_moving = across(down_grads[1], places // 2)
    their_back = core_swap(back_part)
    dmixed, attended_grad, second_gain, branch = settle(
        core.reshape(1), mixed, chip_cot, back_part, their_back, out_weight, gains[1:2]
    )
    dq, dkv, bias_part = retreat(chip.reshape(1), attended_grad, attended, query, key, value, soft)
    pair_meta = jnp.stack([chip, core] + steps)
    attn_grads = weight_grads(
        attn_pieces,
        pair_meta,
        turned,
        dq,
        dkv,
        gains[:1],
        second_gain,
        bias_part,
        joined,
        branch,
        chips,
    )

    near_back, far_back = row_grads(attn_pieces, pair_meta, after(dq, attn_grads), dkv, chips)
    mine = lambda value: lax.dynamic_slice_in_dim(value, core * tok, tok, 0)
    theirs = lambda value: lax.dynamic_slice_in_dim(value, (1 - core) * tok, tok, 0)
    back_arrived = core_swap(far_back)
    attn_grads, gu_arrived, down_moving = lax.optimization_barrier(
        (attn_grads, gu_arrived, down_moving, back_arrived)
    )[:3]
    attn_arrived = [attn_grads[0]] + [plane_swap(attn_grads[step], step) for step in range(1, min(chips, 3))]
    down_sum = add(down_moving, down_grads[0])
    reach = places // 2
    if rows * reach % 16 == 0:
        halves = cut_plane(gu_arrived, place // reach)
        gu_kept, gu_sent = [part.reshape(2, 2, reach, rows, hidden // 2) for part in halves]
    else:
        gu_sum = total(gu_arrived).astype(bf16).reshape(2, 2, places, rows, hidden // 2)
        gu_kept, gu_sent = halves_along(gu_sum, 2, place)
    gu_moving = across(gu_sent, reach)
    down_kept, down_sent = halves_along(down_sum, 0, place)
    down_moving = across(down_sent, reach // 2)
    attn_arrived, gu_moving, down_moving, out_part = lax.optimization_barrier(
        (attn_arrived, gu_moving, down_moving, out_part)
    )
    their_out = core_swap(theirs(out_part))
    last_attn = [plane_swap(attn_grads[step], step) for step in range(3, chips)]
    while reach > 1:
        gu_kept, gu_sent = halves_along(add(gu_kept, gu_moving), 2, place)
        reach //= 2
        gu_moving = across(gu_sent, reach)
        if reach > 1:
            down_kept, down_sent = halves_along(add(down_kept, down_moving), 0, place)
            down_moving = across(down_sent, reach // 2)
    gu_sum = total([gu_kept, gu_moving])[:, :, 0]
    down_halves = halved(add(down_kept, down_moving)[0], chips // 2)
    layer_output = mine(mixed) + mine(out_part) + their_out
    attn_arrived, gu_sum, down_halves, layer_output = lax.optimization_barrier(
        (attn_arrived + last_attn, gu_sum, down_halves, layer_output)
    )
    pick = lambda value, first, dim: jnp.where(
        first, lax.index_in_dim(value, 0, dim, False), lax.index_in_dim(value, 1, dim, False)
    )
    gu_own = pick(gu_sum, first_core, 1)
    gu_their = core_swap(pick(gu_sum, core == 1, 1))
    attn_cuts = sum_plane(attn_arrived, onward)
    attn_sum = spread(attn_cuts)
    merged = total([near_back, back_arrived]).astype(bf16)
    later_steps = [chips // 2 >> turn for turn in range(1, chips.bit_length() - 1)]
    back_sum = summed_half(halved(after(merged, attn_cuts), 1))
    back_halves = halved(back_sum, 2)
    down_sum = after(summed_half(down_halves), back_sum)
    own_down = finished(halved(down_sum, later_steps[0]), later_steps[1:])

    weave = lambda parts: jnp.stack(
        [part.reshape(2, rows, chips, grain) for part in parts], axis=3
    ).reshape(2, rows, hidden)
    own_gu = weave(by_core(gu_own, gu_their))
    all_tokens = places * tok * cycle_size
    inverse_root = 1.0 / math.sqrt(all_tokens)
    ffin_new = update(ffin_weight, own_gu, ffin_momentum, ffin_average, ffin_rate * inverse_root)
    ffout_new = update(
        ffout_weight, own_down, ffout_momentum, ffout_average, ffout_rate * inverse_root
    )
    ffin_new += (ffin_new[0].astype(bf16),)
    ffout_new += (ffout_new[0].astype(bf16),)
    attn_sum, ffin_new, _ = lax.optimization_barrier((attn_sum, ffin_new, back_sum))
    first_grad = finished(back_halves, [2 << turn for turn in range(1, chips.bit_length() - 2)])
    summed, sent = last_sum(core, attn_sum)
    arrived = core_swap(sent)
    scale = rms_scale(flat_tokens)
    gained = first_grad * gains[0]
    inner = jnp.mean(gained * flat_tokens, axis=-1, keepdims=True)
    input_grad = mine(dmixed) + scale * gained - flat_tokens * (scale**3 * inner)

    attn_new = attention_update(
        core,
        summed,
        arrived,
        attention_weight,
        attention_momentum,
        attention_average,
        [rate * inverse_root for rate in attention_rates],
    )
    small_own, small_their = summed[-small_rows:], arrived[-small_rows:]
    gains_reduced = (small_own[:4] + small_their[:4]).reshape(gains.shape)
    pairs = heads // 4
    heads_of = lambda value: value[4 : 4 + pairs, : 2 * lanes].reshape(heads // 2, lanes)[:, : bias_table.shape[0]]
    bias_reduced = jnp.concatenate(by_core(heads_of(small_own), heads_of(small_their)), axis=0).T

    gain_rate = jnp.array(gain_rates, dtype=f32)[:, None] * inverse_root
    bias_new = update(bias_table, bias_reduced, bias_momentum, bias_average, bias_rate * inverse_root)
    gain_new = update(gains, gains_reduced, gain_momentum, gain_average, gain_rate)
    return (
        layer_output.reshape(tokens.shape),
        input_grad.reshape(tokens.shape),
        attn_new[0],
        ffin_new[0],
        ffout_new[0],
        bias_new[0],
        gain_new[0],
        attn_new[1],
        ffin_new[1],
        ffout_new[1],
        bias_new[1],
        gain_new[1],
        attn_new[2],
        ffin_new[2],
        ffout_new[2],
        bias_new[2],
        gain_new[2],
        attn_new[3],
        ffin_new[3],
        ffout_new[3],
    )


def solution(mesh):
    rows = P("batch", "seq", None)
    stacked = P(None, ("seq", "batch"), None)
    single = P(("seq", "batch"), None)
    weights = (stacked, stacked, single, P(), P())
    return jax.shard_map(
        shards,
        mesh=mesh,
        in_specs=(rows, rows, P("batch", "seq")) + weights * 3,
        out_specs=(rows, rows) + weights * 3 + (stacked, stacked, single),
        check_vma=False,
    )
```

```python
import functools
import math

import jax
import jax.numpy as jnp
from jax import lax
from jax.experimental import pallas as pl
from jax.experimental.pallas import tpu as pltpu
from jax.sharding import PartitionSpec as P

eps_norm = 1e-06
momentum_coef = 0.5
average_coef = 0.5
attention_rates = (0.0033, 0.0033, 0.025, 0.2)
ffin_rate = 0.063
ffout_rate = 0.023
bias_rate = 0.08
gain_rates = (0.045, 0.22)
thresholds = (12, 16, 23, 32, 46, 64, 91)
masked_score = -1e30
gelu_scale = math.sqrt(2.0 / math.pi)
gelu_cubic = 0.044715
bf16 = jnp.bfloat16
f32 = jnp.float32
vmem_bytes = 60 * 1024 * 1024
lanes = 128


def product(left, right, left_dim, right_dim):
    return lax.dot_general(
        left, right, (((left_dim,), (right_dim,)), ((), ())), preferred_element_type=f32
    )


def mm(left, right):
    return product(left, right, 1, 0)


def mm_nt(left, right):
    return product(left, right, 1, 1)


def mm_tn(left, right):
    return product(left, right, 0, 0)


def bucket_of(offset):
    magnitude = jnp.abs(offset)
    beyond = jnp.zeros_like(offset)
    for threshold in thresholds:
        beyond = beyond + (magnitude >= threshold).astype(jnp.int32)
    inside = jnp.where(magnitude < 8, magnitude, 8 + beyond)
    return inside + 16 * (offset > 0).astype(jnp.int32)


def update(weight, grad, momentum, average, rate):
    new_momentum = momentum_coef * momentum + grad
    new_weight = weight - rate * (grad + momentum_coef * new_momentum)
    new_average = average_coef * average + (1.0 - average_coef) * new_weight
    return (new_weight, new_momentum, new_average)


def rms_scale(values):
    return lax.rsqrt(jnp.mean(values * values, axis=-1, keepdims=True) + eps_norm)


def params():
    return pltpu.CompilerParams(vmem_limit_bytes=vmem_bytes)


def any_spec():
    return pl.BlockSpec(memory_space=pl.ANY)


def cost(flops, nbytes, exps=0):
    return pl.CostEstimate(flops=1, bytes_accessed=1, transcendentals=0)


def bias_kernel(table_ref, out_ref):
    head = pl.program_id(0)
    spot = lax.broadcasted_iota(jnp.int32, (8, 2 * lanes), 1)
    for block in range(3):
        buckets = bucket_of(lanes * (block - 1) + lanes - 1 - spot)
        row = jnp.zeros((8, 2 * lanes), f32)
        for bucket in range(table_ref.shape[0]):
            row = jnp.where(buckets == bucket, table_ref[bucket, head], row)
        wide = jnp.broadcast_to(row[:1], (lanes, 2 * lanes))
        rolled = pltpu.roll(wide, lanes + 1, 1, stride=1, stride_axis=0)
        out_ref[0, lanes * (block + 1) : lanes * (block + 2), :] = rolled[:, :lanes]
    out_ref[0, 0:lanes, :] = jnp.full((lanes, lanes), table_ref[15, head], f32)
    out_ref[0, 4 * lanes : 5 * lanes, :] = jnp.full((lanes, lanes), table_ref[31, head], f32)


def bias_rows(table):
    heads = table.shape[1]
    return pl.pallas_call(
        bias_kernel,
        grid=(heads,),
        in_specs=[pl.BlockSpec(memory_space=pltpu.SMEM)],
        out_specs=pl.BlockSpec((1, 5 * lanes, lanes), lambda i: (i, 0, 0)),
        out_shape=jax.ShapeDtypeStruct((heads, 5 * lanes, lanes), f32),
        compiler_params=params(),
        cost_estimate=cost(heads * 3e6, 4e6),
        name="bias_rows",
    )(table)


def ready_kernel(meta_ref, attn_ref, ffin_ref, ffout_ref, tokens_ref, ids_ref, gain_ref, *outs):
    attn_out, attn_send, gu_out, gu_send, row_out = outs
    core = meta_ref[0]
    first = core == 0
    width = tokens_ref.shape[1]
    half = width // 2
    low = attn_ref[...].astype(bf16)
    left, right = low[..., :half], low[..., half:]
    attn_out[0:3, core] = jnp.where(first, left[:3], right[:3])
    attn_send[...] = jnp.where(first, right[:3], left[:3])
    attn_out[3, 0] = left[3]
    attn_out[3, 1] = right[3]
    grain = ffin_ref.shape[2] // (2 * meta_ref.shape[0])
    for index in range(meta_ref.shape[0]):
        start = 2 * index * grain
        even = ffin_ref[:, :, start : start + grain].astype(bf16)
        odd = ffin_ref[:, :, start + grain : start + 2 * grain].astype(bf16)
        cols = slice(index * grain, (index + 1) * grain)
        gu_out[:, core, :, cols] = jnp.where(first, even, odd)
        gu_send[:, :, cols] = jnp.where(first, odd, even)
    tok = tokens_ref.shape[0]
    tokens = tokens_ref[...]
    row_out[:tok, :] = (tokens * rms_scale(tokens) * gain_ref[0:1, :]).astype(bf16)
    ids = jnp.broadcast_to(ids_ref[...].astype(f32), (16, tok))
    ids = jnp.concatenate([ids, jnp.zeros((16, width - tok), f32)], axis=1)
    row_out[tok : tok + 16, :] = ids.astype(bf16)
    row_out[tok + 16 :, :] = ffout_ref[...].astype(bf16)


def make_ready(core, attention_weight, ffin_weight, ffout_weight, tokens, ids, gain, chips):
    tok, width = tokens.shape
    rows, half, hidden = attention_weight.shape[1], width // 2, ffin_weight.shape[2]
    return pl.pallas_call(
        ready_kernel,
        in_specs=[smem_spec()] + [whole_spec()] * 6,
        out_specs=[whole_spec()] * 5,
        out_shape=[
            shaped(bf16, 4, 2, rows, half),
            shaped(bf16, 3, rows, half),
            shaped(bf16, 2, 2, rows, hidden // 2),
            shaped(bf16, 2, rows, hidden // 2),
            shaped(bf16, tok + 16 + ffout_weight.shape[0], width),
        ],
        compiler_params=params(),
        cost_estimate=cost(1e6, 2e6),
        name="make_ready",
    )(jnp.broadcast_to(core, (chips,)), attention_weight, ffin_weight, ffout_weight, tokens, ids, gain)


def fill_kernel(core_ref, kept_ref, arrived_ref, out_ref):
    count = arrived_ref.shape[0]
    out_ref[...] = kept_ref[...]
    out_ref[0:count, 1 - core_ref[0]] = arrived_ref[...]


def fill(core, kept, arrived):
    return pl.pallas_call(
        fill_kernel,
        in_specs=[smem_spec(), whole_spec(), whole_spec()],
        out_specs=whole_spec(),
        out_shape=shaped(bf16, *kept.shape),
        compiler_params=params(),
        cost_estimate=cost(0, 1e6),
        name="fill",
    )(core.reshape(1), kept, arrived)


def row_block(meta_ref, slot, rows):
    start = meta_ref[slot] * rows
    return pl.ds(pl.multiple_of(start, 16) if rows % 16 == 0 else start, rows)


def run_copies(pairs, sem):
    copies = [pltpu.make_async_copy(a, b, sem.at[i]) for i, (a, b) in enumerate(pairs)]
    for copy in copies:
        copy.start()
    return copies


def wait_all(copies):
    for copy in copies:
        copy.wait()


def whole_spec():
    return pl.BlockSpec(memory_space=pltpu.VMEM)


def smem_spec():
    return pl.BlockSpec(memory_space=pltpu.SMEM)


def dma(count):
    return pltpu.SemaphoreType.DMA((count,))


def shaped(kind, *shape):
    return jax.ShapeDtypeStruct(shape, kind)


def rows_kernel(meta_ref, near_ref, far_ref, full_ref, turned_ref, mask_ref):
    chips = near_ref.shape[0]
    core = meta_ref[chips]
    groups = lambda block: block[lanes : lanes + 16, :lanes].astype(f32)[:1, :]
    mine, other = groups(near_ref[0]), groups(far_ref[0])
    chip_ids = jnp.where(
        core == 0,
        jnp.concatenate([mine, other], axis=1),
        jnp.concatenate([other, mine], axis=1),
    )
    for source, side in ((near_ref, core), (far_ref, 1 - core)):
        for step in range(chips):
            block = source[step]
            start = (meta_ref[step] * 2 + side) * lanes
            place = pl.ds(pl.multiple_of(start, lanes), lanes)
            normed = block[:lanes, :]
            full_ref[place, :] = normed
            turned_ref[:, place] = normed.T
            wide = jnp.broadcast_to(groups(block), (lanes, lanes)).T
            same = jnp.concatenate([wide, wide], axis=1) == chip_ids
            mask_ref[place, :] = jnp.where(same, 0.0, masked_score)


def place_rows(meta, near, far):
    chips, _, width = near.shape
    length = 2 * chips * lanes
    return pl.pallas_call(
        rows_kernel,
        in_specs=[smem_spec()] + [whole_spec()] * 2,
        out_specs=[whole_spec()] * 3,
        out_shape=[
            shaped(bf16, length, width),
            shaped(bf16, width, length),
            shaped(f32, length, 2 * lanes),
        ],
        compiler_params=params(),
        cost_estimate=cost(3e6, 8e6),
        name="place_rows",
    )(meta, near, far)


def one_head(matrix, half):
    first = lax.broadcasted_iota(jnp.int32, matrix.shape, 1) < matrix.shape[1] // 2
    return jnp.where(first if half == 0 else jnp.logical_not(first), matrix, jnp.zeros_like(matrix))


def band_place(block, chip, part):
    kind = jnp.clip(block - (2 * chip + part) + 2, 0, 4)
    return pl.ds(pl.multiple_of(kind * lanes, lanes), lanes)


def attend_kernel(count, meta_ref, rows_ref, mask_ref, bias_ref, *refs):
    pieces = refs[:count]
    q_ref, k_ref, v_ref, p_ref, o_ref, low_ref, out_rows = refs[count : count + 7]
    weight, score, soft, sem, out_sem = refs[count + 7 :]
    pair = pl.program_id(0)
    chip = meta_ref[0]
    length = rows_ref.shape[0]
    blocks = length // lanes
    group = 2 * lanes
    stacked = [(piece.at[3], out_rows.at[step]) for step, piece in enumerate(pieces)]

    @pl.when(pair == 0)
    def _():
        loads = run_copies(load_pairs(pieces, meta_ref, 0, weight), sem)
        run_copies(stacked, out_sem)
        wait_all(loads)

    cols = pl.ds(pl.multiple_of(pair * lanes, lanes), lanes)
    own = rows_ref[pl.ds(pl.multiple_of(chip * group, group), group), :]
    query = mm(own, weight[0, :, cols]).astype(bf16)
    both = jnp.concatenate([weight[1, :, cols], weight[2, :, cols]], axis=1)
    key_value = mm(rows_ref[...], both).astype(bf16)
    key, value = key_value[:, :lanes], key_value[:, lanes:]
    q_ref[...] = query
    k_ref[...] = key
    v_ref[...] = value
    score[...] = mm_nt(key, jnp.concatenate([one_head(query, half) for half in range(2)], axis=0))
    for half in range(2):
        lane = slice(half * group, (half + 1) * group)
        best = jnp.full((8, group), masked_score, f32)
        for block in range(blocks):
            rows = slice(block * lanes, (block + 1) * lanes)
            bias = [bias_ref[half, band_place(block, chip, part), :] for part in range(2)]
            now = score[rows, lane] + jnp.concatenate(bias, axis=1) + mask_ref[rows, :]
            score[rows, lane] = now
            best = jnp.maximum(best, jnp.max(now.reshape(lanes // 8, 8, group), axis=0))
        top = jnp.max(best, axis=0, keepdims=True)
        total = jnp.zeros((8, group), f32)
        for block in range(blocks):
            rows = slice(block * lanes, (block + 1) * lanes)
            now = jnp.exp(score[rows, lane] - top)
            score[rows, lane] = now
            total = total + jnp.sum(now.reshape(lanes // 8, 8, group), axis=0)
        inverse = 1.0 / jnp.sum(total, axis=0, keepdims=True)
        for block in range(blocks):
            rows = slice(block * lanes, (block + 1) * lanes)
            now = score[rows, lane] * inverse
            p_ref[half, rows, :] = now
            soft[rows, lane] = now.astype(bf16)
    features = lanes // 2
    both_turned = mm_tn(value, soft[...])
    turned = [both_turned[:features, :group], both_turned[features:, group:]]
    attended = jnp.concatenate(turned, axis=0).T
    o_ref[...] = attended
    low_ref[...] = attended.astype(bf16)

    @pl.when(pair == pl.num_programs(0) - 1)
    def _():
        wait_all([pltpu.make_async_copy(a, b, out_sem.at[i]) for i, (a, b) in enumerate(stacked)])


def attend(pieces, meta, rows, mask, bias):
    length, width = rows.shape
    half = width // 2
    group = 2 * lanes
    pairs = half // lanes
    col = lambda i, *_: (0, i)
    fixed = lambda i, *_: (0, 0)
    flops = 2 * (group * width * half + 2 * length * width * half + 4 * group * length * half)
    return pl.pallas_call(
        functools.partial(attend_kernel, len(pieces)),
        grid_spec=pltpu.PrefetchScalarGridSpec(
            num_scalar_prefetch=1,
            grid=(pairs,),
            in_specs=[
                pl.BlockSpec((length, width), fixed),
                pl.BlockSpec((length, group), fixed),
                pl.BlockSpec((2, 5 * lanes, lanes), lambda i, *_: (i, 0, 0)),
            ]
            + [any_spec()] * len(pieces),
            out_specs=[
                pl.BlockSpec((group, lanes), col),
                pl.BlockSpec((length, lanes), col),
                pl.BlockSpec((length, lanes), col),
                pl.BlockSpec((2, length, group), lambda i, *_: (i, 0, 0)),
                pl.BlockSpec((group, lanes), col),
                pl.BlockSpec((group, lanes), col),
                pl.BlockSpec((len(pieces),) + pieces[0].shape[1:], lambda i, *_: (0, 0, 0)),
            ],
            scratch_shapes=[
                pltpu.VMEM((3, width, half), bf16),
                pltpu.VMEM((length, 2 * group), f32),
                pltpu.VMEM((length, 2 * group), bf16),
                dma(len(pieces)),
                dma(len(pieces)),
            ],
        ),
        out_shape=[
            shaped(bf16, group, half),
            shaped(bf16, length, half),
            shaped(bf16, length, half),
            shaped(f32, 2 * pairs, length, group),
            shaped(f32, group, half),
            shaped(bf16, group, half),
            shaped(bf16, len(pieces), *pieces[0].shape[1:]),
        ],
        compiler_params=params(),
        cost_estimate=cost(flops, 30e6, 2 * group * length * pairs),
        name="attend",
    )(meta, rows, mask, bias, *pieces)


def mix_kernel(
    meta_ref, tokens_ref, own_ref, their_ref, gain_ref, near_ref, far_ref, mixed_ref, normed_ref, turned_ref, joined_ref, weight_ref, held, sem
):
    chips, rows, half = near_ref.shape
    rows = rows // 2
    pairs = []
    for index, source in enumerate((near_ref, far_ref)):
        for step in range(chips):
            place = row_block(meta_ref, 1 + index * chips + step, rows)
            for side in range(2):
                pairs.append(
                    (
                        source.at[step, side * rows : (side + 1) * rows, :],
                        weight_ref.at[place, side * half : (side + 1) * half],
                    )
                )
    copies = run_copies(pairs, sem)
    first = meta_ref[0] == 0
    held[:, :half] = jnp.where(first, own_ref[...], their_ref[...])
    held[:, half:] = jnp.where(first, their_ref[...], own_ref[...])
    joined_ref[...] = held[...].T
    wait_all(copies)
    mixed = tokens_ref[...] + mm(held[...], weight_ref[...])
    mixed_ref[...] = mixed
    normed = (mixed * rms_scale(mixed) * gain_ref[...]).astype(bf16)
    normed_ref[...] = normed
    turned_ref[...] = normed.T


def mix(meta, tokens, own, their, gain, near, far):
    group, half = own.shape
    width = 2 * half
    return pl.pallas_call(
        mix_kernel,
        in_specs=[smem_spec()] + [whole_spec()] * 4 + [any_spec()] * 2,
        out_specs=[whole_spec()] * 5,
        out_shape=[
            shaped(f32, group, width),
            shaped(bf16, group, width),
            shaped(bf16, width, group),
            shaped(bf16, width, group),
            shaped(bf16, width, width),
        ],
        scratch_shapes=[pltpu.VMEM((group, width), bf16), dma(4 * near.shape[0])],
        compiler_params=params(),
        cost_estimate=cost(4 * group * width * half, 4e6),
        name="mix",
    )(meta, tokens, own, their, gain, near, far)


def feed_kernel(
    chips,
    places,
    gu_count,
    meta_ref,
    normed_low,
    turned_low,
    cot_ref,
    *refs,
):
    refs = list(refs)
    take = lambda n: [refs.pop(0) for _ in range(n)]
    gu_pieces = take(gu_count)
    down_pieces = take(places)
    out_ref, back_ref = take(2)
    gu_outs, down_outs = take(chips), take(2)
    gu, down, grad_gu, grad_down, cot_low = take(5)
    gu_sem, down_sem, gu_out_sem, down_out_sem = take(4)
    step = pl.program_id(0)
    steps = pl.num_programs(0)
    block = 512

    count = gu.shape[2] // block

    def gu_loads(turn):
        columns = pl.ds(pl.multiple_of(turn * block, block), block)
        pairs = []
        for index, piece in enumerate(gu_pieces):
            place = row_block(meta_ref, min(index, chips - 1), piece.shape[1])
            lead = slice(0, 2) if piece.shape[0] == 2 else slice(index - 3, index - 2)
            pairs.append((piece.at[:, :, columns], gu.at[lead, place, columns]))
        return [
            pltpu.make_async_copy(a, b, gu_sem.at[turn, index]) for index, (a, b) in enumerate(pairs)
        ]

    def gu_stores(turn):
        columns = pl.ds(pl.multiple_of(turn * block, block), block)
        copies = []
        for chip, out in enumerate(gu_outs):
            source = grad_gu.at[:, row_block(meta_ref, chip, out.shape[1]), columns]
            copies.append(pltpu.make_async_copy(source, out.at[:, :, columns], gu_out_sem.at[turn, chip]))
        return copies

    @pl.when(step == 0)
    def _():
        for copy in gu_loads(0):
            copy.start()
        pairs = []
        slot = chips
        for piece in down_pieces:
            for chip in range(chips):
                pairs.append((piece.at[chip], down.at[row_block(meta_ref, slot, piece.shape[1]), :]))
                slot += 1
        down_copies = run_copies(pairs, down_sem)
        for turn in range(1, count):
            for copy in gu_loads(turn):
                copy.start()
        cot_low[...] = cot_ref[...].astype(bf16)
        out_ref[...] = jnp.zeros_like(out_ref)
        back_ref[...] = jnp.zeros_like(back_ref)
        wait_all(down_copies)

    for copy in gu_loads(step):
        copy.wait()
    cols = pl.ds(pl.multiple_of(step * block, block), block)
    normed = normed_low[...]
    cot = cot_low[...]
    gate_w, up_w, down_w = gu[0, :, cols], gu[1, :, cols], down[cols, :]
    gate, up = mm(normed, gate_w), mm(normed, up_w)
    square = gate * gate
    curve = jnp.tanh(gelu_scale * gate * (1.0 + gelu_cubic * square))
    half = 0.5 * (1.0 + curve)
    gelu = gate * half
    slope = half + 0.5 * gate * (1.0 - curve * curve) * gelu_scale * (1.0 + 3.0 * gelu_cubic * square)
    hidden = (gelu * up).astype(bf16)
    dh = mm_nt(cot, down_w)
    dgate = (dh * up * slope).astype(bf16)
    dup = (dh * gelu).astype(bf16)
    out_ref[...] += mm(hidden, down_w)
    back_ref[...] += mm_nt(dgate, gate_w) + mm_nt(dup, up_w)
    grad_down[cols, :] = mm_tn(hidden, cot).astype(bf16)
    both = mm(turned_low[...], jnp.concatenate([dgate, dup], axis=1)).astype(bf16)
    grad_gu[0, :, cols] = both[:, :block]
    grad_gu[1, :, cols] = both[:, block:]

    for copy in gu_stores(step):
        copy.start()

    @pl.when(step == steps - 1)
    def _():
        pairs = []
        for turn, out in enumerate(down_outs):
            for spot in range(places // 2):
                for chip in range(chips):
                    slot = chips * (1 + places + turn * (places // 2) + spot) + chip
                    place = row_block(meta_ref, slot, out.shape[2])
                    pairs.append((grad_down.at[place, :], out.at[spot, chip]))
        down_copies = run_copies(pairs, down_out_sem)
        for turn in range(count):
            wait_all(gu_stores(turn))
        wait_all(down_copies)


def feed(gu_pieces, down_pieces, meta, normed, turned, cot, chips, places):
    group, width = normed.shape
    hidden = gu_pieces[0].shape[2]
    block = 512
    fixed = lambda i, *_: (0, 0)
    full = lambda *shape: pl.BlockSpec(shape, fixed)
    flops = 2 * 9 * group * width * hidden
    results = pl.pallas_call(
        functools.partial(feed_kernel, chips, places, len(gu_pieces)),
        grid_spec=pltpu.PrefetchScalarGridSpec(
            num_scalar_prefetch=1,
            grid=(hidden // block,),
            in_specs=[full(group, width), full(width, group), full(group, width)]
            + [any_spec()] * (len(gu_pieces) + places),
            out_specs=[full(group, width)] * 2 + [any_spec()] * (chips + 2),
            scratch_shapes=[
                pltpu.VMEM((2, width, hidden), bf16),
                pltpu.VMEM((hidden, width), bf16),
                pltpu.VMEM((2, width, hidden), bf16),
                pltpu.VMEM((hidden, width), bf16),
                pltpu.VMEM((group, width), bf16),
                pltpu.SemaphoreType.DMA((hidden // block, len(gu_pieces))),
                dma(chips * places),
                pltpu.SemaphoreType.DMA((hidden // block, chips)),
                dma(chips * places),
            ],
        ),
        out_shape=[shaped(f32, group, width)] * 2
        + [shaped(bf16, 2, width // chips, hidden)] * chips
        + [shaped(bf16, places // 2, chips, hidden // (chips * places), width)] * 2,
        compiler_params=params(),
        cost_estimate=cost(flops, 25e6, group * hidden),
        name="feed",
    )(meta, normed, turned, cot, *gu_pieces, *down_pieces)
    return results[:2], results[2 : 2 + chips], results[2 + chips :]


def settle_kernel(
    meta_ref,
    mixed_ref,
    cot_ref,
    back_ref,
    arrived_ref,
    weight_ref,
    gain_ref,
    dmixed_ref,
    do_ref,
    gain_grad_ref,
    branch_ref,
):
    core = meta_ref[0]
    half = do_ref.shape[1]
    mixed = mixed_ref[...]
    scale = rms_scale(mixed)
    dn2 = back_ref[...] + arrived_ref[...]
    gained = dn2 * gain_ref[...]
    inner = jnp.mean(gained * mixed, axis=-1, keepdims=True)
    dmixed = cot_ref[...] + scale * gained - mixed * (scale * scale * scale * inner)
    dmixed_ref[...] = dmixed
    gain_grad_ref[...] = 0.5 * jnp.sum(dn2 * mixed * scale, axis=0, keepdims=True)
    branch = dmixed.astype(bf16)
    branch_ref[...] = branch
    mine = weight_ref[pl.ds(pl.multiple_of(core * half, half), half), :]
    do_ref[...] = mm_nt(branch, mine).astype(bf16)


def settle(meta, mixed, cot, back, arrived, weight, gain):
    group, width = mixed.shape
    half = width // 2
    return pl.pallas_call(
        settle_kernel,
        in_specs=[smem_spec()] + [whole_spec()] * 6,
        out_specs=[whole_spec()] * 4,
        out_shape=[
            shaped(f32, group, width),
            shaped(bf16, group, half),
            shaped(f32, 1, width),
            shaped(bf16, group, width),
        ],
        compiler_params=params(),
        cost_estimate=cost(2 * group * width * half, 6e6),
        name="settle",
    )(meta, mixed, cot, back, arrived, weight, gain)


def band_rows(band_ref):
    line = lax.broadcasted_iota(jnp.int32, (8, 2 * lanes), 0)
    none = jnp.zeros((8, lanes), f32)
    found = []
    for block in range(3):
        summed = jnp.zeros((8, 2 * lanes), f32)
        for part in range(lanes // 8):
            start = lanes * (block + 1) + 8 * part
            wide = jnp.concatenate([band_ref[start : start + 8, :], none], axis=1)
            move = lanes - 8 - 8 * part
            summed = summed + (pltpu.roll(wide, move, 1) if move else wide)
        for bit in range(3):
            step = 1 << bit
            summed = jnp.where((line & step) == 0, pltpu.roll(summed, step, 1), summed)
        found.append(jnp.sum(summed, axis=0, keepdims=True))
    return jnp.concatenate(found, axis=1)


def retreat_kernel(meta_ref, do_ref, o_ref, q_ref, k_ref, v_ref, p_ref, dq_ref, dkv_ref, bias_ref, low, soft_low, spread_of, band_ref, onehot):
    chip = meta_ref[0]
    blocks = k_ref.shape[0] // lanes
    group = 2 * lanes
    features = lanes // 2
    do = do_ref[...]
    spread = (do.astype(f32) * o_ref[...]).T
    band_ref[...] = jnp.zeros_like(band_ref)
    far = jnp.zeros((8, lanes), f32)
    rows_of = []

    @pl.when(pl.program_id(0) == 0)
    def _():
        bucket = lax.broadcasted_iota(jnp.int32, (6 * lanes, lanes), 1)
        spot = lax.broadcasted_iota(jnp.int32, (6 * lanes, lanes), 0)
        offset = lanes * (spot // (2 * lanes)) - 1 - spot % (2 * lanes)
        onehot[...] = (bucket_of(offset) == bucket).astype(f32)

    do_two = jnp.concatenate([one_head(do, half) for half in range(2)], axis=0)
    query_two = jnp.concatenate([one_head(q_ref[...], half) for half in range(2)], axis=0)
    spread_of[...] = mm_nt(v_ref[...], do_two)
    for half in range(2):
        lane = slice(half * group, (half + 1) * group)
        delta = jnp.sum(spread[half * features : (half + 1) * features], axis=0, keepdims=True)
        for block in range(blocks):
            rows = slice(block * lanes, (block + 1) * lanes)
            soft = p_ref[half, rows, :]
            ds = soft * (spread_of[rows, lane] - delta)
            for part in range(2):
                place = band_place(block, chip, part)
                band_ref[place, :] += ds[:, part * lanes : (part + 1) * lanes]
            low[rows, lane] = ds.astype(bf16)
            soft_low[rows, lane] = soft.astype(bf16)
        rows_of.append(band_rows(band_ref))
        low_sum = jnp.sum(band_ref[0:lanes, :])
        high_sum = jnp.sum(band_ref[4 * lanes : 5 * lanes, :])
        lane_id = lax.broadcasted_iota(jnp.int32, (8, lanes), 1)
        line = lax.broadcasted_iota(jnp.int32, (8, lanes), 0)
        far = far + jnp.where((lane_id == 15) & (line == half), low_sum, 0.0)
        far = far + jnp.where((lane_id == 31) & (line == half), high_sum, 0.0)
        if half == 0:
            band_ref[...] = jnp.zeros_like(band_ref)
    dkv_ref[:, :lanes] = mm(low[...], query_two).astype(bf16)
    dkv_ref[:, lanes:] = mm(soft_low[...], do_two).astype(bf16)
    both_turned = mm_tn(k_ref[...], low[...])
    turned = [both_turned[:features, :group], both_turned[features:, group:]]
    dq_ref[...] = jnp.concatenate(turned, axis=0).T.astype(bf16)
    rows_of.append(jnp.zeros((6, rows_of[0].shape[1]), f32))
    near = lax.dot_general(
        jnp.concatenate(rows_of, axis=0),
        onehot[...],
        (((1,), (0,)), ((), ())),
        precision=lax.Precision.HIGHEST,
        preferred_element_type=f32,
    )
    bias_ref[0] = near + far


def retreat(meta, do, o, q, k, v, p):
    length, half = k.shape
    group = do.shape[0]
    pairs = half // lanes
    col = lambda i, *_: (0, i)
    deep = lambda i, *_: (i, 0, 0)
    flops = 2 * 8 * group * length * half
    return pl.pallas_call(
        retreat_kernel,
        grid_spec=pltpu.PrefetchScalarGridSpec(
            num_scalar_prefetch=1,
            grid=(pairs,),
            in_specs=[
                pl.BlockSpec((group, lanes), col),
                pl.BlockSpec((group, lanes), col),
                pl.BlockSpec((group, lanes), col),
                pl.BlockSpec((length, lanes), col),
                pl.BlockSpec((length, lanes), col),
                pl.BlockSpec((2, length, group), deep),
            ],
            out_specs=[
                pl.BlockSpec((group, lanes), col),
                pl.BlockSpec((length, 2 * lanes), col),
                pl.BlockSpec((1, 8, lanes), deep),
            ],
            scratch_shapes=[
                pltpu.VMEM((length, 2 * group), bf16),
                pltpu.VMEM((length, 2 * group), bf16),
                pltpu.VMEM((length, 2 * group), f32),
                pltpu.VMEM((5 * lanes, lanes), f32),
                pltpu.VMEM((6 * lanes, lanes), f32),
            ],
        ),
        out_shape=[
            shaped(bf16, group, half),
            shaped(bf16, length, 2 * half),
            shaped(f32, pairs, 8, lanes),
        ],
        compiler_params=params(),
        cost_estimate=cost(flops, 20e6),
        name="retreat",
    )(meta, do, o, q, k, v, p)


small_rows = 16


def load_pairs(pieces, meta_ref, first, weight):
    pairs = []
    for step, piece in enumerate(pieces):
        place = row_block(meta_ref, first + step, piece.shape[1])
        pairs.append((piece.at[0:3], weight.at[:, place, :]))
    return pairs


def grads_kernel(
    chips, meta_ref, turned_ref, dq_ref, dkv_ref, gains_ref, second_ref, bias_ref, joined_ref, branch_ref, *refs
):
    refs = list(refs)
    take = lambda n: [refs.pop(0) for _ in range(n)]
    pieces, outs = take(chips), take(chips)
    weight, grad, wo, small, sem, out_sem = take(6)
    chip, core = meta_ref[0], meta_ref[1]
    width = turned_ref.shape[0]
    half = width // 2
    group = dq_ref.shape[0]
    loads = run_copies(load_pairs(pieces, meta_ref, 2, weight), sem)
    wo_rows = wo.shape[1]
    mine = []
    for index in range(chips):
        even = joined_ref[2 * index * wo_rows : (2 * index + 1) * wo_rows, :]
        odd = joined_ref[(2 * index + 1) * wo_rows : (2 * index + 2) * wo_rows, :]
        mine.append(jnp.where(core == 0, even, odd))
    out_grad = mm(jnp.concatenate(mine, axis=0), branch_ref[...]).astype(bf16)
    for index in range(chips):
        wo[index] = out_grad[index * wo_rows : (index + 1) * wo_rows]
    own_rows = pl.ds(pl.multiple_of(chip * group, group), group)
    query_grad = mm(turned_ref[:, own_rows], dq_ref[...])
    grad[0] = query_grad.astype(bf16)
    wait_all(loads)
    along_row = [query_grad[:, at : at + lanes] * weight[0, :, at : at + lanes].astype(f32) for at in range(0, half, lanes)]
    along_row = sum(along_row[1:], along_row[0])
    for pair in range(half // lanes):
        wide = slice(pair * 2 * lanes, (pair + 1) * 2 * lanes)
        cols = slice(pair * lanes, (pair + 1) * lanes)
        summed = mm(turned_ref[...], dkv_ref[:, wide])
        low = summed.astype(bf16)
        grad[1, :, cols] = low[:, :lanes]
        grad[2, :, cols] = low[:, lanes:]
        along_row = along_row + summed[:, :lanes] * weight[1, :, cols].astype(f32)
        along_row = along_row + summed[:, lanes:] * weight[2, :, cols].astype(f32)
    first_gain = jnp.sum(along_row.T, axis=0, keepdims=True) / gains_ref[...]
    second_gain = second_ref[...]
    lines = [first_gain[:, :half], first_gain[:, half:], second_gain[:, :half], second_gain[:, half:]]
    for pair in range(bias_ref.shape[0]):
        both = [bias_ref[pair, 0:1, :], bias_ref[pair, 1:2, :]]
        both.append(jnp.zeros((1, half - 2 * lanes), f32))
        lines.append(jnp.concatenate(both, axis=1))
    lines.append(jnp.zeros((small_rows - len(lines), half), f32))
    small[...] = jnp.concatenate(lines, axis=0).astype(bf16)
    rows = width // chips
    side_rows = rows // 2
    pairs = []
    for step, out in enumerate(outs):
        place = row_block(meta_ref, 2 + step, rows)
        at = 0
        for matrix in range(3):
            pairs.append((grad.at[matrix, place, :], out.at[at : at + rows, :]))
            at += rows
        for side in range(2):
            source = wo.at[meta_ref[2 + step], :, side * half : (side + 1) * half]
            pairs.append((source, out.at[at : at + side_rows, :]))
            at += side_rows
        pairs.append((small, out.at[at : at + small_rows, :]))
    wait_all(run_copies(pairs, out_sem))


def weight_grads(pieces, meta, turned, dq, dkv, gain, second, bias, joined, branch, chips):
    width, length = turned.shape
    half = width // 2
    group = dq.shape[0]
    flops = 2 * (2 * length * width * half + group * width * half)
    block = width // chips
    return pl.pallas_call(
        functools.partial(grads_kernel, chips),
        in_specs=[smem_spec()] + [whole_spec()] * 8 + [any_spec()] * len(pieces),
        out_specs=[any_spec()] * chips,
        out_shape=[shaped(bf16, 4 * block + small_rows, half)] * chips,
        scratch_shapes=[
            pltpu.VMEM((3, width, half), bf16),
            pltpu.VMEM((3, width, half), bf16),
            pltpu.VMEM((chips, block // 2, width), bf16),
            pltpu.VMEM((small_rows, half), bf16),
            dma(chips),
            dma(6 * chips),
        ],
        compiler_params=params(),
        cost_estimate=cost(flops, 12e6),
        name="weight_grads",
    )(meta, turned, dq, dkv, gain, second, bias, joined, branch, *pieces)


def back_kernel(chips, meta_ref, dq_ref, dkv_ref, *refs):
    refs = list(refs)
    take = lambda n: [refs.pop(0) for _ in range(n)]
    pieces = take(chips)
    near_out, far_out = take(2)
    weight, both, back, sem = take(4)
    chip, core = meta_ref[0], meta_ref[1]
    length = dkv_ref.shape[0]
    half = dq_ref.shape[1]
    group = dq_ref.shape[0]
    wait_all(run_copies(load_pairs(pieces, meta_ref, 2, weight), sem))
    for pair in range(half // lanes):
        wide = pair * 2 * lanes
        cols = slice(pair * lanes, (pair + 1) * lanes)
        both[:, wide : wide + lanes] = weight[1, :, cols]
        both[:, wide + lanes : wide + 2 * lanes] = weight[2, :, cols]
    for start in range(0, length, group):
        back[start : start + group, :] = mm_nt(dkv_ref[start : start + group, :], both[...])
    own_rows = pl.ds(pl.multiple_of(chip * group, group), group)
    back[own_rows, :] += mm_nt(dq_ref[...], weight[0])
    for index, step in enumerate(bit_reversed(chips)):
        for side, out in ((core, near_out), (1 - core, far_out)):
            start = meta_ref[2 + step] * group + side * lanes
            out[index] = back[pl.ds(pl.multiple_of(start, lanes), lanes), :].astype(bf16)


def row_grads(pieces, meta, dq, dkv, chips):
    length, width = dkv.shape
    half = width // 2
    return pl.pallas_call(
        functools.partial(back_kernel, chips),
        in_specs=[smem_spec()] + [whole_spec()] * 2 + [any_spec()] * len(pieces),
        out_specs=[whole_spec()] * 2,
        out_shape=[shaped(bf16, chips, lanes, width)] * 2,
        scratch_shapes=[
            pltpu.VMEM((3, width, half), bf16),
            pltpu.VMEM((width, width), bf16),
            pltpu.VMEM((length, width), f32),
            dma(chips),
        ],
        compiler_params=params(),
        cost_estimate=cost(4 * length * width * half, 8e6),
        name="row_grads",
    )(meta, dq, dkv, *pieces)


def cut_kernel(side_ref, *refs):
    sources, (kept_ref, sent_ref) = refs[:-2], refs[-2:]
    count = kept_ref.shape[2]
    for index, out in ((side_ref[0], kept_ref), (1 - side_ref[0], sent_ref)):
        for part in range(2):
            start = pl.multiple_of((2 * part + index) * count, count)
            out[0, part] = total([source[0, pl.ds(start, count), :] for source in sources]).astype(bf16)


def cut_plane(blocks, side):
    lead, height, width = blocks[0].shape
    shape = (lead, 2, height // 4, width)
    row = lambda *shape: pl.BlockSpec((1,) + shape, lambda i: (i,) + (0,) * len(shape))
    return pl.pallas_call(
        cut_kernel,
        grid=(lead,),
        in_specs=[smem_spec()] + [row(height, width)] * len(blocks),
        out_specs=[row(*shape[1:])] * 2,
        out_shape=[shaped(bf16, *shape)] * 2,
        compiler_params=params(),
        cost_estimate=cost(1e6, 6e6),
        name="cut_plane",
    )(side.reshape(1), *blocks)


def sum_kernel(order_ref, *refs):
    places = order_ref.shape[0]
    sources, outs, total_ref = refs[: -1 - places], refs[-1 - places : -1], refs[-1]
    total_ref[...] = total([source[...] for source in sources])
    height = total_ref.shape[0] - small_rows
    rows = height // (8 * places)
    last = total_ref[height:, :]
    for turn, out in enumerate(outs):
        parts = []
        for block in range(8):
            start = block * places * rows + order_ref[turn] * rows
            parts.append(total_ref[pl.ds(pl.multiple_of(start, 8), rows), :])
        out[...] = jnp.concatenate(parts + [last], axis=0).astype(bf16)


def sum_plane(blocks, order):
    height, half = blocks[0].shape
    places = order.shape[0]
    rows = (height - small_rows) // (8 * places)
    if rows % 8:
        summed = total(blocks).astype(bf16)
        split, last = summed[:-small_rows].reshape(8, places, rows, half), summed[-small_rows:]
        pick = lambda turn: lax.dynamic_index_in_dim(split, order[turn], 1, keepdims=False)
        return [jnp.concatenate([pick(turn).reshape(-1, half), last], axis=0) for turn in range(places)]
    return pl.pallas_call(
        sum_kernel,
        in_specs=[smem_spec()] + [whole_spec()] * len(blocks),
        out_specs=[whole_spec()] * places,
        out_shape=[shaped(bf16, (height - small_rows) // places + small_rows, half)] * places,
        scratch_shapes=[pltpu.VMEM((height, half), f32)],
        compiler_params=params(),
        cost_estimate=cost(1e6, 4e6),
        name="sum_plane",
    )(order, *blocks)


def last_kernel(core_ref, *refs):
    sources, (sum_ref, sent_ref) = refs[:-2], refs[-2:]
    summed = total([source[...] for source in sources])
    sum_ref[...] = summed
    rows = (summed.shape[0] - small_rows) // 8
    first = core_ref[0] == 0
    block = lambda index: summed[index * rows : (index + 1) * rows]
    parts = [jnp.where(first, block(2 * matrix + 1), block(2 * matrix)) for matrix in range(3)]
    sent_ref[...] = jnp.concatenate(parts + [summed[8 * rows :]], axis=0)


def last_sum(core, arrived):
    height, half = arrived[0].shape
    rows = (height - small_rows) // 8
    return pl.pallas_call(
        last_kernel,
        in_specs=[smem_spec()] + [whole_spec()] * len(arrived),
        out_specs=[whole_spec()] * 2,
        out_shape=[shaped(f32, height, half), shaped(f32, 3 * rows + small_rows, half)],
        compiler_params=params(),
        cost_estimate=cost(1e6, 1e6),
        name="last_sum",
    )(core.reshape(1), *arrived)


def attention_kernel(
    rates, core_ref, sum_ref, arrived_ref, weight_ref, momentum_ref, average_ref, *outs
):
    new_weight, new_momentum, new_average, copy = outs
    rows, width = weight_ref.shape[1:]
    half = width // 2
    first = core_ref[0] == 0
    block = lambda index: sum_ref[index * rows : (index + 1) * rows, :]
    for matrix in range(4):
        left, right = block(2 * matrix), block(2 * matrix + 1)
        if matrix < 3:
            mine = jnp.where(first, left, right)
            theirs = arrived_ref[matrix * rows : (matrix + 1) * rows, :]
            left, right = jnp.where(first, mine, theirs), jnp.where(first, theirs, mine)
        for side, grad in enumerate((left, right)):
            at = (matrix, slice(None), slice(side * half, (side + 1) * half))
            values = update(
                weight_ref[at], grad, momentum_ref[at], average_ref[at], rates[matrix]
            )
            new_weight[at], new_momentum[at], new_average[at] = values
            copy[at] = values[0].astype(bf16)


def attention_update(core, summed, arrived, weight, momentum, average, rates):
    return pl.pallas_call(
        functools.partial(attention_kernel, rates),
        in_specs=[smem_spec()] + [whole_spec()] * 5,
        out_specs=[whole_spec()] * 4,
        out_shape=[shaped(f32, *weight.shape)] * 3 + [shaped(bf16, *weight.shape)],
        compiler_params=params(),
        cost_estimate=cost(1e6, 2e6),
        name="attention_update",
    )(core.reshape(1), summed, arrived, weight, momentum, average)


def core_swap(value):
    count = lax.axis_size("seq")
    return lax.ppermute(value, "seq", [(i, i ^ 1) for i in range(count)])


def plane_swap(value, step):
    count = lax.axis_size("seq")
    return lax.ppermute(value, "seq", [(i, i ^ (2 * step)) for i in range(count)])


def along(value, step):
    count = lax.axis_size("batch")
    return lax.ppermute(value, "batch", [(i, (i + step) % count) for i in range(count)])


def along_all(value):
    return [value] + [along(value, step) for step in range(1, lax.axis_size("batch"))]


def after(value, *earlier):
    return lax.optimization_barrier((value,) + earlier)[0]


def join_kernel(order_ref, *refs):
    sources, out = refs[:-1], refs[-1]
    for index, source in enumerate(sources):
        out[:, :, order_ref[index]] = source[...]


def join(blocks, order):
    lead, rest = blocks[0].shape[:2], blocks[0].shape[2:]
    return pl.pallas_call(
        join_kernel,
        in_specs=[smem_spec()] + [whole_spec()] * len(blocks),
        out_specs=whole_spec(),
        out_shape=shaped(bf16, *lead, len(blocks), *rest),
        compiler_params=params(),
        cost_estimate=cost(0, 2e6),
        name="join",
    )(order, *blocks)


def gather_plane(value):
    return [value] + [plane_swap(value, step) for step in range(1, lax.axis_size("seq") // 2)]


def total(blocks):
    summed = blocks[0].astype(f32)
    for block in blocks[1:]:
        summed = summed + block.astype(f32)
    return summed


def scatter_plane(blocks):
    return [blocks[0]] + [plane_swap(part, step) for step, part in enumerate(blocks) if step]


def bit_reversed(chips):
    order = [0]
    while len(order) < chips:
        order = [2 * step for step in order] + [2 * step + 1 for step in order]
    return order


def halves_along(value, dim, place):
    count = value.shape[dim] // 2
    split = value.reshape(value.shape[:dim] + (2, count) + value.shape[dim + 1 :])
    side = (place // count) % 2
    pick = lambda index: lax.dynamic_index_in_dim(split, index, dim, keepdims=False)
    return pick(side), pick(1 - side)


def across(value, step):
    count = lax.axis_size("batch")
    return lax.ppermute(value, "batch", [(i, i ^ step) for i in range(count)])


def halved(blocks, step):
    count = blocks.shape[0] // 2
    return blocks[:count], plane_swap(blocks[count:], step)


def summed_half(halves):
    return total(halves).astype(bf16)


def finished(halves, steps):
    for step in steps:
        halves = halved(summed_half(halves), step)
    return total(halves)[0]


def spread(values):
    return [values[0]] + [along(value, step) for step, value in enumerate(values) if step]


def spread_along(split, dim, place):
    count = lax.axis_size("batch")
    pick = lambda step: lax.dynamic_index_in_dim(split, (place + step) % count, dim, keepdims=False)
    return [pick(0)] + [along(pick(step), step) for step in range(1, count)]


def shards(
    tokens,
    cotangent,
    group_ids,
    attention_weight,
    ffin_weight,
    ffout_weight,
    bias_table,
    gains,
    attention_momentum,
    ffin_momentum,
    ffout_momentum,
    bias_momentum,
    gain_momentum,
    attention_average,
    ffin_average,
    ffout_average,
    bias_average,
    gain_average,
):
    _, tok, width = tokens.shape
    cycle_size, places = lax.axis_size("seq"), lax.axis_size("batch")
    cycle_index = lax.axis_index("seq").astype(jnp.int32)
    place = lax.axis_index("batch").astype(jnp.int32)
    chips = cycle_size // 2
    chip, core = cycle_index // 2, cycle_index % 2
    half = width // 2
    rows = attention_weight.shape[1]
    down_rows = ffout_weight.shape[0]
    hidden = ffin_weight.shape[2]
    grain = hidden // cycle_size
    heads = bias_table.shape[1]
    group = 2 * tok
    first_core = core == 0

    def by_core(mine, theirs):
        return [jnp.where(first_core, mine, theirs), jnp.where(first_core, theirs, mine)]

    steps = [chip ^ step for step in range(chips)]
    order = jnp.stack([(place + places - step) % places for step in range(places)])
    onward = jnp.stack([(place + step) % places for step in range(places)])
    flat_tokens, flat_cot = tokens.reshape(tok, width), cotangent.reshape(tok, width)

    attn_kept, attn_sent, gu_kept, gu_sent, row_block_own = make_ready(
        core,
        attention_weight,
        ffin_weight,
        ffout_weight,
        flat_tokens,
        group_ids,
        gains,
        chips,
    )
    their_tokens, their_cot = core_swap(flat_tokens), core_swap(flat_cot)
    attn_from, gu_from = core_swap(attn_sent), core_swap(gu_sent)
    row_block_own, attn_kept = lax.optimization_barrier((row_block_own, attn_kept, their_tokens, their_cot))[:2]
    attn_block = fill(core, after(attn_kept, gu_from), attn_from)
    gu_block = fill(core, gu_kept, gu_from)

    attn_blocks = along_all(attn_block)
    row_blocks, step = row_block_own[None], 1
    while step < chips:
        arrived = plane_swap(row_blocks, step)
        arrived = after(arrived, attn_block if step * 2 < chips else attn_blocks)
        row_blocks = jnp.concatenate([row_blocks, arrived], axis=0)
        step *= 2
    near_rows, down_block = row_blocks[:, : tok + 16], row_blocks[:, tok + 16 :]
    own_heads = jnp.where(first_core, bias_table[:, : heads // 2], bias_table[:, heads // 2 :])
    bias = bias_rows(after(own_heads, attn_block))

    attn_joined = join(after(attn_blocks, near_rows, bias, gu_block), order).reshape(4, 2 * places * rows, half)
    chip_tokens = jnp.concatenate(by_core(flat_tokens, their_tokens), axis=0)
    chip_cot = jnp.concatenate(by_core(flat_cot, their_cot), axis=0)
    far_rows = core_swap(after(near_rows, attn_joined))
    rows_full, turned, mask = place_rows(jnp.stack(steps + [core]), near_rows, far_rows)
    attn_pieces = gather_plane(attn_joined)
    gu_blocks = [after(gu_block, attn_joined)]
    for step in range(1, places):
        if step == 2:
            gu_blocks[-1], down_block = lax.optimization_barrier((gu_blocks[-1], down_block, rows_full))[:2]
        gu_blocks.append(along(gu_blocks[-1], 1))
    down_pieces = [down_block, along(down_block, 1)]
    gu_joined = join(gu_blocks, order)
    attn_pieces, rows_full, gu_joined, down_pieces = lax.optimization_barrier(
        (attn_pieces, rows_full, gu_joined, down_pieces)
    )
    chip_tokens, chip_cot, mask = lax.optimization_barrier((chip_tokens, chip_cot, mask))
    gu_joined, down_pieces, mask = lax.optimization_barrier((gu_joined, down_pieces, mask))
    down_pieces.append(along(down_pieces[-1], 1))
    gu_own = gu_joined.reshape(2, 2 * places * rows, hidden // 2)
    gu_pieces = [gu_own] + [plane_swap(gu_own, step) for step in range(1, 3 if chips == 4 else chips)]
    step_meta = jnp.stack(steps)
    query, key, value, soft, attended, attended_low, wo_near = attend(
        attn_pieces, step_meta, rows_full, mask, bias
    )
    wo_meta = jnp.stack([core] + [step * 2 + core for step in steps] + [step * 2 + 1 - core for step in steps])
    their_attended = core_swap(attended_low)
    their_attended, gu_pieces, down_pieces, wo_near = lax.optimization_barrier(
        (their_attended, gu_pieces, down_pieces, wo_near)
    )
    if chips == 4:
        passed = [gu_pieces[1][:1], gu_pieces[2][1:]]
        their_attended, passed, wo_near = lax.optimization_barrier((their_attended, passed, wo_near))
        gu_pieces += [plane_swap(passed[0], 2), plane_swap(passed[1], 1)]
    for _ in range(3, places):
        down_pieces.append(along(down_pieces[-1], 1))
    wo_far = core_swap(wo_near)
    mixed, second_low, second_turned, joined, out_weight = mix(
        wo_meta, chip_tokens, attended_low, their_attended, gains[1:2], wo_near, wo_far
    )
    down_meta = [step * places + order[index] for index in range(places) for step in steps]
    high = place // (places // 2)
    for side in (high, 1 - high):
        for spot in range(places // 2):
            down_meta += [step * places + side * (places // 2) + spot for step in steps]
    (out_part, back_part), gu_grads, down_grads = feed(
        gu_pieces, down_pieces, jnp.stack(steps + down_meta), second_low, second_turned, chip_cot, chips, places
    )
    add = lambda a, b: total([a, b]).astype(bf16)
    gu_arrived = scatter_plane(gu_grads)
    down_moving = across(down_grads[1], places // 2)
    their_back = core_swap(back_part)
    dmixed, attended_grad, second_gain, branch = settle(
        core.reshape(1), mixed, chip_cot, back_part, their_back, out_weight, gains[1:2]
    )
    dq, dkv, bias_part = retreat(chip.reshape(1), attended_grad, attended, query, key, value, soft)
    pair_meta = jnp.stack([chip, core] + steps)
    attn_grads = weight_grads(
        attn_pieces,
        pair_meta,
        turned,
        dq,
        dkv,
        gains[:1],
        second_gain,
        bias_part,
        joined,
        branch,
        chips,
    )

    near_back, far_back = row_grads(attn_pieces, pair_meta, after(dq, attn_grads), dkv, chips)
    mine = lambda value: lax.dynamic_slice_in_dim(value, core * tok, tok, 0)
    theirs = lambda value: lax.dynamic_slice_in_dim(value, (1 - core) * tok, tok, 0)
    back_arrived = core_swap(far_back)
    attn_grads, gu_arrived, down_moving = lax.optimization_barrier(
        (attn_grads, gu_arrived, down_moving, back_arrived)
    )[:3]
    attn_arrived = [attn_grads[0]] + [plane_swap(attn_grads[step], step) for step in range(1, min(chips, 3))]
    down_sum = add(down_moving, down_grads[0])
    reach = places // 2
    if rows * reach % 16 == 0:
        halves = cut_plane(gu_arrived, place // reach)
        gu_kept, gu_sent = [part.reshape(2, 2, reach, rows, hidden // 2) for part in halves]
    else:
        gu_sum = total(gu_arrived).astype(bf16).reshape(2, 2, places, rows, hidden // 2)
        gu_kept, gu_sent = halves_along(gu_sum, 2, place)
    gu_moving = across(gu_sent, reach)
    down_kept, down_sent = halves_along(down_sum, 0, place)
    down_moving = across(down_sent, reach // 2)
    attn_arrived += [plane_swap(attn_grads[step], step) for step in range(3, chips)]
    attn_arrived, gu_moving, down_moving, out_part = lax.optimization_barrier(
        (attn_arrived, gu_moving, down_moving, out_part)
    )
    their_out = core_swap(theirs(out_part))
    while reach > 2:
        gu_kept, gu_sent = halves_along(add(gu_kept, gu_moving), 2, place)
        reach //= 2
        gu_moving = across(gu_sent, reach)
        down_kept, down_sent = halves_along(add(down_kept, down_moving), 0, place)
        down_moving = across(down_sent, reach // 2)
    down_last = add(down_kept, down_moving)[0]
    gu_kept, gu_sent = halves_along(add(gu_kept, gu_moving), 2, place)
    attn_arrived, gu_sent, down_last = lax.optimization_barrier((attn_arrived, gu_sent, down_last))
    down_halves = halved(down_last, chips // 2)
    gu_moving = across(gu_sent, 1)
    gu_sum = total([gu_kept, gu_moving])[:, :, 0]
    layer_output = mine(mixed) + mine(out_part) + their_out
    pick = lambda value, first, dim: jnp.where(
        first, lax.index_in_dim(value, 0, dim, False), lax.index_in_dim(value, 1, dim, False)
    )
    gu_own = pick(gu_sum, first_core, 1)
    gu_their = core_swap(pick(gu_sum, core == 1, 1))
    attn_cuts = sum_plane(attn_arrived, onward)
    attn_sum = spread(attn_cuts)
    merged = total([near_back, back_arrived]).astype(bf16)
    later_steps = [chips // 2 >> turn for turn in range(1, chips.bit_length() - 1)]
    back_sum = summed_half(halved(after(merged, attn_cuts, gu_sum), 1))
    back_halves = halved(back_sum, 2)
    down_sum = after(summed_half(down_halves), back_sum)
    own_down = finished(halved(down_sum, later_steps[0]), later_steps[1:])

    weave = lambda parts: jnp.stack(
        [part.reshape(2, rows, chips, grain) for part in parts], axis=3
    ).reshape(2, rows, hidden)
    own_gu = weave(by_core(gu_own, gu_their))
    all_tokens = places * tok * cycle_size
    inverse_root = 1.0 / math.sqrt(all_tokens)
    ffin_new = update(ffin_weight, own_gu, ffin_momentum, ffin_average, ffin_rate * inverse_root)
    ffout_new = update(
        ffout_weight, own_down, ffout_momentum, ffout_average, ffout_rate * inverse_root
    )
    ffin_new += (ffin_new[0].astype(bf16),)
    ffout_new += (ffout_new[0].astype(bf16),)
    attn_sum, ffin_new = lax.optimization_barrier((attn_sum, ffin_new))
    summed, sent = last_sum(core, attn_sum)
    arrived = core_swap(sent)
    arrived = lax.optimization_barrier((arrived, back_sum))[0]
    attn_new = attention_update(
        core,
        summed,
        arrived,
        attention_weight,
        attention_momentum,
        attention_average,
        [rate * inverse_root for rate in attention_rates],
    )
    back_halves = after(back_halves, attn_new[0])
    first_grad = finished(back_halves, [2 << turn for turn in range(1, chips.bit_length() - 2)])
    scale = rms_scale(flat_tokens)
    gained = first_grad * gains[0]
    inner = jnp.mean(gained * flat_tokens, axis=-1, keepdims=True)
    input_grad = mine(dmixed) + scale * gained - flat_tokens * (scale**3 * inner)

    small_own, small_their = summed[-small_rows:], arrived[-small_rows:]
    gains_reduced = (small_own[:4] + small_their[:4]).reshape(gains.shape)
    pairs = heads // 4
    heads_of = lambda value: value[4 : 4 + pairs, : 2 * lanes].reshape(heads // 2, lanes)[:, : bias_table.shape[0]]
    bias_reduced = jnp.concatenate(by_core(heads_of(small_own), heads_of(small_their)), axis=0).T

    gain_rate = jnp.array(gain_rates, dtype=f32)[:, None] * inverse_root
    bias_new = update(bias_table, bias_reduced, bias_momentum, bias_average, bias_rate * inverse_root)
    gain_new = update(gains, gains_reduced, gain_momentum, gain_average, gain_rate)
    return (
        layer_output.reshape(tokens.shape),
        input_grad.reshape(tokens.shape),
        attn_new[0],
        ffin_new[0],
        ffout_new[0],
        bias_new[0],
        gain_new[0],
        attn_new[1],
        ffin_new[1],
        ffout_new[1],
        bias_new[1],
        gain_new[1],
        attn_new[2],
        ffin_new[2],
        ffout_new[2],
        bias_new[2],
        gain_new[2],
        attn_new[3],
        ffin_new[3],
        ffout_new[3],
    )


def solution(mesh):
    rows = P("batch", "seq", None)
    stacked = P(None, ("seq", "batch"), None)
    single = P(("seq", "batch"), None)
    weights = (stacked, stacked, single, P(), P())
    return jax.shard_map(
        shards,
        mesh=mesh,
        in_specs=(rows, rows, P("batch", "seq")) + weights * 3,
        out_specs=(rows, rows) + weights * 3 + (stacked, stacked, single),
        check_vma=False,
    )
```

```python
import functools
import math

import jax
import jax.numpy as jnp
from jax import lax
from jax.experimental import pallas as pl
from jax.experimental.pallas import tpu as pltpu
from jax.sharding import PartitionSpec as P

eps_norm = 1e-06
momentum_coef = 0.5
average_coef = 0.5
attention_rates = (0.0033, 0.0033, 0.025, 0.2)
ffin_rate = 0.063
ffout_rate = 0.023
bias_rate = 0.08
gain_rates = (0.045, 0.22)
thresholds = (12, 16, 23, 32, 46, 64, 91)
masked_score = -1e30
gelu_scale = math.sqrt(2.0 / math.pi)
gelu_cubic = 0.044715
bf16 = jnp.bfloat16
f32 = jnp.float32
vmem_bytes = 60 * 1024 * 1024
lanes = 128


def product(left, right, left_dim, right_dim):
    return lax.dot_general(
        left, right, (((left_dim,), (right_dim,)), ((), ())), preferred_element_type=f32
    )


def mm(left, right):
    return product(left, right, 1, 0)


def mm_nt(left, right):
    return product(left, right, 1, 1)


def mm_tn(left, right):
    return product(left, right, 0, 0)


def bucket_of(offset):
    magnitude = jnp.abs(offset)
    beyond = jnp.zeros_like(offset)
    for threshold in thresholds:
        beyond = beyond + (magnitude >= threshold).astype(jnp.int32)
    inside = jnp.where(magnitude < 8, magnitude, 8 + beyond)
    return inside + 16 * (offset > 0).astype(jnp.int32)


def update(weight, grad, momentum, average, rate):
    new_momentum = momentum_coef * momentum + grad
    new_weight = weight - rate * (grad + momentum_coef * new_momentum)
    new_average = average_coef * average + (1.0 - average_coef) * new_weight
    return (new_weight, new_momentum, new_average)


def rms_scale(values):
    return lax.rsqrt(jnp.mean(values * values, axis=-1, keepdims=True) + eps_norm)


def params():
    return pltpu.CompilerParams(vmem_limit_bytes=vmem_bytes)


def any_spec():
    return pl.BlockSpec(memory_space=pl.ANY)


def cost(flops, nbytes, exps=0):
    return pl.CostEstimate(flops=1, bytes_accessed=1, transcendentals=0)


def bias_kernel(table_ref, out_ref):
    head = pl.program_id(0)
    spot = lax.broadcasted_iota(jnp.int32, (8, 2 * lanes), 1)
    for block in range(3):
        buckets = bucket_of(lanes * (block - 1) + lanes - 1 - spot)
        row = jnp.zeros((8, 2 * lanes), f32)
        for bucket in range(table_ref.shape[0]):
            row = jnp.where(buckets == bucket, table_ref[bucket, head], row)
        wide = jnp.broadcast_to(row[:1], (lanes, 2 * lanes))
        rolled = pltpu.roll(wide, lanes + 1, 1, stride=1, stride_axis=0)
        out_ref[0, lanes * (block + 1) : lanes * (block + 2), :] = rolled[:, :lanes]
    out_ref[0, 0:lanes, :] = jnp.full((lanes, lanes), table_ref[15, head], f32)
    out_ref[0, 4 * lanes : 5 * lanes, :] = jnp.full((lanes, lanes), table_ref[31, head], f32)


def bias_rows(table):
    heads = table.shape[1]
    return pl.pallas_call(
        bias_kernel,
        grid=(heads,),
        in_specs=[pl.BlockSpec(memory_space=pltpu.SMEM)],
        out_specs=pl.BlockSpec((1, 5 * lanes, lanes), lambda i: (i, 0, 0)),
        out_shape=jax.ShapeDtypeStruct((heads, 5 * lanes, lanes), f32),
        compiler_params=params(),
        cost_estimate=cost(heads * 3e6, 4e6),
        name="bias_rows",
    )(table)


def ready_kernel(meta_ref, attn_ref, ffin_ref, ffout_ref, tokens_ref, ids_ref, gain_ref, *outs):
    attn_out, attn_send, gu_out, gu_send, row_out = outs
    core = meta_ref[0]
    first = core == 0
    width = tokens_ref.shape[1]
    half = width // 2
    low = attn_ref[...].astype(bf16)
    left, right = low[..., :half], low[..., half:]
    attn_out[0:3, core] = jnp.where(first, left[:3], right[:3])
    attn_send[...] = jnp.where(first, right[:3], left[:3])
    attn_out[3, 0] = left[3]
    attn_out[3, 1] = right[3]
    grain = ffin_ref.shape[2] // (2 * meta_ref.shape[0])
    for index in range(meta_ref.shape[0]):
        start = 2 * index * grain
        even = ffin_ref[:, :, start : start + grain].astype(bf16)
        odd = ffin_ref[:, :, start + grain : start + 2 * grain].astype(bf16)
        cols = slice(index * grain, (index + 1) * grain)
        gu_out[:, core, :, cols] = jnp.where(first, even, odd)
        gu_send[:, :, cols] = jnp.where(first, odd, even)
    tok = tokens_ref.shape[0]
    tokens = tokens_ref[...]
    row_out[:tok, :] = (tokens * rms_scale(tokens) * gain_ref[0:1, :]).astype(bf16)
    ids = jnp.broadcast_to(ids_ref[...].astype(f32), (16, tok))
    ids = jnp.concatenate([ids, jnp.zeros((16, width - tok), f32)], axis=1)
    row_out[tok : tok + 16, :] = ids.astype(bf16)
    row_out[tok + 16 :, :] = ffout_ref[...].astype(bf16)


def make_ready(core, attention_weight, ffin_weight, ffout_weight, tokens, ids, gain, chips):
    tok, width = tokens.shape
    rows, half, hidden = attention_weight.shape[1], width // 2, ffin_weight.shape[2]
    return pl.pallas_call(
        ready_kernel,
        in_specs=[smem_spec()] + [whole_spec()] * 6,
        out_specs=[whole_spec()] * 5,
        out_shape=[
            shaped(bf16, 4, 2, rows, half),
            shaped(bf16, 3, rows, half),
            shaped(bf16, 2, 2, rows, hidden // 2),
            shaped(bf16, 2, rows, hidden // 2),
            shaped(bf16, tok + 16 + ffout_weight.shape[0], width),
        ],
        compiler_params=params(),
        cost_estimate=cost(1e6, 2e6),
        name="make_ready",
    )(jnp.broadcast_to(core, (chips,)), attention_weight, ffin_weight, ffout_weight, tokens, ids, gain)


def fill_kernel(core_ref, kept_ref, arrived_ref, out_ref):
    count = arrived_ref.shape[0]
    out_ref[...] = kept_ref[...]
    out_ref[0:count, 1 - core_ref[0]] = arrived_ref[...]


def fill(core, kept, arrived):
    return pl.pallas_call(
        fill_kernel,
        in_specs=[smem_spec(), whole_spec(), whole_spec()],
        out_specs=whole_spec(),
        out_shape=shaped(bf16, *kept.shape),
        compiler_params=params(),
        cost_estimate=cost(0, 1e6),
        name="fill",
    )(core.reshape(1), kept, arrived)


def row_block(meta_ref, slot, rows):
    start = meta_ref[slot] * rows
    return pl.ds(pl.multiple_of(start, 16) if rows % 16 == 0 else start, rows)


def run_copies(pairs, sem):
    copies = [pltpu.make_async_copy(a, b, sem.at[i]) for i, (a, b) in enumerate(pairs)]
    for copy in copies:
        copy.start()
    return copies


def wait_all(copies):
    for copy in copies:
        copy.wait()


def whole_spec():
    return pl.BlockSpec(memory_space=pltpu.VMEM)


def smem_spec():
    return pl.BlockSpec(memory_space=pltpu.SMEM)


def dma(count):
    return pltpu.SemaphoreType.DMA((count,))


def shaped(kind, *shape):
    return jax.ShapeDtypeStruct(shape, kind)


def rows_kernel(meta_ref, near_ref, far_ref, full_ref, turned_ref, mask_ref):
    chips = near_ref.shape[0]
    core = meta_ref[chips]
    groups = lambda block: block[lanes : lanes + 16, :lanes].astype(f32)[:1, :]
    mine, other = groups(near_ref[0]), groups(far_ref[0])
    chip_ids = jnp.where(
        core == 0,
        jnp.concatenate([mine, other], axis=1),
        jnp.concatenate([other, mine], axis=1),
    )
    for source, side in ((near_ref, core), (far_ref, 1 - core)):
        for step in range(chips):
            block = source[step]
            start = (meta_ref[step] * 2 + side) * lanes
            place = pl.ds(pl.multiple_of(start, lanes), lanes)
            normed = block[:lanes, :]
            full_ref[place, :] = normed
            turned_ref[:, place] = normed.T
            wide = jnp.broadcast_to(groups(block), (lanes, lanes)).T
            same = jnp.concatenate([wide, wide], axis=1) == chip_ids
            mask_ref[place, :] = jnp.where(same, 0.0, masked_score)


def place_rows(meta, near, far):
    chips, _, width = near.shape
    length = 2 * chips * lanes
    return pl.pallas_call(
        rows_kernel,
        in_specs=[smem_spec()] + [whole_spec()] * 2,
        out_specs=[whole_spec()] * 3,
        out_shape=[
            shaped(bf16, length, width),
            shaped(bf16, width, length),
            shaped(f32, length, 2 * lanes),
        ],
        compiler_params=params(),
        cost_estimate=cost(3e6, 8e6),
        name="place_rows",
    )(meta, near, far)


def one_head(matrix, half):
    first = lax.broadcasted_iota(jnp.int32, matrix.shape, 1) < matrix.shape[1] // 2
    return jnp.where(first if half == 0 else jnp.logical_not(first), matrix, jnp.zeros_like(matrix))


def band_place(block, chip, part):
    kind = jnp.clip(block - (2 * chip + part) + 2, 0, 4)
    return pl.ds(pl.multiple_of(kind * lanes, lanes), lanes)


def attend_kernel(count, meta_ref, rows_ref, mask_ref, bias_ref, *refs):
    pieces = refs[:count]
    q_ref, k_ref, v_ref, p_ref, o_ref, low_ref, out_rows = refs[count : count + 7]
    weight, score, soft, sem, out_sem = refs[count + 7 :]
    pair = pl.program_id(0)
    chip = meta_ref[0]
    length = rows_ref.shape[0]
    blocks = length // lanes
    group = 2 * lanes
    stacked = [(piece.at[3], out_rows.at[step]) for step, piece in enumerate(pieces)]

    @pl.when(pair == 0)
    def _():
        loads = run_copies(load_pairs(pieces, meta_ref, 0, weight), sem)
        run_copies(stacked, out_sem)
        wait_all(loads)

    cols = pl.ds(pl.multiple_of(pair * lanes, lanes), lanes)
    own = rows_ref[pl.ds(pl.multiple_of(chip * group, group), group), :]
    query = mm(own, weight[0, :, cols]).astype(bf16)
    both = jnp.concatenate([weight[1, :, cols], weight[2, :, cols]], axis=1)
    key_value = mm(rows_ref[...], both).astype(bf16)
    key, value = key_value[:, :lanes], key_value[:, lanes:]
    q_ref[...] = query
    k_ref[...] = key
    v_ref[...] = value
    score[...] = mm_nt(key, jnp.concatenate([one_head(query, half) for half in range(2)], axis=0))
    for half in range(2):
        lane = slice(half * group, (half + 1) * group)
        best = jnp.full((8, group), masked_score, f32)
        for block in range(blocks):
            rows = slice(block * lanes, (block + 1) * lanes)
            bias = [bias_ref[half, band_place(block, chip, part), :] for part in range(2)]
            now = score[rows, lane] + jnp.concatenate(bias, axis=1) + mask_ref[rows, :]
            score[rows, lane] = now
            best = jnp.maximum(best, jnp.max(now.reshape(lanes // 8, 8, group), axis=0))
        top = jnp.max(best, axis=0, keepdims=True)
        total = jnp.zeros((8, group), f32)
        for block in range(blocks):
            rows = slice(block * lanes, (block + 1) * lanes)
            now = jnp.exp(score[rows, lane] - top)
            score[rows, lane] = now
            total = total + jnp.sum(now.reshape(lanes // 8, 8, group), axis=0)
        inverse = 1.0 / jnp.sum(total, axis=0, keepdims=True)
        for block in range(blocks):
            rows = slice(block * lanes, (block + 1) * lanes)
            now = score[rows, lane] * inverse
            p_ref[half, rows, :] = now
            soft[rows, lane] = now.astype(bf16)
    features = lanes // 2
    both_turned = mm_tn(value, soft[...])
    turned = [both_turned[:features, :group], both_turned[features:, group:]]
    attended = jnp.concatenate(turned, axis=0).T
    o_ref[...] = attended
    low_ref[...] = attended.astype(bf16)

    @pl.when(pair == pl.num_programs(0) - 1)
    def _():
        wait_all([pltpu.make_async_copy(a, b, out_sem.at[i]) for i, (a, b) in enumerate(stacked)])


def attend(pieces, meta, rows, mask, bias):
    length, width = rows.shape
    half = width // 2
    group = 2 * lanes
    pairs = half // lanes
    col = lambda i, *_: (0, i)
    fixed = lambda i, *_: (0, 0)
    flops = 2 * (group * width * half + 2 * length * width * half + 4 * group * length * half)
    return pl.pallas_call(
        functools.partial(attend_kernel, len(pieces)),
        grid_spec=pltpu.PrefetchScalarGridSpec(
            num_scalar_prefetch=1,
            grid=(pairs,),
            in_specs=[
                pl.BlockSpec((length, width), fixed),
                pl.BlockSpec((length, group), fixed),
                pl.BlockSpec((2, 5 * lanes, lanes), lambda i, *_: (i, 0, 0)),
            ]
            + [any_spec()] * len(pieces),
            out_specs=[
                pl.BlockSpec((group, lanes), col),
                pl.BlockSpec((length, lanes), col),
                pl.BlockSpec((length, lanes), col),
                pl.BlockSpec((2, length, group), lambda i, *_: (i, 0, 0)),
                pl.BlockSpec((group, lanes), col),
                pl.BlockSpec((group, lanes), col),
                pl.BlockSpec((len(pieces),) + pieces[0].shape[1:], lambda i, *_: (0, 0, 0)),
            ],
            scratch_shapes=[
                pltpu.VMEM((3, width, half), bf16),
                pltpu.VMEM((length, 2 * group), f32),
                pltpu.VMEM((length, 2 * group), bf16),
                dma(len(pieces)),
                dma(len(pieces)),
            ],
        ),
        out_shape=[
            shaped(bf16, group, half),
            shaped(bf16, length, half),
            shaped(bf16, length, half),
            shaped(f32, 2 * pairs, length, group),
            shaped(f32, group, half),
            shaped(bf16, group, half),
            shaped(bf16, len(pieces), *pieces[0].shape[1:]),
        ],
        compiler_params=params(),
        cost_estimate=cost(flops, 30e6, 2 * group * length * pairs),
        name="attend",
    )(meta, rows, mask, bias, *pieces)


def mix_kernel(
    meta_ref, tokens_ref, own_ref, their_ref, gain_ref, near_ref, far_ref, mixed_ref, normed_ref, turned_ref, joined_ref, weight_ref, held, sem
):
    chips, rows, half = near_ref.shape
    rows = rows // 2
    pairs = []
    for index, source in enumerate((near_ref, far_ref)):
        for step in range(chips):
            place = row_block(meta_ref, 1 + index * chips + step, rows)
            for side in range(2):
                pairs.append(
                    (
                        source.at[step, side * rows : (side + 1) * rows, :],
                        weight_ref.at[place, side * half : (side + 1) * half],
                    )
                )
    copies = run_copies(pairs, sem)
    first = meta_ref[0] == 0
    held[:, :half] = jnp.where(first, own_ref[...], their_ref[...])
    held[:, half:] = jnp.where(first, their_ref[...], own_ref[...])
    joined_ref[...] = held[...].T
    wait_all(copies)
    mixed = tokens_ref[...] + mm(held[...], weight_ref[...])
    mixed_ref[...] = mixed
    normed = (mixed * rms_scale(mixed) * gain_ref[...]).astype(bf16)
    normed_ref[...] = normed
    turned_ref[...] = normed.T


def mix(meta, tokens, own, their, gain, near, far):
    group, half = own.shape
    width = 2 * half
    return pl.pallas_call(
        mix_kernel,
        in_specs=[smem_spec()] + [whole_spec()] * 4 + [any_spec()] * 2,
        out_specs=[whole_spec()] * 5,
        out_shape=[
            shaped(f32, group, width),
            shaped(bf16, group, width),
            shaped(bf16, width, group),
            shaped(bf16, width, group),
            shaped(bf16, width, width),
        ],
        scratch_shapes=[pltpu.VMEM((group, width), bf16), dma(4 * near.shape[0])],
        compiler_params=params(),
        cost_estimate=cost(4 * group * width * half, 4e6),
        name="mix",
    )(meta, tokens, own, their, gain, near, far)


def feed_kernel(
    chips,
    places,
    gu_count,
    meta_ref,
    normed_low,
    turned_low,
    cot_ref,
    *refs,
):
    refs = list(refs)
    take = lambda n: [refs.pop(0) for _ in range(n)]
    gu_pieces = take(gu_count)
    down_pieces = take(places)
    out_ref, back_ref = take(2)
    gu_outs, down_outs = take(chips), take(2)
    gu, down, grad_gu, grad_down, cot_low = take(5)
    gu_sem, down_sem, gu_out_sem, down_out_sem = take(4)
    step = pl.program_id(0)
    steps = pl.num_programs(0)
    block = 512

    count = gu.shape[2] // block

    def gu_loads(turn):
        columns = pl.ds(pl.multiple_of(turn * block, block), block)
        pairs = []
        for index, piece in enumerate(gu_pieces):
            place = row_block(meta_ref, min(index, chips - 1), piece.shape[1])
            lead = slice(0, 2) if piece.shape[0] == 2 else slice(index - 3, index - 2)
            pairs.append((piece.at[:, :, columns], gu.at[lead, place, columns]))
        return [
            pltpu.make_async_copy(a, b, gu_sem.at[turn, index]) for index, (a, b) in enumerate(pairs)
        ]

    def gu_stores(turn):
        columns = pl.ds(pl.multiple_of(turn * block, block), block)
        copies = []
        for chip, out in enumerate(gu_outs):
            source = grad_gu.at[:, row_block(meta_ref, chip, out.shape[1]), columns]
            copies.append(pltpu.make_async_copy(source, out.at[:, :, columns], gu_out_sem.at[turn, chip]))
        return copies

    @pl.when(step == 0)
    def _():
        for copy in gu_loads(0):
            copy.start()
        pairs = []
        slot = chips
        for piece in down_pieces:
            for chip in range(chips):
                pairs.append((piece.at[chip], down.at[row_block(meta_ref, slot, piece.shape[1]), :]))
                slot += 1
        down_copies = run_copies(pairs, down_sem)
        for turn in range(1, count):
            for copy in gu_loads(turn):
                copy.start()
        cot_low[...] = cot_ref[...].astype(bf16)
        out_ref[...] = jnp.zeros_like(out_ref)
        back_ref[...] = jnp.zeros_like(back_ref)
        wait_all(down_copies)

    for copy in gu_loads(step):
        copy.wait()
    cols = pl.ds(pl.multiple_of(step * block, block), block)
    normed = normed_low[...]
    cot = cot_low[...]
    gate_w, up_w, down_w = gu[0, :, cols], gu[1, :, cols], down[cols, :]
    gate, up = mm(normed, gate_w), mm(normed, up_w)
    square = gate * gate
    curve = jnp.tanh(gelu_scale * gate * (1.0 + gelu_cubic * square))
    half = 0.5 * (1.0 + curve)
    gelu = gate * half
    slope = half + 0.5 * gate * (1.0 - curve * curve) * gelu_scale * (1.0 + 3.0 * gelu_cubic * square)
    hidden = (gelu * up).astype(bf16)
    dh = mm_nt(cot, down_w)
    dgate = (dh * up * slope).astype(bf16)
    dup = (dh * gelu).astype(bf16)
    out_ref[...] += mm(hidden, down_w)
    back_ref[...] += mm_nt(dgate, gate_w) + mm_nt(dup, up_w)
    grad_down[cols, :] = mm_tn(hidden, cot).astype(bf16)
    both = mm(turned_low[...], jnp.concatenate([dgate, dup], axis=1)).astype(bf16)
    grad_gu[0, :, cols] = both[:, :block]
    grad_gu[1, :, cols] = both[:, block:]

    for copy in gu_stores(step):
        copy.start()

    @pl.when(step == steps - 1)
    def _():
        pairs = []
        for turn, out in enumerate(down_outs):
            for spot in range(places // 2):
                for chip in range(chips):
                    slot = chips * (1 + places + turn * (places // 2) + spot) + chip
                    place = row_block(meta_ref, slot, out.shape[2])
                    pairs.append((grad_down.at[place, :], out.at[spot, chip]))
        down_copies = run_copies(pairs, down_out_sem)
        for turn in range(count):
            wait_all(gu_stores(turn))
        wait_all(down_copies)


def feed(gu_pieces, down_pieces, meta, normed, turned, cot, chips, places):
    group, width = normed.shape
    hidden = gu_pieces[0].shape[2]
    block = 512
    fixed = lambda i, *_: (0, 0)
    full = lambda *shape: pl.BlockSpec(shape, fixed)
    flops = 2 * 9 * group * width * hidden
    results = pl.pallas_call(
        functools.partial(feed_kernel, chips, places, len(gu_pieces)),
        grid_spec=pltpu.PrefetchScalarGridSpec(
            num_scalar_prefetch=1,
            grid=(hidden // block,),
            in_specs=[full(group, width), full(width, group), full(group, width)]
            + [any_spec()] * (len(gu_pieces) + places),
            out_specs=[full(group, width)] * 2 + [any_spec()] * (chips + 2),
            scratch_shapes=[
                pltpu.VMEM((2, width, hidden), bf16),
                pltpu.VMEM((hidden, width), bf16),
                pltpu.VMEM((2, width, hidden), bf16),
                pltpu.VMEM((hidden, width), bf16),
                pltpu.VMEM((group, width), bf16),
                pltpu.SemaphoreType.DMA((hidden // block, len(gu_pieces))),
                dma(chips * places),
                pltpu.SemaphoreType.DMA((hidden // block, chips)),
                dma(chips * places),
            ],
        ),
        out_shape=[shaped(f32, group, width)] * 2
        + [shaped(bf16, 2, width // chips, hidden)] * chips
        + [shaped(bf16, places // 2, chips, hidden // (chips * places), width)] * 2,
        compiler_params=params(),
        cost_estimate=cost(flops, 25e6, group * hidden),
        name="feed",
    )(meta, normed, turned, cot, *gu_pieces, *down_pieces)
    return results[:2], results[2 : 2 + chips], results[2 + chips :]


def settle_kernel(
    meta_ref,
    mixed_ref,
    cot_ref,
    back_ref,
    arrived_ref,
    weight_ref,
    gain_ref,
    dmixed_ref,
    do_ref,
    gain_grad_ref,
    branch_ref,
):
    core = meta_ref[0]
    half = do_ref.shape[1]
    mixed = mixed_ref[...]
    scale = rms_scale(mixed)
    dn2 = back_ref[...] + arrived_ref[...]
    gained = dn2 * gain_ref[...]
    inner = jnp.mean(gained * mixed, axis=-1, keepdims=True)
    dmixed = cot_ref[...] + scale * gained - mixed * (scale * scale * scale * inner)
    dmixed_ref[...] = dmixed
    gain_grad_ref[...] = 0.5 * jnp.sum(dn2 * mixed * scale, axis=0, keepdims=True)
    branch = dmixed.astype(bf16)
    branch_ref[...] = branch
    mine = weight_ref[pl.ds(pl.multiple_of(core * half, half), half), :]
    do_ref[...] = mm_nt(branch, mine).astype(bf16)


def settle(meta, mixed, cot, back, arrived, weight, gain):
    group, width = mixed.shape
    half = width // 2
    return pl.pallas_call(
        settle_kernel,
        in_specs=[smem_spec()] + [whole_spec()] * 6,
        out_specs=[whole_spec()] * 4,
        out_shape=[
            shaped(f32, group, width),
            shaped(bf16, group, half),
            shaped(f32, 1, width),
            shaped(bf16, group, width),
        ],
        compiler_params=params(),
        cost_estimate=cost(2 * group * width * half, 6e6),
        name="settle",
    )(meta, mixed, cot, back, arrived, weight, gain)


def band_rows(band_ref):
    line = lax.broadcasted_iota(jnp.int32, (8, 2 * lanes), 0)
    none = jnp.zeros((8, lanes), f32)
    found = []
    for block in range(3):
        summed = jnp.zeros((8, 2 * lanes), f32)
        for part in range(lanes // 8):
            start = lanes * (block + 1) + 8 * part
            wide = jnp.concatenate([band_ref[start : start + 8, :], none], axis=1)
            move = lanes - 8 - 8 * part
            summed = summed + (pltpu.roll(wide, move, 1) if move else wide)
        for bit in range(3):
            step = 1 << bit
            summed = jnp.where((line & step) == 0, pltpu.roll(summed, step, 1), summed)
        found.append(jnp.sum(summed, axis=0, keepdims=True))
    return jnp.concatenate(found, axis=1)


def retreat_kernel(meta_ref, do_ref, o_ref, q_ref, k_ref, v_ref, p_ref, dq_ref, dkv_ref, bias_ref, low, soft_low, spread_of, band_ref, onehot):
    chip = meta_ref[0]
    blocks = k_ref.shape[0] // lanes
    group = 2 * lanes
    features = lanes // 2
    do = do_ref[...]
    spread = (do.astype(f32) * o_ref[...]).T
    band_ref[...] = jnp.zeros_like(band_ref)
    far = jnp.zeros((8, lanes), f32)
    rows_of = []

    @pl.when(pl.program_id(0) == 0)
    def _():
        bucket = lax.broadcasted_iota(jnp.int32, (6 * lanes, lanes), 1)
        spot = lax.broadcasted_iota(jnp.int32, (6 * lanes, lanes), 0)
        offset = lanes * (spot // (2 * lanes)) - 1 - spot % (2 * lanes)
        onehot[...] = (bucket_of(offset) == bucket).astype(f32)

    do_two = jnp.concatenate([one_head(do, half) for half in range(2)], axis=0)
    query_two = jnp.concatenate([one_head(q_ref[...], half) for half in range(2)], axis=0)
    spread_of[...] = mm_nt(v_ref[...], do_two)
    for half in range(2):
        lane = slice(half * group, (half + 1) * group)
        delta = jnp.sum(spread[half * features : (half + 1) * features], axis=0, keepdims=True)
        for block in range(blocks):
            rows = slice(block * lanes, (block + 1) * lanes)
            soft = p_ref[half, rows, :]
            ds = soft * (spread_of[rows, lane] - delta)
            for part in range(2):
                place = band_place(block, chip, part)
                band_ref[place, :] += ds[:, part * lanes : (part + 1) * lanes]
            low[rows, lane] = ds.astype(bf16)
            soft_low[rows, lane] = soft.astype(bf16)
        rows_of.append(band_rows(band_ref))
        low_sum = jnp.sum(band_ref[0:lanes, :])
        high_sum = jnp.sum(band_ref[4 * lanes : 5 * lanes, :])
        lane_id = lax.broadcasted_iota(jnp.int32, (8, lanes), 1)
        line = lax.broadcasted_iota(jnp.int32, (8, lanes), 0)
        far = far + jnp.where((lane_id == 15) & (line == half), low_sum, 0.0)
        far = far + jnp.where((lane_id == 31) & (line == half), high_sum, 0.0)
        if half == 0:
            band_ref[...] = jnp.zeros_like(band_ref)
    dkv_ref[:, :lanes] = mm(low[...], query_two).astype(bf16)
    dkv_ref[:, lanes:] = mm(soft_low[...], do_two).astype(bf16)
    both_turned = mm_tn(k_ref[...], low[...])
    turned = [both_turned[:features, :group], both_turned[features:, group:]]
    dq_ref[...] = jnp.concatenate(turned, axis=0).T.astype(bf16)
    rows_of.append(jnp.zeros((6, rows_of[0].shape[1]), f32))
    near = lax.dot_general(
        jnp.concatenate(rows_of, axis=0),
        onehot[...],
        (((1,), (0,)), ((), ())),
        precision=lax.Precision.HIGHEST,
        preferred_element_type=f32,
    )
    bias_ref[0] = near + far


def retreat(meta, do, o, q, k, v, p):
    length, half = k.shape
    group = do.shape[0]
    pairs = half // lanes
    col = lambda i, *_: (0, i)
    deep = lambda i, *_: (i, 0, 0)
    flops = 2 * 8 * group * length * half
    return pl.pallas_call(
        retreat_kernel,
        grid_spec=pltpu.PrefetchScalarGridSpec(
            num_scalar_prefetch=1,
            grid=(pairs,),
            in_specs=[
                pl.BlockSpec((group, lanes), col),
                pl.BlockSpec((group, lanes), col),
                pl.BlockSpec((group, lanes), col),
                pl.BlockSpec((length, lanes), col),
                pl.BlockSpec((length, lanes), col),
                pl.BlockSpec((2, length, group), deep),
            ],
            out_specs=[
                pl.BlockSpec((group, lanes), col),
                pl.BlockSpec((length, 2 * lanes), col),
                pl.BlockSpec((1, 8, lanes), deep),
            ],
            scratch_shapes=[
                pltpu.VMEM((length, 2 * group), bf16),
                pltpu.VMEM((length, 2 * group), bf16),
                pltpu.VMEM((length, 2 * group), f32),
                pltpu.VMEM((5 * lanes, lanes), f32),
                pltpu.VMEM((6 * lanes, lanes), f32),
            ],
        ),
        out_shape=[
            shaped(bf16, group, half),
            shaped(bf16, length, 2 * half),
            shaped(f32, pairs, 8, lanes),
        ],
        compiler_params=params(),
        cost_estimate=cost(flops, 20e6),
        name="retreat",
    )(meta, do, o, q, k, v, p)


small_rows = 16


def load_pairs(pieces, meta_ref, first, weight):
    pairs = []
    for step, piece in enumerate(pieces):
        place = row_block(meta_ref, first + step, piece.shape[1])
        pairs.append((piece.at[0:3], weight.at[:, place, :]))
    return pairs


def grads_kernel(
    chips, meta_ref, turned_ref, dq_ref, dkv_ref, gains_ref, second_ref, bias_ref, joined_ref, branch_ref, *refs
):
    refs = list(refs)
    take = lambda n: [refs.pop(0) for _ in range(n)]
    pieces, outs = take(chips), take(chips)
    weight, grad, wo, small, sem, out_sem = take(6)
    chip, core = meta_ref[0], meta_ref[1]
    width = turned_ref.shape[0]
    half = width // 2
    group = dq_ref.shape[0]
    loads = run_copies(load_pairs(pieces, meta_ref, 2, weight), sem)
    wo_rows = wo.shape[1]
    mine = []
    for index in range(chips):
        even = joined_ref[2 * index * wo_rows : (2 * index + 1) * wo_rows, :]
        odd = joined_ref[(2 * index + 1) * wo_rows : (2 * index + 2) * wo_rows, :]
        mine.append(jnp.where(core == 0, even, odd))
    out_grad = mm(jnp.concatenate(mine, axis=0), branch_ref[...]).astype(bf16)
    for index in range(chips):
        wo[index] = out_grad[index * wo_rows : (index + 1) * wo_rows]
    own_rows = pl.ds(pl.multiple_of(chip * group, group), group)
    query_grad = mm(turned_ref[:, own_rows], dq_ref[...])
    grad[0] = query_grad.astype(bf16)
    wait_all(loads)
    along_row = [query_grad[:, at : at + lanes] * weight[0, :, at : at + lanes].astype(f32) for at in range(0, half, lanes)]
    along_row = sum(along_row[1:], along_row[0])
    for pair in range(half // lanes):
        wide = slice(pair * 2 * lanes, (pair + 1) * 2 * lanes)
        cols = slice(pair * lanes, (pair + 1) * lanes)
        summed = mm(turned_ref[...], dkv_ref[:, wide])
        low = summed.astype(bf16)
        grad[1, :, cols] = low[:, :lanes]
        grad[2, :, cols] = low[:, lanes:]
        along_row = along_row + summed[:, :lanes] * weight[1, :, cols].astype(f32)
        along_row = along_row + summed[:, lanes:] * weight[2, :, cols].astype(f32)
    first_gain = jnp.sum(along_row.T, axis=0, keepdims=True) / gains_ref[...]
    second_gain = second_ref[...]
    lines = [first_gain[:, :half], first_gain[:, half:], second_gain[:, :half], second_gain[:, half:]]
    for pair in range(bias_ref.shape[0]):
        both = [bias_ref[pair, 0:1, :], bias_ref[pair, 1:2, :]]
        both.append(jnp.zeros((1, half - 2 * lanes), f32))
        lines.append(jnp.concatenate(both, axis=1))
    lines.append(jnp.zeros((small_rows - len(lines), half), f32))
    small[...] = jnp.concatenate(lines, axis=0).astype(bf16)
    rows = width // chips
    side_rows = rows // 2
    pairs = []
    for step, out in enumerate(outs):
        place = row_block(meta_ref, 2 + step, rows)
        at = 0
        for matrix in range(3):
            pairs.append((grad.at[matrix, place, :], out.at[at : at + rows, :]))
            at += rows
        for side in range(2):
            source = wo.at[meta_ref[2 + step], :, side * half : (side + 1) * half]
            pairs.append((source, out.at[at : at + side_rows, :]))
            at += side_rows
        pairs.append((small, out.at[at : at + small_rows, :]))
    wait_all(run_copies(pairs, out_sem))


def weight_grads(pieces, meta, turned, dq, dkv, gain, second, bias, joined, branch, chips):
    width, length = turned.shape
    half = width // 2
    group = dq.shape[0]
    flops = 2 * (2 * length * width * half + group * width * half)
    block = width // chips
    return pl.pallas_call(
        functools.partial(grads_kernel, chips),
        in_specs=[smem_spec()] + [whole_spec()] * 8 + [any_spec()] * len(pieces),
        out_specs=[any_spec()] * chips,
        out_shape=[shaped(bf16, 4 * block + small_rows, half)] * chips,
        scratch_shapes=[
            pltpu.VMEM((3, width, half), bf16),
            pltpu.VMEM((3, width, half), bf16),
            pltpu.VMEM((chips, block // 2, width), bf16),
            pltpu.VMEM((small_rows, half), bf16),
            dma(chips),
            dma(6 * chips),
        ],
        compiler_params=params(),
        cost_estimate=cost(flops, 12e6),
        name="weight_grads",
    )(meta, turned, dq, dkv, gain, second, bias, joined, branch, *pieces)


def back_kernel(chips, meta_ref, dq_ref, dkv_ref, *refs):
    refs = list(refs)
    take = lambda n: [refs.pop(0) for _ in range(n)]
    pieces = take(chips)
    near_out, far_out = take(2)
    weight, both, back, sem = take(4)
    chip, core = meta_ref[0], meta_ref[1]
    length = dkv_ref.shape[0]
    half = dq_ref.shape[1]
    group = dq_ref.shape[0]
    wait_all(run_copies(load_pairs(pieces, meta_ref, 2, weight), sem))
    for pair in range(half // lanes):
        wide = pair * 2 * lanes
        cols = slice(pair * lanes, (pair + 1) * lanes)
        both[:, wide : wide + lanes] = weight[1, :, cols]
        both[:, wide + lanes : wide + 2 * lanes] = weight[2, :, cols]
    for start in range(0, length, group):
        back[start : start + group, :] = mm_nt(dkv_ref[start : start + group, :], both[...])
    own_rows = pl.ds(pl.multiple_of(chip * group, group), group)
    back[own_rows, :] += mm_nt(dq_ref[...], weight[0])
    for index, step in enumerate(bit_reversed(chips)):
        for side, out in ((core, near_out), (1 - core, far_out)):
            start = meta_ref[2 + step] * group + side * lanes
            out[index] = back[pl.ds(pl.multiple_of(start, lanes), lanes), :].astype(bf16)


def row_grads(pieces, meta, dq, dkv, chips):
    length, width = dkv.shape
    half = width // 2
    return pl.pallas_call(
        functools.partial(back_kernel, chips),
        in_specs=[smem_spec()] + [whole_spec()] * 2 + [any_spec()] * len(pieces),
        out_specs=[whole_spec()] * 2,
        out_shape=[shaped(bf16, chips, lanes, width)] * 2,
        scratch_shapes=[
            pltpu.VMEM((3, width, half), bf16),
            pltpu.VMEM((width, width), bf16),
            pltpu.VMEM((length, width), f32),
            dma(chips),
        ],
        compiler_params=params(),
        cost_estimate=cost(4 * length * width * half, 8e6),
        name="row_grads",
    )(meta, dq, dkv, *pieces)


def cut_kernel(side_ref, *refs):
    sources, (kept_ref, sent_ref) = refs[:-2], refs[-2:]
    count = kept_ref.shape[2]
    for index, out in ((side_ref[0], kept_ref), (1 - side_ref[0], sent_ref)):
        for part in range(2):
            start = pl.multiple_of((2 * part + index) * count, count)
            out[0, part] = total([source[0, pl.ds(start, count), :] for source in sources]).astype(bf16)


def cut_plane(blocks, side):
    lead, height, width = blocks[0].shape
    shape = (lead, 2, height // 4, width)
    row = lambda *shape: pl.BlockSpec((1,) + shape, lambda i: (i,) + (0,) * len(shape))
    return pl.pallas_call(
        cut_kernel,
        grid=(lead,),
        in_specs=[smem_spec()] + [row(height, width)] * len(blocks),
        out_specs=[row(*shape[1:])] * 2,
        out_shape=[shaped(bf16, *shape)] * 2,
        compiler_params=params(),
        cost_estimate=cost(1e6, 6e6),
        name="cut_plane",
    )(side.reshape(1), *blocks)


def sum_kernel(order_ref, *refs):
    places = order_ref.shape[0]
    sources, outs, total_ref = refs[: -1 - places], refs[-1 - places : -1], refs[-1]
    total_ref[...] = total([source[...] for source in sources])
    height = total_ref.shape[0] - small_rows
    rows = height // (8 * places)
    last = total_ref[height:, :]
    for turn, out in enumerate(outs):
        parts = []
        for block in range(8):
            start = block * places * rows + order_ref[turn] * rows
            parts.append(total_ref[pl.ds(pl.multiple_of(start, 8), rows), :])
        out[...] = jnp.concatenate(parts + [last], axis=0).astype(bf16)


def sum_plane(blocks, order):
    height, half = blocks[0].shape
    places = order.shape[0]
    rows = (height - small_rows) // (8 * places)
    if rows % 8:
        summed = total(blocks).astype(bf16)
        split, last = summed[:-small_rows].reshape(8, places, rows, half), summed[-small_rows:]
        pick = lambda turn: lax.dynamic_index_in_dim(split, order[turn], 1, keepdims=False)
        return [jnp.concatenate([pick(turn).reshape(-1, half), last], axis=0) for turn in range(places)]
    return pl.pallas_call(
        sum_kernel,
        in_specs=[smem_spec()] + [whole_spec()] * len(blocks),
        out_specs=[whole_spec()] * places,
        out_shape=[shaped(bf16, (height - small_rows) // places + small_rows, half)] * places,
        scratch_shapes=[pltpu.VMEM((height, half), f32)],
        compiler_params=params(),
        cost_estimate=cost(1e6, 4e6),
        name="sum_plane",
    )(order, *blocks)


def last_kernel(core_ref, *refs):
    sources, (sum_ref, sent_ref) = refs[:-2], refs[-2:]
    summed = total([source[...] for source in sources])
    sum_ref[...] = summed
    rows = (summed.shape[0] - small_rows) // 8
    first = core_ref[0] == 0
    block = lambda index: summed[index * rows : (index + 1) * rows]
    parts = [jnp.where(first, block(2 * matrix + 1), block(2 * matrix)) for matrix in range(3)]
    sent_ref[...] = jnp.concatenate(parts + [summed[8 * rows :]], axis=0)


def last_sum(core, arrived):
    height, half = arrived[0].shape
    rows = (height - small_rows) // 8
    return pl.pallas_call(
        last_kernel,
        in_specs=[smem_spec()] + [whole_spec()] * len(arrived),
        out_specs=[whole_spec()] * 2,
        out_shape=[shaped(f32, height, half), shaped(f32, 3 * rows + small_rows, half)],
        compiler_params=params(),
        cost_estimate=cost(1e6, 1e6),
        name="last_sum",
    )(core.reshape(1), *arrived)


def attention_kernel(
    rates, core_ref, sum_ref, arrived_ref, weight_ref, momentum_ref, average_ref, *outs
):
    new_weight, new_momentum, new_average, copy = outs
    rows, width = weight_ref.shape[1:]
    half = width // 2
    first = core_ref[0] == 0
    block = lambda index: sum_ref[index * rows : (index + 1) * rows, :]
    for matrix in range(4):
        left, right = block(2 * matrix), block(2 * matrix + 1)
        if matrix < 3:
            mine = jnp.where(first, left, right)
            theirs = arrived_ref[matrix * rows : (matrix + 1) * rows, :]
            left, right = jnp.where(first, mine, theirs), jnp.where(first, theirs, mine)
        for side, grad in enumerate((left, right)):
            at = (matrix, slice(None), slice(side * half, (side + 1) * half))
            values = update(
                weight_ref[at], grad, momentum_ref[at], average_ref[at], rates[matrix]
            )
            new_weight[at], new_momentum[at], new_average[at] = values
            copy[at] = values[0].astype(bf16)


def attention_update(core, summed, arrived, weight, momentum, average, rates):
    return pl.pallas_call(
        functools.partial(attention_kernel, rates),
        in_specs=[smem_spec()] + [whole_spec()] * 5,
        out_specs=[whole_spec()] * 4,
        out_shape=[shaped(f32, *weight.shape)] * 3 + [shaped(bf16, *weight.shape)],
        compiler_params=params(),
        cost_estimate=cost(1e6, 2e6),
        name="attention_update",
    )(core.reshape(1), summed, arrived, weight, momentum, average)


def core_swap(value):
    count = lax.axis_size("seq")
    return lax.ppermute(value, "seq", [(i, i ^ 1) for i in range(count)])


def plane_swap(value, step):
    count = lax.axis_size("seq")
    return lax.ppermute(value, "seq", [(i, i ^ (2 * step)) for i in range(count)])


def along(value, step):
    count = lax.axis_size("batch")
    return lax.ppermute(value, "batch", [(i, (i + step) % count) for i in range(count)])


def along_all(value):
    return [value] + [along(value, step) for step in range(1, lax.axis_size("batch"))]


def after(value, *earlier):
    return lax.optimization_barrier((value,) + earlier)[0]


def join_kernel(order_ref, *refs):
    sources, out = refs[:-1], refs[-1]
    for index, source in enumerate(sources):
        out[:, :, order_ref[index]] = source[...]


def join(blocks, order):
    lead, rest = blocks[0].shape[:2], blocks[0].shape[2:]
    return pl.pallas_call(
        join_kernel,
        in_specs=[smem_spec()] + [whole_spec()] * len(blocks),
        out_specs=whole_spec(),
        out_shape=shaped(bf16, *lead, len(blocks), *rest),
        compiler_params=params(),
        cost_estimate=cost(0, 2e6),
        name="join",
    )(order, *blocks)


def gather_plane(value):
    return [value] + [plane_swap(value, step) for step in range(1, lax.axis_size("seq") // 2)]


def total(blocks):
    summed = blocks[0].astype(f32)
    for block in blocks[1:]:
        summed = summed + block.astype(f32)
    return summed


def scatter_plane(blocks):
    return [blocks[0]] + [plane_swap(part, step) for step, part in enumerate(blocks) if step]


def bit_reversed(chips):
    order = [0]
    while len(order) < chips:
        order = [2 * step for step in order] + [2 * step + 1 for step in order]
    return order


def halves_along(value, dim, place):
    count = value.shape[dim] // 2
    split = value.reshape(value.shape[:dim] + (2, count) + value.shape[dim + 1 :])
    side = (place // count) % 2
    pick = lambda index: lax.dynamic_index_in_dim(split, index, dim, keepdims=False)
    return pick(side), pick(1 - side)


def across(value, step):
    count = lax.axis_size("batch")
    return lax.ppermute(value, "batch", [(i, i ^ step) for i in range(count)])


def halved(blocks, step):
    count = blocks.shape[0] // 2
    return blocks[:count], plane_swap(blocks[count:], step)


def summed_half(halves):
    return total(halves).astype(bf16)


def finished(halves, steps):
    for step in steps:
        halves = halved(summed_half(halves), step)
    return total(halves)[0]


def spread(values):
    return [values[0]] + [along(value, step) for step, value in enumerate(values) if step]


def spread_along(split, dim, place):
    count = lax.axis_size("batch")
    pick = lambda step: lax.dynamic_index_in_dim(split, (place + step) % count, dim, keepdims=False)
    return [pick(0)] + [along(pick(step), step) for step in range(1, count)]


def shards(
    tokens,
    cotangent,
    group_ids,
    attention_weight,
    ffin_weight,
    ffout_weight,
    bias_table,
    gains,
    attention_momentum,
    ffin_momentum,
    ffout_momentum,
    bias_momentum,
    gain_momentum,
    attention_average,
    ffin_average,
    ffout_average,
    bias_average,
    gain_average,
):
    _, tok, width = tokens.shape
    cycle_size, places = lax.axis_size("seq"), lax.axis_size("batch")
    cycle_index = lax.axis_index("seq").astype(jnp.int32)
    place = lax.axis_index("batch").astype(jnp.int32)
    chips = cycle_size // 2
    chip, core = cycle_index // 2, cycle_index % 2
    half = width // 2
    rows = attention_weight.shape[1]
    down_rows = ffout_weight.shape[0]
    hidden = ffin_weight.shape[2]
    grain = hidden // cycle_size
    heads = bias_table.shape[1]
    group = 2 * tok
    first_core = core == 0

    def by_core(mine, theirs):
        return [jnp.where(first_core, mine, theirs), jnp.where(first_core, theirs, mine)]

    steps = [chip ^ step for step in range(chips)]
    order = jnp.stack([(place + places - step) % places for step in range(places)])
    onward = jnp.stack([(place + step) % places for step in range(places)])
    flat_tokens, flat_cot = tokens.reshape(tok, width), cotangent.reshape(tok, width)

    attn_kept, attn_sent, gu_kept, gu_sent, row_block_own = make_ready(
        core,
        attention_weight,
        ffin_weight,
        ffout_weight,
        flat_tokens,
        group_ids,
        gains,
        chips,
    )
    their_tokens, their_cot = core_swap(flat_tokens), core_swap(flat_cot)
    attn_from, gu_from = core_swap(attn_sent), core_swap(gu_sent)
    row_block_own, attn_kept = lax.optimization_barrier((row_block_own, attn_kept, their_tokens, their_cot))[:2]
    attn_block = fill(core, after(attn_kept, gu_from), attn_from)
    gu_block = fill(core, gu_kept, gu_from)

    attn_blocks = along_all(attn_block)
    row_blocks, step = row_block_own[None], 1
    while step < chips:
        arrived = plane_swap(row_blocks, step)
        arrived = after(arrived, attn_block if step * 2 < chips else attn_blocks)
        row_blocks = jnp.concatenate([row_blocks, arrived], axis=0)
        step *= 2
    near_rows, down_block = row_blocks[:, : tok + 16], row_blocks[:, tok + 16 :]
    own_heads = jnp.where(first_core, bias_table[:, : heads // 2], bias_table[:, heads // 2 :])
    bias = bias_rows(after(own_heads, attn_block))

    attn_joined = join(after(attn_blocks, near_rows, bias, gu_block), order).reshape(4, 2 * places * rows, half)
    chip_tokens = jnp.concatenate(by_core(flat_tokens, their_tokens), axis=0)
    chip_cot = jnp.concatenate(by_core(flat_cot, their_cot), axis=0)
    far_rows = core_swap(after(near_rows, attn_joined))
    rows_full, turned, mask = place_rows(jnp.stack(steps + [core]), near_rows, far_rows)
    attn_pieces = gather_plane(attn_joined)
    gu_blocks = [after(gu_block, attn_joined)]
    for step in range(1, places):
        if step == 2:
            gu_blocks[-1], down_block = lax.optimization_barrier((gu_blocks[-1], down_block, rows_full))[:2]
        gu_blocks.append(along(gu_blocks[-1], 1))
    down_pieces = [down_block, along(down_block, 1)]
    gu_joined = join(gu_blocks, order)
    attn_pieces, rows_full, gu_joined, down_pieces = lax.optimization_barrier(
        (attn_pieces, rows_full, gu_joined, down_pieces)
    )
    chip_tokens, chip_cot, mask = lax.optimization_barrier((chip_tokens, chip_cot, mask))
    gu_joined, down_pieces, mask = lax.optimization_barrier((gu_joined, down_pieces, mask))
    down_pieces.append(along(down_pieces[-1], 1))
    gu_own = gu_joined.reshape(2, 2 * places * rows, hidden // 2)
    gu_pieces = [gu_own] + [plane_swap(gu_own, step) for step in range(1, 3 if chips == 4 else chips)]
    step_meta = jnp.stack(steps)
    query, key, value, soft, attended, attended_low, wo_near = attend(
        attn_pieces, step_meta, rows_full, mask, bias
    )
    wo_meta = jnp.stack([core] + [step * 2 + core for step in steps] + [step * 2 + 1 - core for step in steps])
    their_attended = core_swap(attended_low)
    their_attended, gu_pieces, down_pieces, wo_near = lax.optimization_barrier(
        (their_attended, gu_pieces, down_pieces, wo_near)
    )
    if chips == 4:
        passed = [gu_pieces[1][:1], gu_pieces[2][1:]]
        their_attended, passed, wo_near = lax.optimization_barrier((their_attended, passed, wo_near))
        gu_pieces += [plane_swap(passed[0], 2), plane_swap(passed[1], 1)]
    for _ in range(3, places):
        down_pieces.append(along(down_pieces[-1], 1))
    wo_far = core_swap(wo_near)
    mixed, second_low, second_turned, joined, out_weight = mix(
        wo_meta, chip_tokens, attended_low, their_attended, gains[1:2], wo_near, wo_far
    )
    down_meta = [step * places + order[index] for index in range(places) for step in steps]
    high = place // (places // 2)
    for side in (high, 1 - high):
        for spot in range(places // 2):
            down_meta += [step * places + side * (places // 2) + spot for step in steps]
    (out_part, back_part), gu_grads, down_grads = feed(
        gu_pieces, down_pieces, jnp.stack(steps + down_meta), second_low, second_turned, chip_cot, chips, places
    )
    add = lambda a, b: total([a, b]).astype(bf16)
    gu_arrived = scatter_plane(gu_grads)
    down_moving = across(down_grads[1], places // 2)
    their_back = core_swap(back_part)
    dmixed, attended_grad, second_gain, branch = settle(
        core.reshape(1), mixed, chip_cot, back_part, their_back, out_weight, gains[1:2]
    )
    dq, dkv, bias_part = retreat(chip.reshape(1), attended_grad, attended, query, key, value, soft)
    pair_meta = jnp.stack([chip, core] + steps)
    attn_grads = weight_grads(
        attn_pieces,
        pair_meta,
        turned,
        dq,
        dkv,
        gains[:1],
        second_gain,
        bias_part,
        joined,
        branch,
        chips,
    )

    near_back, far_back = row_grads(attn_pieces, pair_meta, after(dq, attn_grads), dkv, chips)
    mine = lambda value: lax.dynamic_slice_in_dim(value, core * tok, tok, 0)
    theirs = lambda value: lax.dynamic_slice_in_dim(value, (1 - core) * tok, tok, 0)
    back_arrived = core_swap(far_back)
    attn_grads, gu_arrived, down_moving = lax.optimization_barrier(
        (attn_grads, gu_arrived, down_moving, back_arrived)
    )[:3]
    attn_arrived = [attn_grads[0]] + [plane_swap(attn_grads[step], step) for step in range(1, min(chips, 3))]
    reach = places // 2
    if rows * reach % 16 == 0:
        halves = cut_plane(gu_arrived, place // reach)
        gu_kept, gu_sent = [part.reshape(2, 2, reach, rows, hidden // 2) for part in halves]
    else:
        gu_sum = total(gu_arrived).astype(bf16).reshape(2, 2, places, rows, hidden // 2)
        gu_kept, gu_sent = halves_along(gu_sum, 2, place)
    gu_moving = across(gu_sent, reach)
    down_sum = add(after(down_moving, gu_sent), down_grads[0])
    down_kept, down_sent = halves_along(down_sum, 0, place)
    down_moving = across(down_sent, reach // 2)
    attn_arrived += [plane_swap(attn_grads[step], step) for step in range(3, chips)]
    attn_arrived, gu_moving, down_moving, out_part = lax.optimization_barrier(
        (attn_arrived, gu_moving, down_moving, out_part)
    )
    their_out = core_swap(theirs(out_part))
    while reach > 2:
        gu_kept, gu_sent = halves_along(add(gu_kept, gu_moving), 2, place)
        reach //= 2
        gu_moving = across(gu_sent, reach)
        down_kept, down_sent = halves_along(add(down_kept, down_moving), 0, place)
        down_moving = across(down_sent, reach // 2)
    down_last = add(down_kept, down_moving)[0]
    gu_kept, gu_sent = halves_along(add(gu_kept, gu_moving), 2, place)
    attn_arrived, gu_sent, down_last = lax.optimization_barrier((attn_arrived, gu_sent, down_last))
    down_halves = halved(down_last, chips // 2)
    gu_moving = across(gu_sent, 1)
    gu_sum = total([gu_kept, gu_moving])[:, :, 0]
    layer_output = mine(mixed) + mine(out_part) + their_out
    pick = lambda value, first, dim: jnp.where(
        first, lax.index_in_dim(value, 0, dim, False), lax.index_in_dim(value, 1, dim, False)
    )
    gu_own = pick(gu_sum, first_core, 1)
    gu_their = core_swap(pick(gu_sum, core == 1, 1))
    attn_cuts = sum_plane(attn_arrived, onward)
    attn_sum = spread(attn_cuts)
    merged = total([near_back, back_arrived]).astype(bf16)
    later_steps = [chips // 2 >> turn for turn in range(1, chips.bit_length() - 1)]
    back_sum = summed_half(halved(after(merged, attn_cuts, gu_sum), 1))
    back_halves = halved(back_sum, 2)
    down_sum = after(summed_half(down_halves), back_sum)
    own_down = finished(halved(down_sum, later_steps[0]), later_steps[1:])

    weave = lambda parts: jnp.stack(
        [part.reshape(2, rows, chips, grain) for part in parts], axis=3
    ).reshape(2, rows, hidden)
    own_gu = weave(by_core(gu_own, gu_their))
    all_tokens = places * tok * cycle_size
    inverse_root = 1.0 / math.sqrt(all_tokens)
    ffin_new = update(ffin_weight, own_gu, ffin_momentum, ffin_average, ffin_rate * inverse_root)
    ffout_new = update(
        ffout_weight, own_down, ffout_momentum, ffout_average, ffout_rate * inverse_root
    )
    ffin_new += (ffin_new[0].astype(bf16),)
    ffout_new += (ffout_new[0].astype(bf16),)
    attn_sum, ffin_new = lax.optimization_barrier((attn_sum, ffin_new))
    summed, sent = last_sum(core, attn_sum)
    arrived = core_swap(sent)
    arrived = lax.optimization_barrier((arrived, back_sum))[0]
    attn_new = attention_update(
        core,
        summed,
        arrived,
        attention_weight,
        attention_momentum,
        attention_average,
        [rate * inverse_root for rate in attention_rates],
    )
    back_halves = after(back_halves, attn_new[0])
    first_grad = finished(back_halves, [2 << turn for turn in range(1, chips.bit_length() - 2)])
    scale = rms_scale(flat_tokens)
    gained = first_grad * gains[0]
    inner = jnp.mean(gained * flat_tokens, axis=-1, keepdims=True)
    input_grad = mine(dmixed) + scale * gained - flat_tokens * (scale**3 * inner)

    small_own, small_their = summed[-small_rows:], arrived[-small_rows:]
    gains_reduced = (small_own[:4] + small_their[:4]).reshape(gains.shape)
    pairs = heads // 4
    heads_of = lambda value: value[4 : 4 + pairs, : 2 * lanes].reshape(heads // 2, lanes)[:, : bias_table.shape[0]]
    bias_reduced = jnp.concatenate(by_core(heads_of(small_own), heads_of(small_their)), axis=0).T

    gain_rate = jnp.array(gain_rates, dtype=f32)[:, None] * inverse_root
    bias_new = update(bias_table, bias_reduced, bias_momentum, bias_average, bias_rate * inverse_root)
    gain_new = update(gains, gains_reduced, gain_momentum, gain_average, gain_rate)
    return (
        layer_output.reshape(tokens.shape),
        input_grad.reshape(tokens.shape),
        attn_new[0],
        ffin_new[0],
        ffout_new[0],
        bias_new[0],
        gain_new[0],
        attn_new[1],
        ffin_new[1],
        ffout_new[1],
        bias_new[1],
        gain_new[1],
        attn_new[2],
        ffin_new[2],
        ffout_new[2],
        bias_new[2],
        gain_new[2],
        attn_new[3],
        ffin_new[3],
        ffout_new[3],
    )


def solution(mesh):
    rows = P("batch", "seq", None)
    stacked = P(None, ("seq", "batch"), None)
    single = P(("seq", "batch"), None)
    weights = (stacked, stacked, single, P(), P())
    return jax.shard_map(
        shards,
        mesh=mesh,
        in_specs=(rows, rows, P("batch", "seq")) + weights * 3,
        out_specs=(rows, rows) + weights * 3 + (stacked, stacked, single),
        check_vma=False,
    )
```

```python
import functools
import math

import jax
import jax.numpy as jnp
from jax import lax
from jax.experimental import pallas as pl
from jax.experimental.pallas import tpu as pltpu
from jax.sharding import PartitionSpec as P

eps_norm = 1e-06
momentum_coef = 0.5
average_coef = 0.5
attention_rates = (0.0033, 0.0033, 0.025, 0.2)
ffin_rate = 0.063
ffout_rate = 0.023
bias_rate = 0.08
gain_rates = (0.045, 0.22)
thresholds = (12, 16, 23, 32, 46, 64, 91)
masked_score = -1e30
gelu_scale = math.sqrt(2.0 / math.pi)
gelu_cubic = 0.044715
bf16 = jnp.bfloat16
f32 = jnp.float32
vmem_bytes = 60 * 1024 * 1024
lanes = 128


def product(left, right, left_dim, right_dim):
    return lax.dot_general(
        left, right, (((left_dim,), (right_dim,)), ((), ())), preferred_element_type=f32
    )


def mm(left, right):
    return product(left, right, 1, 0)


def mm_nt(left, right):
    return product(left, right, 1, 1)


def mm_tn(left, right):
    return product(left, right, 0, 0)


def bucket_of(offset):
    magnitude = jnp.abs(offset)
    beyond = jnp.zeros_like(offset)
    for threshold in thresholds:
        beyond = beyond + (magnitude >= threshold).astype(jnp.int32)
    inside = jnp.where(magnitude < 8, magnitude, 8 + beyond)
    return inside + 16 * (offset > 0).astype(jnp.int32)


def update(weight, grad, momentum, average, rate):
    new_momentum = momentum_coef * momentum + grad
    new_weight = weight - rate * (grad + momentum_coef * new_momentum)
    new_average = average_coef * average + (1.0 - average_coef) * new_weight
    return (new_weight, new_momentum, new_average)


def rms_scale(values):
    return lax.rsqrt(jnp.mean(values * values, axis=-1, keepdims=True) + eps_norm)


def params():
    return pltpu.CompilerParams(vmem_limit_bytes=vmem_bytes)


def any_spec():
    return pl.BlockSpec(memory_space=pl.ANY)


def cost(flops, nbytes, exps=0):
    return pl.CostEstimate(flops=1, bytes_accessed=1, transcendentals=0)


def bias_kernel(table_ref, out_ref):
    head = pl.program_id(0)
    spot = lax.broadcasted_iota(jnp.int32, (8, 2 * lanes), 1)
    for block in range(3):
        buckets = bucket_of(lanes * (block - 1) + lanes - 1 - spot)
        row = jnp.zeros((8, 2 * lanes), f32)
        for bucket in range(table_ref.shape[0]):
            row = jnp.where(buckets == bucket, table_ref[bucket, head], row)
        wide = jnp.broadcast_to(row[:1], (lanes, 2 * lanes))
        rolled = pltpu.roll(wide, lanes + 1, 1, stride=1, stride_axis=0)
        out_ref[0, lanes * (block + 1) : lanes * (block + 2), :] = rolled[:, :lanes]
    out_ref[0, 0:lanes, :] = jnp.full((lanes, lanes), table_ref[15, head], f32)
    out_ref[0, 4 * lanes : 5 * lanes, :] = jnp.full((lanes, lanes), table_ref[31, head], f32)


def bias_rows(table):
    heads = table.shape[1]
    return pl.pallas_call(
        bias_kernel,
        grid=(heads,),
        in_specs=[pl.BlockSpec(memory_space=pltpu.SMEM)],
        out_specs=pl.BlockSpec((1, 5 * lanes, lanes), lambda i: (i, 0, 0)),
        out_shape=jax.ShapeDtypeStruct((heads, 5 * lanes, lanes), f32),
        compiler_params=params(),
        cost_estimate=cost(heads * 3e6, 4e6),
        name="bias_rows",
    )(table)


def ready_kernel(meta_ref, attn_ref, ffin_ref, ffout_ref, tokens_ref, ids_ref, gain_ref, *outs):
    attn_out, attn_send, gu_out, gu_send, row_out = outs
    core = meta_ref[0]
    first = core == 0
    width = tokens_ref.shape[1]
    half = width // 2
    low = attn_ref[...].astype(bf16)
    left, right = low[..., :half], low[..., half:]
    attn_out[0:3, core] = jnp.where(first, left[:3], right[:3])
    attn_send[...] = jnp.where(first, right[:3], left[:3])
    attn_out[3, 0] = left[3]
    attn_out[3, 1] = right[3]
    grain = ffin_ref.shape[2] // (2 * meta_ref.shape[0])
    for index in range(meta_ref.shape[0]):
        start = 2 * index * grain
        even = ffin_ref[:, :, start : start + grain].astype(bf16)
        odd = ffin_ref[:, :, start + grain : start + 2 * grain].astype(bf16)
        cols = slice(index * grain, (index + 1) * grain)
        gu_out[:, core, :, cols] = jnp.where(first, even, odd)
        gu_send[:, :, cols] = jnp.where(first, odd, even)
    tok = tokens_ref.shape[0]
    tokens = tokens_ref[...]
    row_out[:tok, :] = (tokens * rms_scale(tokens) * gain_ref[0:1, :]).astype(bf16)
    ids = jnp.broadcast_to(ids_ref[...].astype(f32), (16, tok))
    ids = jnp.concatenate([ids, jnp.zeros((16, width - tok), f32)], axis=1)
    row_out[tok : tok + 16, :] = ids.astype(bf16)
    row_out[tok + 16 :, :] = ffout_ref[...].astype(bf16)


def make_ready(core, attention_weight, ffin_weight, ffout_weight, tokens, ids, gain, chips):
    tok, width = tokens.shape
    rows, half, hidden = attention_weight.shape[1], width // 2, ffin_weight.shape[2]
    return pl.pallas_call(
        ready_kernel,
        in_specs=[smem_spec()] + [whole_spec()] * 6,
        out_specs=[whole_spec()] * 5,
        out_shape=[
            shaped(bf16, 4, 2, rows, half),
            shaped(bf16, 3, rows, half),
            shaped(bf16, 2, 2, rows, hidden // 2),
            shaped(bf16, 2, rows, hidden // 2),
            shaped(bf16, tok + 16 + ffout_weight.shape[0], width),
        ],
        compiler_params=params(),
        cost_estimate=cost(1e6, 2e6),
        name="make_ready",
    )(jnp.broadcast_to(core, (chips,)), attention_weight, ffin_weight, ffout_weight, tokens, ids, gain)


def fill_kernel(core_ref, kept_ref, arrived_ref, out_ref):
    count = arrived_ref.shape[0]
    out_ref[...] = kept_ref[...]
    out_ref[0:count, 1 - core_ref[0]] = arrived_ref[...]


def fill(core, kept, arrived):
    return pl.pallas_call(
        fill_kernel,
        in_specs=[smem_spec(), whole_spec(), whole_spec()],
        out_specs=whole_spec(),
        out_shape=shaped(bf16, *kept.shape),
        compiler_params=params(),
        cost_estimate=cost(0, 1e6),
        name="fill",
    )(core.reshape(1), kept, arrived)


def row_block(meta_ref, slot, rows):
    start = meta_ref[slot] * rows
    return pl.ds(pl.multiple_of(start, 16) if rows % 16 == 0 else start, rows)


def run_copies(pairs, sem):
    copies = [pltpu.make_async_copy(a, b, sem.at[i]) for i, (a, b) in enumerate(pairs)]
    for copy in copies:
        copy.start()
    return copies


def wait_all(copies):
    for copy in copies:
        copy.wait()


def whole_spec():
    return pl.BlockSpec(memory_space=pltpu.VMEM)


def smem_spec():
    return pl.BlockSpec(memory_space=pltpu.SMEM)


def dma(count):
    return pltpu.SemaphoreType.DMA((count,))


def shaped(kind, *shape):
    return jax.ShapeDtypeStruct(shape, kind)


def rows_kernel(meta_ref, near_ref, far_ref, full_ref, turned_ref, mask_ref):
    chips = near_ref.shape[0]
    core = meta_ref[chips]
    groups = lambda block: block[lanes : lanes + 16, :lanes].astype(f32)[:1, :]
    mine, other = groups(near_ref[0]), groups(far_ref[0])
    chip_ids = jnp.where(
        core == 0,
        jnp.concatenate([mine, other], axis=1),
        jnp.concatenate([other, mine], axis=1),
    )
    for source, side in ((near_ref, core), (far_ref, 1 - core)):
        for step in range(chips):
            block = source[step]
            start = (meta_ref[step] * 2 + side) * lanes
            place = pl.ds(pl.multiple_of(start, lanes), lanes)
            normed = block[:lanes, :]
            full_ref[place, :] = normed
            turned_ref[:, place] = normed.T
            wide = jnp.broadcast_to(groups(block), (lanes, lanes)).T
            same = jnp.concatenate([wide, wide], axis=1) == chip_ids
            mask_ref[place, :] = jnp.where(same, 0.0, masked_score)


def place_rows(meta, near, far):
    chips, _, width = near.shape
    length = 2 * chips * lanes
    return pl.pallas_call(
        rows_kernel,
        in_specs=[smem_spec()] + [whole_spec()] * 2,
        out_specs=[whole_spec()] * 3,
        out_shape=[
            shaped(bf16, length, width),
            shaped(bf16, width, length),
            shaped(f32, length, 2 * lanes),
        ],
        compiler_params=params(),
        cost_estimate=cost(3e6, 8e6),
        name="place_rows",
    )(meta, near, far)


def one_head(matrix, half):
    first = lax.broadcasted_iota(jnp.int32, matrix.shape, 1) < matrix.shape[1] // 2
    return jnp.where(first if half == 0 else jnp.logical_not(first), matrix, jnp.zeros_like(matrix))


def band_place(block, chip, part):
    kind = jnp.clip(block - (2 * chip + part) + 2, 0, 4)
    return pl.ds(pl.multiple_of(kind * lanes, lanes), lanes)


def attend_kernel(count, meta_ref, rows_ref, mask_ref, bias_ref, *refs):
    pieces = refs[:count]
    q_ref, k_ref, v_ref, p_ref, o_ref, low_ref, out_rows = refs[count : count + 7]
    weight, score, soft, sem, out_sem = refs[count + 7 :]
    pair = pl.program_id(0)
    chip = meta_ref[0]
    length = rows_ref.shape[0]
    blocks = length // lanes
    group = 2 * lanes
    stacked = [(piece.at[3], out_rows.at[step]) for step, piece in enumerate(pieces)]

    @pl.when(pair == 0)
    def _():
        loads = run_copies(load_pairs(pieces, meta_ref, 0, weight), sem)
        run_copies(stacked, out_sem)
        wait_all(loads)

    cols = pl.ds(pl.multiple_of(pair * lanes, lanes), lanes)
    own = rows_ref[pl.ds(pl.multiple_of(chip * group, group), group), :]
    query = mm(own, weight[0, :, cols]).astype(bf16)
    both = jnp.concatenate([weight[1, :, cols], weight[2, :, cols]], axis=1)
    key_value = mm(rows_ref[...], both).astype(bf16)
    key, value = key_value[:, :lanes], key_value[:, lanes:]
    q_ref[...] = query
    k_ref[...] = key
    v_ref[...] = value
    score[...] = mm_nt(key, jnp.concatenate([one_head(query, half) for half in range(2)], axis=0))
    for half in range(2):
        lane = slice(half * group, (half + 1) * group)
        best = jnp.full((8, group), masked_score, f32)
        for block in range(blocks):
            rows = slice(block * lanes, (block + 1) * lanes)
            bias = [bias_ref[half, band_place(block, chip, part), :] for part in range(2)]
            now = score[rows, lane] + jnp.concatenate(bias, axis=1) + mask_ref[rows, :]
            score[rows, lane] = now
            best = jnp.maximum(best, jnp.max(now.reshape(lanes // 8, 8, group), axis=0))
        top = jnp.max(best, axis=0, keepdims=True)
        total = jnp.zeros((8, group), f32)
        for block in range(blocks):
            rows = slice(block * lanes, (block + 1) * lanes)
            now = jnp.exp(score[rows, lane] - top)
            score[rows, lane] = now
            total = total + jnp.sum(now.reshape(lanes // 8, 8, group), axis=0)
        inverse = 1.0 / jnp.sum(total, axis=0, keepdims=True)
        for block in range(blocks):
            rows = slice(block * lanes, (block + 1) * lanes)
            now = score[rows, lane] * inverse
            p_ref[half, rows, :] = now
            soft[rows, lane] = now.astype(bf16)
    features = lanes // 2
    both_turned = mm_tn(value, soft[...])
    turned = [both_turned[:features, :group], both_turned[features:, group:]]
    attended = jnp.concatenate(turned, axis=0).T
    o_ref[...] = attended
    low_ref[...] = attended.astype(bf16)

    @pl.when(pair == pl.num_programs(0) - 1)
    def _():
        wait_all([pltpu.make_async_copy(a, b, out_sem.at[i]) for i, (a, b) in enumerate(stacked)])


def attend(pieces, meta, rows, mask, bias):
    length, width = rows.shape
    half = width // 2
    group = 2 * lanes
    pairs = half // lanes
    col = lambda i, *_: (0, i)
    fixed = lambda i, *_: (0, 0)
    flops = 2 * (group * width * half + 2 * length * width * half + 4 * group * length * half)
    return pl.pallas_call(
        functools.partial(attend_kernel, len(pieces)),
        grid_spec=pltpu.PrefetchScalarGridSpec(
            num_scalar_prefetch=1,
            grid=(pairs,),
            in_specs=[
                pl.BlockSpec((length, width), fixed),
                pl.BlockSpec((length, group), fixed),
                pl.BlockSpec((2, 5 * lanes, lanes), lambda i, *_: (i, 0, 0)),
            ]
            + [any_spec()] * len(pieces),
            out_specs=[
                pl.BlockSpec((group, lanes), col),
                pl.BlockSpec((length, lanes), col),
                pl.BlockSpec((length, lanes), col),
                pl.BlockSpec((2, length, group), lambda i, *_: (i, 0, 0)),
                pl.BlockSpec((group, lanes), col),
                pl.BlockSpec((group, lanes), col),
                pl.BlockSpec((len(pieces),) + pieces[0].shape[1:], lambda i, *_: (0, 0, 0)),
            ],
            scratch_shapes=[
                pltpu.VMEM((3, width, half), bf16),
                pltpu.VMEM((length, 2 * group), f32),
                pltpu.VMEM((length, 2 * group), bf16),
                dma(len(pieces)),
                dma(len(pieces)),
            ],
        ),
        out_shape=[
            shaped(bf16, group, half),
            shaped(bf16, length, half),
            shaped(bf16, length, half),
            shaped(f32, 2 * pairs, length, group),
            shaped(f32, group, half),
            shaped(bf16, group, half),
            shaped(bf16, len(pieces), *pieces[0].shape[1:]),
        ],
        compiler_params=params(),
        cost_estimate=cost(flops, 30e6, 2 * group * length * pairs),
        name="attend",
    )(meta, rows, mask, bias, *pieces)


def mix_kernel(
    meta_ref, tokens_ref, own_ref, their_ref, gain_ref, near_ref, far_ref, mixed_ref, normed_ref, turned_ref, joined_ref, weight_ref, held, sem
):
    chips, rows, half = near_ref.shape
    rows = rows // 2
    pairs = []
    for index, source in enumerate((near_ref, far_ref)):
        for step in range(chips):
            place = row_block(meta_ref, 1 + index * chips + step, rows)
            for side in range(2):
                pairs.append(
                    (
                        source.at[step, side * rows : (side + 1) * rows, :],
                        weight_ref.at[place, side * half : (side + 1) * half],
                    )
                )
    copies = run_copies(pairs, sem)
    first = meta_ref[0] == 0
    held[:, :half] = jnp.where(first, own_ref[...], their_ref[...])
    held[:, half:] = jnp.where(first, their_ref[...], own_ref[...])
    joined_ref[...] = held[...].T
    wait_all(copies)
    mixed = tokens_ref[...] + mm(held[...], weight_ref[...])
    mixed_ref[...] = mixed
    normed = (mixed * rms_scale(mixed) * gain_ref[...]).astype(bf16)
    normed_ref[...] = normed
    turned_ref[...] = normed.T


def mix(meta, tokens, own, their, gain, near, far):
    group, half = own.shape
    width = 2 * half
    return pl.pallas_call(
        mix_kernel,
        in_specs=[smem_spec()] + [whole_spec()] * 4 + [any_spec()] * 2,
        out_specs=[whole_spec()] * 5,
        out_shape=[
            shaped(f32, group, width),
            shaped(bf16, group, width),
            shaped(bf16, width, group),
            shaped(bf16, width, group),
            shaped(bf16, width, width),
        ],
        scratch_shapes=[pltpu.VMEM((group, width), bf16), dma(4 * near.shape[0])],
        compiler_params=params(),
        cost_estimate=cost(4 * group * width * half, 4e6),
        name="mix",
    )(meta, tokens, own, their, gain, near, far)


def feed_kernel(
    chips,
    places,
    gu_count,
    meta_ref,
    normed_low,
    turned_low,
    cot_ref,
    *refs,
):
    refs = list(refs)
    take = lambda n: [refs.pop(0) for _ in range(n)]
    gu_pieces = take(gu_count)
    down_pieces = take(places)
    out_ref, back_ref = take(2)
    gu_outs, down_outs = take(chips), take(2)
    gu, down, grad_gu, grad_down, cot_low = take(5)
    gu_sem, down_sem, gu_out_sem, down_out_sem = take(4)
    step = pl.program_id(0)
    steps = pl.num_programs(0)
    block = 512

    count = gu.shape[2] // block

    def gu_loads(turn):
        columns = pl.ds(pl.multiple_of(turn * block, block), block)
        pairs = []
        for index, piece in enumerate(gu_pieces):
            place = row_block(meta_ref, min(index, chips - 1), piece.shape[1])
            lead = slice(0, 2) if piece.shape[0] == 2 else slice(index - 3, index - 2)
            pairs.append((piece.at[:, :, columns], gu.at[lead, place, columns]))
        return [
            pltpu.make_async_copy(a, b, gu_sem.at[turn, index]) for index, (a, b) in enumerate(pairs)
        ]

    def gu_stores(turn):
        columns = pl.ds(pl.multiple_of(turn * block, block), block)
        copies = []
        for chip, out in enumerate(gu_outs):
            source = grad_gu.at[:, row_block(meta_ref, chip, out.shape[1]), columns]
            copies.append(pltpu.make_async_copy(source, out.at[:, :, columns], gu_out_sem.at[turn, chip]))
        return copies

    @pl.when(step == 0)
    def _():
        for copy in gu_loads(0):
            copy.start()
        pairs = []
        slot = chips
        for piece in down_pieces:
            for chip in range(chips):
                pairs.append((piece.at[chip], down.at[row_block(meta_ref, slot, piece.shape[1]), :]))
                slot += 1
        down_copies = run_copies(pairs, down_sem)
        for turn in range(1, count):
            for copy in gu_loads(turn):
                copy.start()
        cot_low[...] = cot_ref[...].astype(bf16)
        out_ref[...] = jnp.zeros_like(out_ref)
        back_ref[...] = jnp.zeros_like(back_ref)
        wait_all(down_copies)

    for copy in gu_loads(step):
        copy.wait()
    cols = pl.ds(pl.multiple_of(step * block, block), block)
    normed = normed_low[...]
    cot = cot_low[...]
    gate_w, up_w, down_w = gu[0, :, cols], gu[1, :, cols], down[cols, :]
    gate, up = mm(normed, gate_w), mm(normed, up_w)
    square = gate * gate
    curve = jnp.tanh(gelu_scale * gate * (1.0 + gelu_cubic * square))
    half = 0.5 * (1.0 + curve)
    gelu = gate * half
    slope = half + 0.5 * gate * (1.0 - curve * curve) * gelu_scale * (1.0 + 3.0 * gelu_cubic * square)
    hidden = (gelu * up).astype(bf16)
    dh = mm_nt(cot, down_w)
    dgate = (dh * up * slope).astype(bf16)
    dup = (dh * gelu).astype(bf16)
    out_ref[...] += mm(hidden, down_w)
    back_ref[...] += mm_nt(dgate, gate_w) + mm_nt(dup, up_w)
    grad_down[cols, :] = mm_tn(hidden, cot).astype(bf16)
    both = mm(turned_low[...], jnp.concatenate([dgate, dup], axis=1)).astype(bf16)
    grad_gu[0, :, cols] = both[:, :block]
    grad_gu[1, :, cols] = both[:, block:]

    for copy in gu_stores(step):
        copy.start()

    @pl.when(step == steps - 1)
    def _():
        pairs = []
        for turn, out in enumerate(down_outs):
            for spot in range(places // 2):
                for chip in range(chips):
                    slot = chips * (1 + places + turn * (places // 2) + spot) + chip
                    place = row_block(meta_ref, slot, out.shape[2])
                    pairs.append((grad_down.at[place, :], out.at[spot, chip]))
        down_copies = run_copies(pairs, down_out_sem)
        for turn in range(count):
            wait_all(gu_stores(turn))
        wait_all(down_copies)


def feed(gu_pieces, down_pieces, meta, normed, turned, cot, chips, places):
    group, width = normed.shape
    hidden = gu_pieces[0].shape[2]
    block = 512
    fixed = lambda i, *_: (0, 0)
    full = lambda *shape: pl.BlockSpec(shape, fixed)
    flops = 2 * 9 * group * width * hidden
    results = pl.pallas_call(
        functools.partial(feed_kernel, chips, places, len(gu_pieces)),
        grid_spec=pltpu.PrefetchScalarGridSpec(
            num_scalar_prefetch=1,
            grid=(hidden // block,),
            in_specs=[full(group, width), full(width, group), full(group, width)]
            + [any_spec()] * (len(gu_pieces) + places),
            out_specs=[full(group, width)] * 2 + [any_spec()] * (chips + 2),
            scratch_shapes=[
                pltpu.VMEM((2, width, hidden), bf16),
                pltpu.VMEM((hidden, width), bf16),
                pltpu.VMEM((2, width, hidden), bf16),
                pltpu.VMEM((hidden, width), bf16),
                pltpu.VMEM((group, width), bf16),
                pltpu.SemaphoreType.DMA((hidden // block, len(gu_pieces))),
                dma(chips * places),
                pltpu.SemaphoreType.DMA((hidden // block, chips)),
                dma(chips * places),
            ],
        ),
        out_shape=[shaped(f32, group, width)] * 2
        + [shaped(bf16, 2, width // chips, hidden)] * chips
        + [shaped(bf16, places // 2, chips, hidden // (chips * places), width)] * 2,
        compiler_params=params(),
        cost_estimate=cost(flops, 25e6, group * hidden),
        name="feed",
    )(meta, normed, turned, cot, *gu_pieces, *down_pieces)
    return results[:2], results[2 : 2 + chips], results[2 + chips :]


def settle_kernel(
    meta_ref,
    mixed_ref,
    cot_ref,
    back_ref,
    arrived_ref,
    weight_ref,
    gain_ref,
    dmixed_ref,
    do_ref,
    gain_grad_ref,
    branch_ref,
):
    core = meta_ref[0]
    half = do_ref.shape[1]
    mixed = mixed_ref[...]
    scale = rms_scale(mixed)
    dn2 = back_ref[...] + arrived_ref[...]
    gained = dn2 * gain_ref[...]
    inner = jnp.mean(gained * mixed, axis=-1, keepdims=True)
    dmixed = cot_ref[...] + scale * gained - mixed * (scale * scale * scale * inner)
    dmixed_ref[...] = dmixed
    gain_grad_ref[...] = 0.5 * jnp.sum(dn2 * mixed * scale, axis=0, keepdims=True)
    branch = dmixed.astype(bf16)
    branch_ref[...] = branch
    mine = weight_ref[pl.ds(pl.multiple_of(core * half, half), half), :]
    do_ref[...] = mm_nt(branch, mine).astype(bf16)


def settle(meta, mixed, cot, back, arrived, weight, gain):
    group, width = mixed.shape
    half = width // 2
    return pl.pallas_call(
        settle_kernel,
        in_specs=[smem_spec()] + [whole_spec()] * 6,
        out_specs=[whole_spec()] * 4,
        out_shape=[
            shaped(f32, group, width),
            shaped(bf16, group, half),
            shaped(f32, 1, width),
            shaped(bf16, group, width),
        ],
        compiler_params=params(),
        cost_estimate=cost(2 * group * width * half, 6e6),
        name="settle",
    )(meta, mixed, cot, back, arrived, weight, gain)


def band_rows(band_ref):
    line = lax.broadcasted_iota(jnp.int32, (8, 2 * lanes), 0)
    none = jnp.zeros((8, lanes), f32)
    found = []
    for block in range(3):
        summed = jnp.zeros((8, 2 * lanes), f32)
        for part in range(lanes // 8):
            start = lanes * (block + 1) + 8 * part
            wide = jnp.concatenate([band_ref[start : start + 8, :], none], axis=1)
            move = lanes - 8 - 8 * part
            summed = summed + (pltpu.roll(wide, move, 1) if move else wide)
        for bit in range(3):
            step = 1 << bit
            summed = jnp.where((line & step) == 0, pltpu.roll(summed, step, 1), summed)
        found.append(jnp.sum(summed, axis=0, keepdims=True))
    return jnp.concatenate(found, axis=1)


def retreat_kernel(meta_ref, do_ref, o_ref, q_ref, k_ref, v_ref, p_ref, dq_ref, dkv_ref, bias_ref, low, soft_low, spread_of, band_ref, onehot):
    chip = meta_ref[0]
    blocks = k_ref.shape[0] // lanes
    group = 2 * lanes
    features = lanes // 2
    do = do_ref[...]
    spread = (do.astype(f32) * o_ref[...]).T
    band_ref[...] = jnp.zeros_like(band_ref)
    far = jnp.zeros((8, lanes), f32)
    rows_of = []

    @pl.when(pl.program_id(0) == 0)
    def _():
        bucket = lax.broadcasted_iota(jnp.int32, (6 * lanes, lanes), 1)
        spot = lax.broadcasted_iota(jnp.int32, (6 * lanes, lanes), 0)
        offset = lanes * (spot // (2 * lanes)) - 1 - spot % (2 * lanes)
        onehot[...] = (bucket_of(offset) == bucket).astype(f32)

    do_two = jnp.concatenate([one_head(do, half) for half in range(2)], axis=0)
    query_two = jnp.concatenate([one_head(q_ref[...], half) for half in range(2)], axis=0)
    spread_of[...] = mm_nt(v_ref[...], do_two)
    for half in range(2):
        lane = slice(half * group, (half + 1) * group)
        delta = jnp.sum(spread[half * features : (half + 1) * features], axis=0, keepdims=True)
        for block in range(blocks):
            rows = slice(block * lanes, (block + 1) * lanes)
            soft = p_ref[half, rows, :]
            ds = soft * (spread_of[rows, lane] - delta)
            for part in range(2):
                place = band_place(block, chip, part)
                band_ref[place, :] += ds[:, part * lanes : (part + 1) * lanes]
            low[rows, lane] = ds.astype(bf16)
            soft_low[rows, lane] = soft.astype(bf16)
        rows_of.append(band_rows(band_ref))
        low_sum = jnp.sum(band_ref[0:lanes, :])
        high_sum = jnp.sum(band_ref[4 * lanes : 5 * lanes, :])
        lane_id = lax.broadcasted_iota(jnp.int32, (8, lanes), 1)
        line = lax.broadcasted_iota(jnp.int32, (8, lanes), 0)
        far = far + jnp.where((lane_id == 15) & (line == half), low_sum, 0.0)
        far = far + jnp.where((lane_id == 31) & (line == half), high_sum, 0.0)
        if half == 0:
            band_ref[...] = jnp.zeros_like(band_ref)
    dkv_ref[:, :lanes] = mm(low[...], query_two).astype(bf16)
    dkv_ref[:, lanes:] = mm(soft_low[...], do_two).astype(bf16)
    both_turned = mm_tn(k_ref[...], low[...])
    turned = [both_turned[:features, :group], both_turned[features:, group:]]
    dq_ref[...] = jnp.concatenate(turned, axis=0).T.astype(bf16)
    rows_of.append(jnp.zeros((6, rows_of[0].shape[1]), f32))
    near = lax.dot_general(
        jnp.concatenate(rows_of, axis=0),
        onehot[...],
        (((1,), (0,)), ((), ())),
        precision=lax.Precision.HIGHEST,
        preferred_element_type=f32,
    )
    bias_ref[0] = near + far


def retreat(meta, do, o, q, k, v, p):
    length, half = k.shape
    group = do.shape[0]
    pairs = half // lanes
    col = lambda i, *_: (0, i)
    deep = lambda i, *_: (i, 0, 0)
    flops = 2 * 8 * group * length * half
    return pl.pallas_call(
        retreat_kernel,
        grid_spec=pltpu.PrefetchScalarGridSpec(
            num_scalar_prefetch=1,
            grid=(pairs,),
            in_specs=[
                pl.BlockSpec((group, lanes), col),
                pl.BlockSpec((group, lanes), col),
                pl.BlockSpec((group, lanes), col),
                pl.BlockSpec((length, lanes), col),
                pl.BlockSpec((length, lanes), col),
                pl.BlockSpec((2, length, group), deep),
            ],
            out_specs=[
                pl.BlockSpec((group, lanes), col),
                pl.BlockSpec((length, 2 * lanes), col),
                pl.BlockSpec((1, 8, lanes), deep),
            ],
            scratch_shapes=[
                pltpu.VMEM((length, 2 * group), bf16),
                pltpu.VMEM((length, 2 * group), bf16),
                pltpu.VMEM((length, 2 * group), f32),
                pltpu.VMEM((5 * lanes, lanes), f32),
                pltpu.VMEM((6 * lanes, lanes), f32),
            ],
        ),
        out_shape=[
            shaped(bf16, group, half),
            shaped(bf16, length, 2 * half),
            shaped(f32, pairs, 8, lanes),
        ],
        compiler_params=params(),
        cost_estimate=cost(flops, 20e6),
        name="retreat",
    )(meta, do, o, q, k, v, p)


small_rows = 16


def load_pairs(pieces, meta_ref, first, weight):
    pairs = []
    for step, piece in enumerate(pieces):
        place = row_block(meta_ref, first + step, piece.shape[1])
        pairs.append((piece.at[0:3], weight.at[:, place, :]))
    return pairs


def grads_kernel(
    chips, meta_ref, turned_ref, dq_ref, dkv_ref, gains_ref, second_ref, bias_ref, joined_ref, branch_ref, *refs
):
    refs = list(refs)
    take = lambda n: [refs.pop(0) for _ in range(n)]
    pieces, outs = take(chips), take(chips)
    weight, grad, wo, small, sem, out_sem = take(6)
    chip, core = meta_ref[0], meta_ref[1]
    width = turned_ref.shape[0]
    half = width // 2
    group = dq_ref.shape[0]
    loads = run_copies(load_pairs(pieces, meta_ref, 2, weight), sem)
    wo_rows = wo.shape[1]
    mine = []
    for index in range(chips):
        even = joined_ref[2 * index * wo_rows : (2 * index + 1) * wo_rows, :]
        odd = joined_ref[(2 * index + 1) * wo_rows : (2 * index + 2) * wo_rows, :]
        mine.append(jnp.where(core == 0, even, odd))
    out_grad = mm(jnp.concatenate(mine, axis=0), branch_ref[...]).astype(bf16)
    for index in range(chips):
        wo[index] = out_grad[index * wo_rows : (index + 1) * wo_rows]
    own_rows = pl.ds(pl.multiple_of(chip * group, group), group)
    query_grad = mm(turned_ref[:, own_rows], dq_ref[...])
    grad[0] = query_grad.astype(bf16)
    wait_all(loads)
    along_row = [query_grad[:, at : at + lanes] * weight[0, :, at : at + lanes].astype(f32) for at in range(0, half, lanes)]
    along_row = sum(along_row[1:], along_row[0])
    for pair in range(half // lanes):
        wide = slice(pair * 2 * lanes, (pair + 1) * 2 * lanes)
        cols = slice(pair * lanes, (pair + 1) * lanes)
        summed = mm(turned_ref[...], dkv_ref[:, wide])
        low = summed.astype(bf16)
        grad[1, :, cols] = low[:, :lanes]
        grad[2, :, cols] = low[:, lanes:]
        along_row = along_row + summed[:, :lanes] * weight[1, :, cols].astype(f32)
        along_row = along_row + summed[:, lanes:] * weight[2, :, cols].astype(f32)
    first_gain = jnp.sum(along_row.T, axis=0, keepdims=True) / gains_ref[...]
    second_gain = second_ref[...]
    lines = [first_gain[:, :half], first_gain[:, half:], second_gain[:, :half], second_gain[:, half:]]
    for pair in range(bias_ref.shape[0]):
        both = [bias_ref[pair, 0:1, :], bias_ref[pair, 1:2, :]]
        both.append(jnp.zeros((1, half - 2 * lanes), f32))
        lines.append(jnp.concatenate(both, axis=1))
    lines.append(jnp.zeros((small_rows - len(lines), half), f32))
    small[...] = jnp.concatenate(lines, axis=0).astype(bf16)
    rows = width // chips
    side_rows = rows // 2
    pairs = []
    for step, out in enumerate(outs):
        place = row_block(meta_ref, 2 + step, rows)
        at = 0
        for matrix in range(3):
            pairs.append((grad.at[matrix, place, :], out.at[at : at + rows, :]))
            at += rows
        for side in range(2):
            source = wo.at[meta_ref[2 + step], :, side * half : (side + 1) * half]
            pairs.append((source, out.at[at : at + side_rows, :]))
            at += side_rows
        pairs.append((small, out.at[at : at + small_rows, :]))
    wait_all(run_copies(pairs, out_sem))


def weight_grads(pieces, meta, turned, dq, dkv, gain, second, bias, joined, branch, chips):
    width, length = turned.shape
    half = width // 2
    group = dq.shape[0]
    flops = 2 * (2 * length * width * half + group * width * half)
    block = width // chips
    return pl.pallas_call(
        functools.partial(grads_kernel, chips),
        in_specs=[smem_spec()] + [whole_spec()] * 8 + [any_spec()] * len(pieces),
        out_specs=[any_spec()] * chips,
        out_shape=[shaped(bf16, 4 * block + small_rows, half)] * chips,
        scratch_shapes=[
            pltpu.VMEM((3, width, half), bf16),
            pltpu.VMEM((3, width, half), bf16),
            pltpu.VMEM((chips, block // 2, width), bf16),
            pltpu.VMEM((small_rows, half), bf16),
            dma(chips),
            dma(6 * chips),
        ],
        compiler_params=params(),
        cost_estimate=cost(flops, 12e6),
        name="weight_grads",
    )(meta, turned, dq, dkv, gain, second, bias, joined, branch, *pieces)


def back_kernel(chips, meta_ref, dq_ref, dkv_ref, *refs):
    refs = list(refs)
    take = lambda n: [refs.pop(0) for _ in range(n)]
    pieces = take(chips)
    near_out, far_out = take(2)
    weight, both, back, sem = take(4)
    chip, core = meta_ref[0], meta_ref[1]
    length = dkv_ref.shape[0]
    half = dq_ref.shape[1]
    group = dq_ref.shape[0]
    wait_all(run_copies(load_pairs(pieces, meta_ref, 2, weight), sem))
    for pair in range(half // lanes):
        wide = pair * 2 * lanes
        cols = slice(pair * lanes, (pair + 1) * lanes)
        both[:, wide : wide + lanes] = weight[1, :, cols]
        both[:, wide + lanes : wide + 2 * lanes] = weight[2, :, cols]
    for start in range(0, length, group):
        back[start : start + group, :] = mm_nt(dkv_ref[start : start + group, :], both[...])
    own_rows = pl.ds(pl.multiple_of(chip * group, group), group)
    back[own_rows, :] += mm_nt(dq_ref[...], weight[0])
    for index, step in enumerate(bit_reversed(chips)):
        for side, out in ((core, near_out), (1 - core, far_out)):
            start = meta_ref[2 + step] * group + side * lanes
            out[index] = back[pl.ds(pl.multiple_of(start, lanes), lanes), :].astype(bf16)


def row_grads(pieces, meta, dq, dkv, chips):
    length, width = dkv.shape
    half = width // 2
    return pl.pallas_call(
        functools.partial(back_kernel, chips),
        in_specs=[smem_spec()] + [whole_spec()] * 2 + [any_spec()] * len(pieces),
        out_specs=[whole_spec()] * 2,
        out_shape=[shaped(bf16, chips, lanes, width)] * 2,
        scratch_shapes=[
            pltpu.VMEM((3, width, half), bf16),
            pltpu.VMEM((width, width), bf16),
            pltpu.VMEM((length, width), f32),
            dma(chips),
        ],
        compiler_params=params(),
        cost_estimate=cost(4 * length * width * half, 8e6),
        name="row_grads",
    )(meta, dq, dkv, *pieces)


def cut_kernel(side_ref, *refs):
    sources, (kept_ref, sent_ref) = refs[:-2], refs[-2:]
    count = kept_ref.shape[2]
    for index, out in ((side_ref[0], kept_ref), (1 - side_ref[0], sent_ref)):
        for part in range(2):
            start = pl.multiple_of((2 * part + index) * count, count)
            out[0, part] = total([source[0, pl.ds(start, count), :] for source in sources]).astype(bf16)


def cut_plane(blocks, side):
    lead, height, width = blocks[0].shape
    shape = (lead, 2, height // 4, width)
    row = lambda *shape: pl.BlockSpec((1,) + shape, lambda i: (i,) + (0,) * len(shape))
    return pl.pallas_call(
        cut_kernel,
        grid=(lead,),
        in_specs=[smem_spec()] + [row(height, width)] * len(blocks),
        out_specs=[row(*shape[1:])] * 2,
        out_shape=[shaped(bf16, *shape)] * 2,
        compiler_params=params(),
        cost_estimate=cost(1e6, 6e6),
        name="cut_plane",
    )(side.reshape(1), *blocks)


def sum_kernel(order_ref, *refs):
    places = order_ref.shape[0]
    sources, outs, total_ref = refs[: -1 - places], refs[-1 - places : -1], refs[-1]
    total_ref[...] = total([source[...] for source in sources])
    height = total_ref.shape[0] - small_rows
    rows = height // (8 * places)
    last = total_ref[height:, :]
    for turn, out in enumerate(outs):
        parts = []
        for block in range(8):
            start = block * places * rows + order_ref[turn] * rows
            parts.append(total_ref[pl.ds(pl.multiple_of(start, 8), rows), :])
        out[...] = jnp.concatenate(parts + [last], axis=0).astype(bf16)


def sum_plane(blocks, order):
    height, half = blocks[0].shape
    places = order.shape[0]
    rows = (height - small_rows) // (8 * places)
    if rows % 8:
        summed = total(blocks).astype(bf16)
        split, last = summed[:-small_rows].reshape(8, places, rows, half), summed[-small_rows:]
        pick = lambda turn: lax.dynamic_index_in_dim(split, order[turn], 1, keepdims=False)
        return [jnp.concatenate([pick(turn).reshape(-1, half), last], axis=0) for turn in range(places)]
    return pl.pallas_call(
        sum_kernel,
        in_specs=[smem_spec()] + [whole_spec()] * len(blocks),
        out_specs=[whole_spec()] * places,
        out_shape=[shaped(bf16, (height - small_rows) // places + small_rows, half)] * places,
        scratch_shapes=[pltpu.VMEM((height, half), f32)],
        compiler_params=params(),
        cost_estimate=cost(1e6, 4e6),
        name="sum_plane",
    )(order, *blocks)


def last_kernel(core_ref, *refs):
    sources, (sum_ref, sent_ref) = refs[:-2], refs[-2:]
    summed = total([source[...] for source in sources])
    sum_ref[...] = summed
    rows = (summed.shape[0] - small_rows) // 8
    first = core_ref[0] == 0
    block = lambda index: summed[index * rows : (index + 1) * rows]
    parts = [jnp.where(first, block(2 * matrix + 1), block(2 * matrix)) for matrix in range(3)]
    sent_ref[...] = jnp.concatenate(parts + [summed[8 * rows :]], axis=0)


def last_sum(core, arrived):
    height, half = arrived[0].shape
    rows = (height - small_rows) // 8
    return pl.pallas_call(
        last_kernel,
        in_specs=[smem_spec()] + [whole_spec()] * len(arrived),
        out_specs=[whole_spec()] * 2,
        out_shape=[shaped(f32, height, half), shaped(f32, 3 * rows + small_rows, half)],
        compiler_params=params(),
        cost_estimate=cost(1e6, 1e6),
        name="last_sum",
    )(core.reshape(1), *arrived)


def attention_kernel(
    rates, core_ref, sum_ref, arrived_ref, weight_ref, momentum_ref, average_ref, *outs
):
    new_weight, new_momentum, new_average, copy = outs
    rows, width = weight_ref.shape[1:]
    half = width // 2
    first = core_ref[0] == 0
    block = lambda index: sum_ref[index * rows : (index + 1) * rows, :]
    for matrix in range(4):
        left, right = block(2 * matrix), block(2 * matrix + 1)
        if matrix < 3:
            mine = jnp.where(first, left, right)
            theirs = arrived_ref[matrix * rows : (matrix + 1) * rows, :]
            left, right = jnp.where(first, mine, theirs), jnp.where(first, theirs, mine)
        for side, grad in enumerate((left, right)):
            at = (matrix, slice(None), slice(side * half, (side + 1) * half))
            values = update(
                weight_ref[at], grad, momentum_ref[at], average_ref[at], rates[matrix]
            )
            new_weight[at], new_momentum[at], new_average[at] = values
            copy[at] = values[0].astype(bf16)


def attention_update(core, summed, arrived, weight, momentum, average, rates):
    return pl.pallas_call(
        functools.partial(attention_kernel, rates),
        in_specs=[smem_spec()] + [whole_spec()] * 5,
        out_specs=[whole_spec()] * 4,
        out_shape=[shaped(f32, *weight.shape)] * 3 + [shaped(bf16, *weight.shape)],
        compiler_params=params(),
        cost_estimate=cost(1e6, 2e6),
        name="attention_update",
    )(core.reshape(1), summed, arrived, weight, momentum, average)


def core_swap(value):
    count = lax.axis_size("seq")
    return lax.ppermute(value, "seq", [(i, i ^ 1) for i in range(count)])


def plane_swap(value, step):
    count = lax.axis_size("seq")
    return lax.ppermute(value, "seq", [(i, i ^ (2 * step)) for i in range(count)])


def along(value, step):
    count = lax.axis_size("batch")
    return lax.ppermute(value, "batch", [(i, (i + step) % count) for i in range(count)])


def along_all(value):
    return [value] + [along(value, step) for step in range(1, lax.axis_size("batch"))]


def after(value, *earlier):
    return lax.optimization_barrier((value,) + earlier)[0]


def join_kernel(order_ref, *refs):
    sources, out = refs[:-1], refs[-1]
    for index, source in enumerate(sources):
        out[:, :, order_ref[index]] = source[...]


def join(blocks, order):
    lead, rest = blocks[0].shape[:2], blocks[0].shape[2:]
    return pl.pallas_call(
        join_kernel,
        in_specs=[smem_spec()] + [whole_spec()] * len(blocks),
        out_specs=whole_spec(),
        out_shape=shaped(bf16, *lead, len(blocks), *rest),
        compiler_params=params(),
        cost_estimate=cost(0, 2e6),
        name="join",
    )(order, *blocks)


def gather_plane(value):
    return [value] + [plane_swap(value, step) for step in range(1, lax.axis_size("seq") // 2)]


def total(blocks):
    summed = blocks[0].astype(f32)
    for block in blocks[1:]:
        summed = summed + block.astype(f32)
    return summed


def scatter_plane(blocks):
    return [blocks[0]] + [plane_swap(part, step) for step, part in enumerate(blocks) if step]


def bit_reversed(chips):
    order = [0]
    while len(order) < chips:
        order = [2 * step for step in order] + [2 * step + 1 for step in order]
    return order


def halves_along(value, dim, place):
    count = value.shape[dim] // 2
    split = value.reshape(value.shape[:dim] + (2, count) + value.shape[dim + 1 :])
    side = (place // count) % 2
    pick = lambda index: lax.dynamic_index_in_dim(split, index, dim, keepdims=False)
    return pick(side), pick(1 - side)


def across(value, step):
    count = lax.axis_size("batch")
    return lax.ppermute(value, "batch", [(i, i ^ step) for i in range(count)])


def halved(blocks, step):
    count = blocks.shape[0] // 2
    return blocks[:count], plane_swap(blocks[count:], step)


def summed_half(halves):
    return total(halves).astype(bf16)


def finished(halves, steps):
    for step in steps:
        halves = halved(summed_half(halves), step)
    return total(halves)[0]


def spread(values):
    return [values[0]] + [along(value, step) for step, value in enumerate(values) if step]


def spread_along(split, dim, place):
    count = lax.axis_size("batch")
    pick = lambda step: lax.dynamic_index_in_dim(split, (place + step) % count, dim, keepdims=False)
    return [pick(0)] + [along(pick(step), step) for step in range(1, count)]


def shards(
    tokens,
    cotangent,
    group_ids,
    attention_weight,
    ffin_weight,
    ffout_weight,
    bias_table,
    gains,
    attention_momentum,
    ffin_momentum,
    ffout_momentum,
    bias_momentum,
    gain_momentum,
    attention_average,
    ffin_average,
    ffout_average,
    bias_average,
    gain_average,
):
    _, tok, width = tokens.shape
    cycle_size, places = lax.axis_size("seq"), lax.axis_size("batch")
    cycle_index = lax.axis_index("seq").astype(jnp.int32)
    place = lax.axis_index("batch").astype(jnp.int32)
    chips = cycle_size // 2
    chip, core = cycle_index // 2, cycle_index % 2
    half = width // 2
    rows = attention_weight.shape[1]
    down_rows = ffout_weight.shape[0]
    hidden = ffin_weight.shape[2]
    grain = hidden // cycle_size
    heads = bias_table.shape[1]
    group = 2 * tok
    first_core = core == 0

    def by_core(mine, theirs):
        return [jnp.where(first_core, mine, theirs), jnp.where(first_core, theirs, mine)]

    steps = [chip ^ step for step in range(chips)]
    order = jnp.stack([(place + places - step) % places for step in range(places)])
    onward = jnp.stack([(place + step) % places for step in range(places)])
    flat_tokens, flat_cot = tokens.reshape(tok, width), cotangent.reshape(tok, width)

    attn_kept, attn_sent, gu_kept, gu_sent, row_block_own = make_ready(
        core,
        attention_weight,
        ffin_weight,
        ffout_weight,
        flat_tokens,
        group_ids,
        gains,
        chips,
    )
    their_tokens, their_cot = core_swap(flat_tokens), core_swap(flat_cot)
    attn_from, gu_from = core_swap(attn_sent), core_swap(gu_sent)
    row_block_own, attn_kept = lax.optimization_barrier((row_block_own, attn_kept, their_tokens, their_cot))[:2]
    attn_block = fill(core, after(attn_kept, gu_from), attn_from)
    gu_block = fill(core, gu_kept, gu_from)

    attn_blocks = along_all(attn_block)
    row_blocks, step = row_block_own[None], 1
    while step < chips:
        arrived = plane_swap(row_blocks, step)
        arrived = after(arrived, attn_block if step * 2 < chips else attn_blocks)
        row_blocks = jnp.concatenate([row_blocks, arrived], axis=0)
        step *= 2
    near_rows, down_block = row_blocks[:, : tok + 16], row_blocks[:, tok + 16 :]
    own_heads = jnp.where(first_core, bias_table[:, : heads // 2], bias_table[:, heads // 2 :])
    bias = bias_rows(after(own_heads, attn_block))

    attn_joined = join(after(attn_blocks, near_rows, bias, gu_block), order).reshape(4, 2 * places * rows, half)
    chip_tokens = jnp.concatenate(by_core(flat_tokens, their_tokens), axis=0)
    chip_cot = jnp.concatenate(by_core(flat_cot, their_cot), axis=0)
    far_rows = core_swap(after(near_rows, attn_joined))
    rows_full, turned, mask = place_rows(jnp.stack(steps + [core]), near_rows, far_rows)
    attn_pieces = gather_plane(attn_joined)
    gu_blocks = [after(gu_block, attn_joined)]
    for step in range(1, places):
        if step == 2:
            gu_blocks[-1], down_block = lax.optimization_barrier((gu_blocks[-1], down_block, far_rows))[:2]
        if step == 3:
            gu_blocks[-1] = after(gu_blocks[-1], rows_full)
        gu_blocks.append(along(gu_blocks[-1], 1))
    down_pieces = [down_block, along(down_block, 1)]
    gu_joined = join(gu_blocks, order)
    attn_pieces, rows_full, gu_joined, down_pieces = lax.optimization_barrier(
        (attn_pieces, rows_full, gu_joined, down_pieces)
    )
    chip_tokens, chip_cot, mask = lax.optimization_barrier((chip_tokens, chip_cot, mask))
    gu_joined, down_pieces, mask = lax.optimization_barrier((gu_joined, down_pieces, mask))
    down_pieces.append(along(down_pieces[-1], 1))
    gu_own = gu_joined.reshape(2, 2 * places * rows, hidden // 2)
    gu_pieces = [gu_own] + [plane_swap(gu_own, step) for step in range(1, 3 if chips == 4 else chips)]
    step_meta = jnp.stack(steps)
    query, key, value, soft, attended, attended_low, wo_near = attend(
        attn_pieces, step_meta, rows_full, mask, bias
    )
    wo_meta = jnp.stack([core] + [step * 2 + core for step in steps] + [step * 2 + 1 - core for step in steps])
    their_attended = core_swap(attended_low)
    their_attended, gu_pieces, down_pieces, wo_near = lax.optimization_barrier(
        (their_attended, gu_pieces, down_pieces, wo_near)
    )
    if chips == 4:
        passed = [gu_pieces[1][:1], gu_pieces[2][1:]]
        their_attended, passed, wo_near = lax.optimization_barrier((their_attended, passed, wo_near))
        gu_pieces += [plane_swap(passed[0], 2), plane_swap(passed[1], 1)]
    for _ in range(3, places):
        down_pieces.append(along(down_pieces[-1], 1))
    wo_far = core_swap(wo_near)
    mixed, second_low, second_turned, joined, out_weight = mix(
        wo_meta, chip_tokens, attended_low, their_attended, gains[1:2], wo_near, wo_far
    )
    down_meta = [step * places + order[index] for index in range(places) for step in steps]
    high = place // (places // 2)
    for side in (high, 1 - high):
        for spot in range(places // 2):
            down_meta += [step * places + side * (places // 2) + spot for step in steps]
    (out_part, back_part), gu_grads, down_grads = feed(
        gu_pieces, down_pieces, jnp.stack(steps + down_meta), second_low, second_turned, chip_cot, chips, places
    )
    add = lambda a, b: total([a, b]).astype(bf16)
    gu_arrived = scatter_plane(gu_grads)
    down_moving = across(down_grads[1], places // 2)
    their_back = core_swap(back_part)
    dmixed, attended_grad, second_gain, branch = settle(
        core.reshape(1), mixed, chip_cot, back_part, their_back, out_weight, gains[1:2]
    )
    dq, dkv, bias_part = retreat(chip.reshape(1), attended_grad, attended, query, key, value, soft)
    pair_meta = jnp.stack([chip, core] + steps)
    attn_grads = weight_grads(
        attn_pieces,
        pair_meta,
        turned,
        dq,
        dkv,
        gains[:1],
        second_gain,
        bias_part,
        joined,
        branch,
        chips,
    )

    near_back, far_back = row_grads(attn_pieces, pair_meta, after(dq, attn_grads), dkv, chips)
    mine = lambda value: lax.dynamic_slice_in_dim(value, core * tok, tok, 0)
    theirs = lambda value: lax.dynamic_slice_in_dim(value, (1 - core) * tok, tok, 0)
    back_arrived = core_swap(far_back)
    attn_grads, gu_arrived, down_moving = lax.optimization_barrier(
        (attn_grads, gu_arrived, down_moving, back_arrived)
    )[:3]
    attn_arrived = [attn_grads[0]] + [plane_swap(attn_grads[step], step) for step in range(1, min(chips, 3))]
    reach = places // 2
    if rows * reach % 16 == 0:
        halves = cut_plane(gu_arrived, place // reach)
        gu_kept, gu_sent = [part.reshape(2, 2, reach, rows, hidden // 2) for part in halves]
    else:
        gu_sum = total(gu_arrived).astype(bf16).reshape(2, 2, places, rows, hidden // 2)
        gu_kept, gu_sent = halves_along(gu_sum, 2, place)
    gu_moving = across(gu_sent, reach)
    down_sum = add(after(down_moving, gu_sent), down_grads[0])
    down_kept, down_sent = halves_along(down_sum, 0, place)
    down_moving = across(down_sent, reach // 2)
    attn_arrived += [plane_swap(attn_grads[step], step) for step in range(3, chips)]
    attn_arrived, gu_moving, down_moving, out_part = lax.optimization_barrier(
        (attn_arrived, gu_moving, down_moving, out_part)
    )
    their_out = core_swap(theirs(out_part))
    while reach > 2:
        gu_kept, gu_sent = halves_along(add(gu_kept, gu_moving), 2, place)
        reach //= 2
        gu_moving = across(gu_sent, reach)
        down_kept, down_sent = halves_along(add(down_kept, down_moving), 0, place)
        down_moving = across(down_sent, reach // 2)
    down_last = add(down_kept, down_moving)[0]
    gu_kept, gu_sent = halves_along(add(gu_kept, gu_moving), 2, place)
    attn_arrived, gu_sent, down_last = lax.optimization_barrier((attn_arrived, gu_sent, down_last))
    down_halves = halved(down_last, chips // 2)
    gu_moving = across(gu_sent, 1)
    gu_sum = total([gu_kept, gu_moving])[:, :, 0]
    layer_output = mine(mixed) + mine(out_part) + their_out
    pick = lambda value, first, dim: jnp.where(
        first, lax.index_in_dim(value, 0, dim, False), lax.index_in_dim(value, 1, dim, False)
    )
    gu_own = pick(gu_sum, first_core, 1)
    gu_their = core_swap(pick(gu_sum, core == 1, 1))
    attn_cuts = sum_plane(attn_arrived, onward)
    attn_sum = spread(attn_cuts)
    merged = total([near_back, back_arrived]).astype(bf16)
    later_steps = [chips // 2 >> turn for turn in range(1, chips.bit_length() - 1)]
    back_sum = summed_half(halved(after(merged, attn_cuts, gu_sum), 1))
    back_halves = halved(back_sum, 2)
    down_sum = after(summed_half(down_halves), back_sum)
    own_down = finished(halved(down_sum, later_steps[0]), later_steps[1:])

    weave = lambda parts: jnp.stack(
        [part.reshape(2, rows, chips, grain) for part in parts], axis=3
    ).reshape(2, rows, hidden)
    own_gu = weave(by_core(gu_own, gu_their))
    all_tokens = places * tok * cycle_size
    inverse_root = 1.0 / math.sqrt(all_tokens)
    ffin_new = update(ffin_weight, own_gu, ffin_momentum, ffin_average, ffin_rate * inverse_root)
    ffout_new = update(
        ffout_weight, own_down, ffout_momentum, ffout_average, ffout_rate * inverse_root
    )
    ffin_new += (ffin_new[0].astype(bf16),)
    ffout_new += (ffout_new[0].astype(bf16),)
    attn_sum, ffin_new = lax.optimization_barrier((attn_sum, ffin_new))
    summed, sent = last_sum(core, attn_sum)
    arrived = core_swap(sent)
    arrived = lax.optimization_barrier((arrived, back_sum))[0]
    attn_new = attention_update(
        core,
        summed,
        arrived,
        attention_weight,
        attention_momentum,
        attention_average,
        [rate * inverse_root for rate in attention_rates],
    )
    back_halves = after(back_halves, attn_new[0])
    first_grad = finished(back_halves, [2 << turn for turn in range(1, chips.bit_length() - 2)])
    scale = rms_scale(flat_tokens)
    gained = first_grad * gains[0]
    inner = jnp.mean(gained * flat_tokens, axis=-1, keepdims=True)
    input_grad = mine(dmixed) + scale * gained - flat_tokens * (scale**3 * inner)

    small_own, small_their = summed[-small_rows:], arrived[-small_rows:]
    gains_reduced = (small_own[:4] + small_their[:4]).reshape(gains.shape)
    pairs = heads // 4
    heads_of = lambda value: value[4 : 4 + pairs, : 2 * lanes].reshape(heads // 2, lanes)[:, : bias_table.shape[0]]
    bias_reduced = jnp.concatenate(by_core(heads_of(small_own), heads_of(small_their)), axis=0).T

    gain_rate = jnp.array(gain_rates, dtype=f32)[:, None] * inverse_root
    bias_new = update(bias_table, bias_reduced, bias_momentum, bias_average, bias_rate * inverse_root)
    gain_new = update(gains, gains_reduced, gain_momentum, gain_average, gain_rate)
    return (
        layer_output.reshape(tokens.shape),
        input_grad.reshape(tokens.shape),
        attn_new[0],
        ffin_new[0],
        ffout_new[0],
        bias_new[0],
        gain_new[0],
        attn_new[1],
        ffin_new[1],
        ffout_new[1],
        bias_new[1],
        gain_new[1],
        attn_new[2],
        ffin_new[2],
        ffout_new[2],
        bias_new[2],
        gain_new[2],
        attn_new[3],
        ffin_new[3],
        ffout_new[3],
    )


def solution(mesh):
    rows = P("batch", "seq", None)
    stacked = P(None, ("seq", "batch"), None)
    single = P(("seq", "batch"), None)
    weights = (stacked, stacked, single, P(), P())
    return jax.shard_map(
        shards,
        mesh=mesh,
        in_specs=(rows, rows, P("batch", "seq")) + weights * 3,
        out_specs=(rows, rows) + weights * 3 + (stacked, stacked, single),
        check_vma=False,
    )
```
